32 devices in a mesh: tok: 8 (over z, y), head: 4 (over x, core).
Axes of the slice: x: 2, y: 2, z: 4, core: 2. Of those that a mesh axis runs over, the one named last changes fastest.
Arguments:
- prefill_states: bfloat16 [1, 2048, 2048], P(None, 'tok'), may hold values from -6 to 6
- decode_states: bfloat16 [64, 2048], P('tok'), may hold values from -6 to 6
- attn_gain: float32 [2048], replicated, may hold values from 0.1 to 1.9
- w_qkv: bfloat16 [2048, 3, 2048], P(None, None, 'head'), may hold values from -0.125 to 0.125
- w_out: bfloat16 [2048, 2048], P('head'), may hold values from -0.125 to 0.125
- ffn_gain: float32 [2048], replicated, may hold values from 0.1 to 1.9
- w_gate_up: bfloat16 [2048, 2, 5120], P(None, None, 'tok'), may hold values from -0.125 to 0.125
- w_down: bfloat16 [5120, 2048], P('tok'), may hold values from -0.078125 to 0.078125
- prefill_pool: bfloat16 [384, 128, 512], P('tok', None, 'head')
- prefill_pages: int32 [8, 48], P('tok'), may hold values from 0 to 47, as said below
- prefill_lengths: int32 [1], replicated, may hold values from 1 to 6144, as said below
- prefill_home: int32 [8], replicated, may hold values from 0 to 7, each once
- decode_pool: bfloat16 [512, 128, 4096], P('tok', None, 'head')
- decode_pages: int32 [64, 32], P('tok'), may hold values from 0 to 63, as said below
- decode_lengths: int32 [64], P('tok'), may hold values from 1 to 4096, as said below
- decode_home: int32 [64], replicated, may hold values from 0 to 63, each once
Outputs:
- prefill_out: bfloat16 [1, 2048, 2048], P(None, ('tok', 'head'))
- decode_out: bfloat16 [64, 2048], P(('tok', 'head'))
The draws below stay inside these ranges and needn't reach their ends.
Inputs may be any that keep to these rules, and one draw needn't show every extreme that they name: `prefill_pages`: each row is an ordering of all 48 pages of the prefill pool on that row's tok index. `prefill_lengths`: one prefill request has exactly 6144 cached tokens. `decode_pages`: slot s lies on tok index s // 8; within one tok index the first ceil(length / 128) pages of its slots are all different. `decode_lengths`: every tok index hosts one decode request of exactly 4096 cached tokens.
All inputs are finite; a program needn't handle non-finite values.
Results may differ from the reference program's by a relative error of at most 0.017.
The reference program's roundings to bfloat16 on the way count: a program that leaves them out, or rounds other values in their place, can miss the bound.
Values may be sent and summed in bfloat16 or wider, within the bound.
No kernel may reach another device: no remote copies, remote signals or barrier semaphores. Data moves between devices by JAX's collectives and lax.ppermute only.
A program may use at most 128 MiB of HBM per device.

```python
import jax
import jax.numpy as jnp
from jax import lax

D = 2048
H = 32
HD = 64
FF = 5120
PAGE = 128
STRETCH = 2048
PCACHE = 6144
DEC_DEV = 8
DCACHE = 4096
HH = 8
NPRE = 1
NDEC = 64
PPD = 48
DPD = 64
DMAXP = 32
N_TOK = 8
N_HEAD = 4


def pool_values(key, rows, width):
    base = jax.random.normal(key, (rows, PAGE, width), jnp.float32)
    return base.astype(jnp.bfloat16)


def draw_prefill_pool(key, part):
    return pool_values(jax.random.fold_in(key, 21), N_TOK * PPD, N_HEAD * 2 * HD)


def draw_decode_pool(key, part):
    return pool_values(jax.random.fold_in(key, 22), N_TOK * DPD, H * 2 * HD)


def draw_prefill_pages(key, part):
    subkeys = jax.random.split(jax.random.fold_in(key, 5), N_TOK)
    return jax.vmap(lambda subkey: jax.random.permutation(subkey, PPD))(subkeys).astype(jnp.int32)


def draw_prefill_lengths(key, part):
    base = jax.random.fold_in(key, 9)
    lengths = jax.random.randint(jax.random.fold_in(base, 1), (NPRE,), 1, PCACHE + 1)
    longest = jax.random.randint(jax.random.fold_in(base, 2), (), 0, NPRE)
    return jnp.where(jnp.arange(NPRE) == longest, PCACHE, lengths).astype(jnp.int32)


def decode_layout(key):
    base = jax.random.fold_in(key, 11)
    longest = jax.random.randint(jax.random.fold_in(base, 1), (N_TOK,), 0, DEC_DEV)
    shorter = min(DCACHE, (DPD - DMAXP) // (DEC_DEV - 1) * PAGE)
    lengths = jax.random.randint(jax.random.fold_in(base, 2), (N_TOK, DEC_DEV), 1, shorter + 1)
    lengths = jnp.where(jnp.arange(DEC_DEV)[None, :] == longest[:, None], DCACHE, lengths)
    used = (lengths + PAGE - 1) // PAGE
    offset = jnp.cumsum(used, axis=1) - used
    subkeys = jax.random.split(jax.random.fold_in(base, 3), N_TOK)
    orders = jax.vmap(lambda subkey: jax.random.permutation(subkey, DPD))(subkeys)
    index = (offset[:, :, None] + jnp.arange(DMAXP)[None, None, :]) % DPD
    pages = jax.vmap(lambda order, where_at: order[where_at])(orders, index)
    return (lengths.reshape(NDEC).astype(jnp.int32), pages.reshape(NDEC, DMAXP).astype(jnp.int32))


def draw_decode_lengths(key, part):
    return decode_layout(key)[0]


def draw_decode_pages(key, part):
    return decode_layout(key)[1]


def block_levels(rng, dims, cuts, smallest, top_value):
    loudness, own = 1.0, jax.random.fold_in(rng, 6)
    for dim, parts in cuts:
        draws = jnp.exp(jax.random.uniform(jax.random.fold_in(own, dim), (parts,), jnp.float32, smallest / len(cuts), top_value / len(cuts)))
        loudness = loudness * jnp.repeat(draws, dims[dim] // parts).reshape([-1 if axis == dim else 1 for axis in range(len(dims))])
    return loudness


def gaussian(own_key, dims, spread, most, cuts=(), kind=jnp.bfloat16):
    values = jax.random.normal(own_key, dims, jnp.float32) * spread
    if len(cuts) > 0:
        values = block_levels(own_key, dims, cuts, -0.22, 0.18) * values
    return jnp.clip(values, min=-most, max=most).astype(kind)


def setup_inputs(seed: int = 0) -> dict:
    splits = jax.random.split(jax.random.key(seed), 17)
    prefill_states = gaussian(splits[0], (NPRE, STRETCH, D), 1.0, 6.0, ((1, 8),))
    decode_states = gaussian(splits[1], (NDEC, D), 1.0, 6.0, ((0, 8),))
    attn_gain = jnp.clip(1.0 + 0.18 * jax.random.normal(splits[2], (D,), jnp.float32), 0.1, 1.9)
    w_qkv = gaussian(splits[3], (D, 3, H * HD), D ** -0.5, 0.125, ((2, 4),))
    w_out = gaussian(splits[4], (H * HD, D), (H * HD) ** -0.5, 0.125, ((0, 4),))
    ffn_gain = jnp.clip(1.0 + 0.18 * jax.random.normal(splits[5], (D,), jnp.float32), 0.1, 1.9)
    w_gate_up = gaussian(splits[6], (D, 2, FF), D ** -0.5, 0.125, ((2, 8),))
    w_down = gaussian(splits[7], (FF, D), FF ** -0.5, 0.078125, ((0, 8),))
    prefill_pool = draw_prefill_pool(jax.random.fold_in(splits[16], 71), 0)
    prefill_pages = draw_prefill_pages(jax.random.fold_in(splits[16], 71), 0)
    prefill_lengths = draw_prefill_lengths(jax.random.fold_in(splits[16], 71), 0)
    prefill_home = jax.random.permutation(splits[11], N_TOK).astype(jnp.int32)
    decode_pool = draw_decode_pool(jax.random.fold_in(splits[16], 71), 0)
    decode_pages = draw_decode_pages(jax.random.fold_in(splits[16], 71), 0)
    decode_lengths = draw_decode_lengths(jax.random.fold_in(splits[16], 71), 0)
    decode_home = jax.random.permutation(splits[15], NDEC).astype(jnp.int32)
    return {"prefill_states": prefill_states, "decode_states": decode_states, "attn_gain": attn_gain, "w_qkv": w_qkv, "w_out": w_out, "ffn_gain": ffn_gain, "w_gate_up": w_gate_up, "w_down": w_down, "prefill_pool": prefill_pool, "prefill_pages": prefill_pages, "prefill_lengths": prefill_lengths, "prefill_home": prefill_home, "decode_pool": decode_pool, "decode_pages": decode_pages, "decode_lengths": decode_lengths, "decode_home": decode_home}


EPSILON = 1e-06
SCALE = 0.125
MASKED = -1e+30

def rms_norm(rows, gain):
    values = rows.astype(jnp.float32)
    inverse = lax.rsqrt(lax.optimization_barrier(jnp.mean(values * values, axis=-1, keepdims=True)) + EPSILON)
    return (values * inverse * gain.astype(jnp.float32)).astype(jnp.bfloat16)

def split_sum(left, right, groups):
    width = left.shape[1] // groups

    def add_part(index, total):
        piece_left = lax.dynamic_slice_in_dim(left, index * width, width, 1)
        piece_right = lax.dynamic_slice_in_dim(right, index * width, width, 0)
        term = jnp.dot(piece_left, piece_right, preferred_element_type=jnp.float32)
        term = lax.optimization_barrier(term.astype(jnp.bfloat16)).astype(jnp.float32)
        return total + term
    start = jnp.zeros((left.shape[0], right.shape[1]), jnp.float32)
    return lax.fori_loop(0, groups, add_part, start)

def reference(prefill_states, decode_states, attn_gain, w_qkv, w_out, ffn_gain, w_gate_up, w_down, prefill_pool, prefill_pages, prefill_lengths, prefill_home, decode_pool, decode_pages, decode_lengths, decode_home):
    weight = w_qkv.reshape(D, 3 * H * HD)
    normed_pre = rms_norm(prefill_states, attn_gain).reshape(NPRE * STRETCH, D)
    normed_dec = rms_norm(decode_states, attn_gain)
    proj_pre = jnp.dot(normed_pre, weight, preferred_element_type=jnp.float32).astype(jnp.bfloat16).reshape(NPRE, STRETCH, 3, H, HD)
    proj_dec = jnp.dot(normed_dec, weight, preferred_element_type=jnp.float32).astype(jnp.bfloat16).reshape(NDEC, 3, H, HD)
    causal = jnp.arange(STRETCH)[None, :] <= jnp.arange(STRETCH)[:, None]

    def prefill_unit(unit):
        request = unit // H
        head = unit % H
        host = prefill_home[request * HH + head % HH]
        rows = host * PPD + prefill_pages[host]
        pages = jnp.take(prefill_pool, rows, axis=0)
        cache = lax.dynamic_slice_in_dim(pages, head // HH * 2 * HD, 2 * HD, 2).reshape(PCACHE, 2 * HD)
        length = prefill_lengths[request]
        own = lax.dynamic_index_in_dim(proj_pre[request], head, axis=2, keepdims=False)
        query, key_rows, value_rows = (own[:, 0], own[:, 1], own[:, 2])
        score_cache = jnp.dot(query, cache[:, :HD].T, preferred_element_type=jnp.float32) * SCALE
        score_cache = jnp.where(jnp.arange(PCACHE)[None, :] < length, score_cache, MASKED)
        score_stretch = jnp.dot(query, key_rows.T, preferred_element_type=jnp.float32) * SCALE
        score_stretch = jnp.where(causal, score_stretch, MASKED)
        scores = jnp.concatenate([score_cache, score_stretch], axis=1)
        values = jnp.concatenate([cache[:, HD:], value_rows], axis=0)
        top = lax.optimization_barrier(jnp.max(scores, axis=1, keepdims=True))
        weights = jnp.exp(scores - top)
        total = lax.optimization_barrier(jnp.sum(weights, axis=1, keepdims=True))
        mixed = jnp.dot(weights.astype(jnp.bfloat16), values, preferred_element_type=jnp.float32)
        return (mixed / total).astype(jnp.bfloat16)
    units = lax.map(prefill_unit, jnp.arange(NPRE * H, dtype=jnp.int32))
    attn_pre = jnp.transpose(units.reshape(NPRE, H, STRETCH, HD), (0, 2, 1, 3)).reshape(NPRE * STRETCH, H * HD)

    def decode_one(request):
        slot = decode_home[request]
        host = slot // DEC_DEV
        rows = host * DPD + decode_pages[slot]
        cache = jnp.take(decode_pool, rows, axis=0).reshape(DCACHE, H, 2 * HD).astype(jnp.float32)
        length = decode_lengths[slot]
        own = proj_dec[request].astype(jnp.float32)
        scores = jnp.einsum('hd,khd->hk', own[0], cache[:, :, :HD], precision=lax.Precision.HIGHEST) * SCALE
        scores = jnp.where(jnp.arange(DCACHE)[None, :] < length, scores, MASKED)
        own_score = lax.optimization_barrier(jnp.sum(own[0] * own[1], axis=1, keepdims=True)) * SCALE
        top = jnp.maximum(lax.optimization_barrier(jnp.max(scores, axis=1, keepdims=True)), own_score)
        weights = jnp.exp(scores - top)
        own_weight = jnp.exp(own_score - top)
        total = lax.optimization_barrier(jnp.sum(weights, axis=1, keepdims=True)) + own_weight
        mixed = jnp.einsum('hk,khd->hd', weights.astype(jnp.bfloat16).astype(jnp.float32), cache[:, :, HD:], precision=lax.Precision.HIGHEST)
        mixed = mixed + own_weight.astype(jnp.bfloat16).astype(jnp.float32) * own[2]
        return (mixed / total).astype(jnp.bfloat16).reshape(H * HD)
    attn_dec = lax.map(decode_one, jnp.arange(NDEC, dtype=jnp.int32))
    attn = jnp.concatenate([attn_pre, attn_dec], axis=0)
    states = jnp.concatenate([prefill_states.reshape(NPRE * STRETCH, D), decode_states], axis=0).astype(jnp.float32)
    resid = states + split_sum(attn, w_out, N_HEAD)
    normed_mid = rms_norm(resid, ffn_gain)
    gate = jnp.dot(normed_mid, w_gate_up[:, 0], preferred_element_type=jnp.float32)
    upper = jnp.dot(normed_mid, w_gate_up[:, 1], preferred_element_type=jnp.float32)
    hidden = (jax.nn.gelu(gate, approximate=True) * upper).astype(jnp.bfloat16)
    result = (resid + split_sum(hidden, w_down, N_TOK)).astype(jnp.bfloat16)
    prefill_out = result[:NPRE * STRETCH].reshape(NPRE, STRETCH, D)
    decode_out = result[NPRE * STRETCH:]
    return (prefill_out, decode_out)
```

```python
import functools
import jax
import jax.numpy as jnp
from jax import lax
from jax.experimental import pallas as pl
from jax.experimental.pallas import tpu as pltpu
from jax.sharding import PartitionSpec as P

HD = 64
PAGE = 128
EPSILON = 1e-06
SCALE = 0.125
MASKED = -1e30
LOG2E = 1.4426950408889634
BLOCK = 512
F32 = jnp.float32
BF16 = jnp.bfloat16
VMEM = pl.BlockSpec(memory_space=pltpu.VMEM)
SMEM = pl.BlockSpec(memory_space=pltpu.SMEM)
ANY = pl.BlockSpec(memory_space=pl.ANY)


def contract_last(left, right):
    return lax.dot_general(left, right, (((1,), (1,)), ((), ())), preferred_element_type=F32)


def prefill_kernel(positions, n_pages, scal, pages, msg, pool, out, kv, queries, scores, top, acc, sems):
    blocks = msg.shape[0]
    stretch = blocks * positions
    half = positions // 2
    length = scal[0]
    used = pl.cdiv(length, BLOCK)
    cached = used * BLOCK
    per_chunk = BLOCK // PAGE
    n_copies = used * per_chunk

    def page_copy(index):
        page = pages[jnp.minimum(index, n_pages - 1)]
        return pltpu.make_async_copy(
            pool.at[page], kv.at[pl.ds(pl.multiple_of(index * PAGE, PAGE), PAGE), pl.ds(0, 2 * HD)], sems.at[index]
        )

    @pl.loop(0, n_copies)
    def _(index):
        page_copy(index).start()

    lane = lax.broadcasted_iota(jnp.int32, (positions, 4 * HD), 1)
    tail = lax.broadcasted_iota(jnp.int32, (half, 2 * HD), 1)
    one_hot = jnp.where(tail == 2 * HD - 1, 1.0, 0.0).astype(BF16)

    @pl.loop(0, blocks)
    def _(b):
        packed = msg[b, pl.ds(positions, half), :].astype(F32) * (SCALE * LOG2E)
        high = packed.astype(BF16)
        low = (packed - high.astype(F32)).astype(BF16)
        zero = jnp.zeros((half, HD), BF16)
        row = pl.multiple_of(b * positions, positions)
        for part in range(2):
            lanes = slice(part * HD, (part + 1) * HD)
            rows = pl.ds(row + part * half, half)
            queries[rows, 0 : 2 * HD] = jnp.concatenate([high[:, lanes], zero], axis=1)
            queries[rows, 2 * HD : 4 * HD] = jnp.where(
                tail < HD, jnp.concatenate([low[:, lanes], zero], axis=1), one_hot
            )
        own = msg[b, pl.ds(0, positions), :]
        spot = pl.multiple_of(cached + row, positions)
        kv[pl.ds(spot, positions), 0 : 2 * HD] = own
        side = lax.broadcasted_iota(jnp.int32, (positions, 2 * HD), 1)
        fill = jnp.where(side == 2 * HD - 1, 0.0, 1.0).astype(BF16)
        kv[pl.ds(spot, positions), 2 * HD : 4 * HD] = jnp.where(side < HD, own, fill)

    @pl.loop(0, n_copies)
    def _(index):
        page_copy(index).wait()
        rows = pl.ds(pl.multiple_of(index * PAGE, PAGE), PAGE)
        side = lax.broadcasted_iota(jnp.int32, (PAGE, 2 * HD), 1)
        place = index * PAGE + lax.broadcasted_iota(jnp.int32, (PAGE, 2 * HD), 0)
        bias = jnp.where(place < length, 0.0, MASKED)
        fill = jnp.where(side == 2 * HD - 1, bias, 1.0).astype(BF16)
        kv[rows, 2 * HD : 4 * HD] = jnp.where(side < HD, kv[rows, 0 : 2 * HD], fill)

    def chunk(c):
        return kv[pl.ds(pl.multiple_of(c * BLOCK, BLOCK), BLOCK), :]

    def raise_top(values):
        best = top[...]
        for k in range(BLOCK // 128):
            best = jnp.maximum(best, values[:, k * 128 : (k + 1) * 128])
        top[...] = best

    def score(i, c):
        values = contract_last(queries[pl.ds(pl.multiple_of(i * BLOCK, BLOCK), BLOCK), :], chunk(c))
        scores[c] = values
        raise_top(values)

    def score_diagonal(i):
        c = used + i
        values = contract_last(queries[pl.ds(pl.multiple_of(i * BLOCK, BLOCK), BLOCK), :], chunk(c))
        rows = lax.broadcasted_iota(jnp.int32, (BLOCK, BLOCK), 0)
        cols = lax.broadcasted_iota(jnp.int32, (BLOCK, BLOCK), 1)
        values = jnp.where(cols <= rows, values, MASKED)
        scores[c] = values
        raise_top(values)

    final = acc.at[1]
    total = acc.at[0]

    def settle():
        best = jnp.max(top[...], axis=1, keepdims=True)
        final[:, 0:128] = jnp.broadcast_to(best, (BLOCK, 128))
        top[...] = jnp.full_like(top, -jnp.inf)
        total[...] = jnp.zeros_like(total)

    def mix(c):
        best = final[:, 0:128]
        values = scores[c]
        weights = jnp.concatenate(
            [jnp.exp2(values[:, k * 128 : (k + 1) * 128] - best).astype(BF16) for k in range(BLOCK // 128)], axis=1
        )
        total[...] += jnp.dot(weights, chunk(c), preferred_element_type=F32)

    def emit(i):
        mixed = (total[:, HD : 2 * HD] / total[:, 3 * HD : 3 * HD + 1]).astype(BF16)
        for k in range(BLOCK // positions):
            part = mixed[k * positions : (k + 1) * positions]
            out[i * (BLOCK // positions) + k] = jnp.concatenate([part[:half], part[half:]], axis=1)

    top[...] = jnp.full_like(top, -jnp.inf)

    @pl.loop(0, used)
    def _(c):
        score(0, c)

    score_diagonal(0)
    settle()
    steps = stretch // BLOCK

    @pl.loop(1, steps)
    def _(i):
        @pl.loop(0, used + i)
        def _(c):
            mix(c)
            score(i, c)

        emit(i - 1)
        score_diagonal(i)
        settle()

    @pl.loop(0, used + steps)
    def _(c):
        mix(c)

    emit(steps - 1)


def prefill_attention(length, pages, msg, pool):
    blocks, rows, _ = msg.shape
    positions = rows * 2 // 3
    n_pages = pool.shape[0]
    stretch = blocks * positions
    chunks = pl.cdiv(n_pages * PAGE, BLOCK) + stretch // BLOCK
    keys = chunks * BLOCK
    return pl.pallas_call(
        functools.partial(prefill_kernel, positions, n_pages),
        out_shape=jax.ShapeDtypeStruct((blocks, positions // 2, 2 * HD), BF16),
        in_specs=[SMEM, SMEM, VMEM, ANY],
        out_specs=VMEM,
        scratch_shapes=[
            pltpu.VMEM((keys, 4 * HD), BF16),
            pltpu.VMEM((stretch, 4 * HD), BF16),
            pltpu.VMEM((chunks, BLOCK, BLOCK), F32),
            pltpu.VMEM((BLOCK, 128), F32),
            pltpu.VMEM((2, BLOCK, 4 * HD), F32),
            pltpu.SemaphoreType.DMA((pl.cdiv(n_pages * PAGE, BLOCK) * (BLOCK // PAGE),)),
        ],
        compiler_params=pltpu.CompilerParams(vmem_limit_bytes=48 * 2**20),
        cost_estimate=pl.CostEstimate(flops=4 * stretch * keys * HD, bytes_accessed=4 * 2**20, transcendentals=stretch * keys),
    )(length, pages, msg, pool)


def decode_kernel(heads, scal, pages, x, gain, w, pool, out, buf, wbuf, normed, qrows, cacherows, rowout, wsems, sems):
    slots = pages.shape[0]
    width = heads * 2 * HD
    per_group = BLOCK // PAGE
    depth = pages.shape[1]
    w_copies = [pltpu.make_async_copy(w.at[j], wbuf.at[j], wsems.at[j]) for j in range(3)]
    for copy in w_copies:
        copy.start()

    def groups(s):
        return pl.cdiv(scal[s], BLOCK)

    def page_copy(s, start, index):
        page = pages[s, jnp.minimum(index, depth - 1)]
        place = start * per_group + index
        return pltpu.make_async_copy(
            pool.at[page], buf.at[pl.ds(pl.multiple_of(place * PAGE, PAGE), PAGE), :], sems.at[place]
        )

    def begin(s, start):
        @pl.loop(0, groups(s) * per_group)
        def _(index):
            page_copy(s, start, index).start()

        return start + groups(s)

    lax.fori_loop(0, slots, begin, 0)
    values = x[...].astype(F32)
    inverse = lax.rsqrt(jnp.mean(values * values, axis=-1, keepdims=True) + EPSILON)
    normed[...] = (values * inverse * gain[...]).astype(BF16)
    rows = values.shape[0]
    zero = jnp.zeros((rows, HD), F32)
    parts = []
    for j in range(3):
        w_copies[j].wait()
        parts.append(jnp.dot(normed[...], wbuf[j], preferred_element_type=F32).astype(BF16).astype(F32))
    for g in range(heads):
        cut = slice(g * HD, (g + 1) * HD)
        span = slice(g * 2 * HD, (g + 1) * 2 * HD)
        qrows[:, span] = jnp.concatenate([parts[0][:, cut] * SCALE, zero], axis=1)
        cacherows[:, span] = jnp.concatenate([parts[1][:, cut], parts[2][:, cut]], axis=1)
    owner = lax.broadcasted_iota(jnp.int32, (8, width), 1) // (2 * HD)
    diagonal = owner == lax.broadcasted_iota(jnp.int32, (8, width), 0)

    def slot(s, start):
        row = scal[slots + s]
        length = scal[s]
        query = jnp.where(diagonal, jnp.broadcast_to(qrows[pl.ds(row, 1), :], (8, width)), 0.0)
        own = jnp.broadcast_to(cacherows[pl.ds(row, 1), :], (8, width))
        own_score = jnp.sum(query * own, axis=1, keepdims=True)
        query = query.astype(BF16)

        def step(g, carry):
            best, total, mixed = carry

            for k in range(per_group):
                page_copy(s, start, g * per_group + k).wait()
            cache = buf[pl.ds(pl.multiple_of((start + g) * BLOCK, BLOCK), BLOCK), :]
            values = contract_last(query, cache)
            place = g * BLOCK + lax.broadcasted_iota(jnp.int32, (8, BLOCK), 1)
            values = jnp.where(place < length, values, MASKED)
            newer = jnp.maximum(best, jnp.max(values, axis=1, keepdims=True))
            shrink = jnp.exp(best - newer)
            weights = jnp.exp(values - newer)
            total = total * shrink + jnp.sum(weights, axis=1, keepdims=True)
            mixed = mixed * shrink + jnp.dot(weights.astype(BF16), cache, preferred_element_type=F32)
            return newer, total, mixed

        best, total, mixed = lax.fori_loop(
            0, groups(s), step, (own_score, jnp.zeros((8, 1), F32), jnp.zeros((8, width), F32))
        )
        own_weight = jnp.exp(own_score - best)
        total = total + own_weight
        mixed = mixed + own_weight.astype(BF16).astype(F32) * own
        mixed = jnp.where(diagonal, mixed / total, 0.0)
        rowout[pl.ds(s, 1), :] = jnp.sum(mixed, axis=0, keepdims=True)
        return start + groups(s)

    lax.fori_loop(0, slots, slot, 0)
    done = rowout[...].astype(BF16)
    for g in range(0, heads, 2):
        out[:, g * HD : (g + 2) * HD] = jnp.concatenate(
            [done[:, g * 2 * HD + HD : (g + 1) * 2 * HD], done[:, (g + 1) * 2 * HD + HD : (g + 2) * 2 * HD]], axis=1
        )


def decode_attention(scal, pages, x, gain, w, pool):
    slots = pages.shape[0]
    features = w.shape[2]
    heads = features // HD
    width = heads * 2 * HD
    rows = x.shape[0]
    most = pool.shape[0] + slots * (BLOCK // PAGE - 1)
    return pl.pallas_call(
        functools.partial(decode_kernel, heads),
        out_shape=jax.ShapeDtypeStruct((slots, features), BF16),
        in_specs=[SMEM, SMEM, VMEM, VMEM, ANY, ANY],
        out_specs=VMEM,
        scratch_shapes=[
            pltpu.VMEM((most * PAGE, width), BF16),
            pltpu.VMEM(w.shape, BF16),
            pltpu.VMEM(x.shape, BF16),
            pltpu.VMEM((rows, width), F32),
            pltpu.VMEM((rows, width), F32),
            pltpu.VMEM((slots, width), F32),
            pltpu.SemaphoreType.DMA((3,)),
            pltpu.SemaphoreType.DMA((most,)),
        ],
        compiler_params=pltpu.CompilerParams(vmem_limit_bytes=48 * 2**20),
        cost_estimate=pl.CostEstimate(flops=2 * 10**9, bytes_accessed=22 * 2**20, transcendentals=10**6),
    )(scal, pages, x, gain, w, pool)


def qkv_kernel(requests, heads, home, x, gain, w, out, normed, keys):
    j = pl.program_id(0)
    rows = x.shape[0]
    positions = rows // requests
    half = positions // 2

    @pl.when(j == 0)
    def _():
        values = x[...].astype(F32)
        inverse = lax.rsqrt(jnp.mean(values * values, axis=-1, keepdims=True) + EPSILON)
        normed[...] = (values * inverse * gain[...]).astype(BF16)

    y = jnp.dot(normed[...], w[0], preferred_element_type=F32).astype(BF16)

    @pl.when(j == 0)
    def _():
        for r in range(requests):
            for g in range(heads):
                part = y[r * positions : (r + 1) * positions, g * HD : (g + 1) * HD]
                out[home[r * heads + g], positions : positions + half, :] = jnp.concatenate(
                    [part[:half], part[half:]], axis=1
                )

    @pl.when(j == 1)
    def _():
        keys[...] = y

    @pl.when(j == 2)
    def _():
        for r in range(requests):
            span = slice(r * positions, (r + 1) * positions)
            for g in range(heads):
                cut = slice(g * HD, (g + 1) * HD)
                out[home[r * heads + g], 0:positions, :] = jnp.concatenate([keys[span, cut], y[span, cut]], axis=1)


def qkv_messages(home, x, gain, w, requests):
    rows, width = x.shape
    features = w.shape[2]
    heads = features // HD
    units = requests * heads
    positions = rows // requests
    return pl.pallas_call(
        functools.partial(qkv_kernel, requests, heads),
        grid=(3,),
        out_shape=jax.ShapeDtypeStruct((units, positions * 3 // 2, 2 * HD), BF16),
        in_specs=[
            SMEM,
            pl.BlockSpec((rows, width), lambda j: (0, 0)),
            pl.BlockSpec((1, width), lambda j: (0, 0)),
            pl.BlockSpec((1, width, features), lambda j: (j, 0, 0)),
        ],
        out_specs=pl.BlockSpec((units, positions * 3 // 2, 2 * HD), lambda j: (0, 0, 0)),
        scratch_shapes=[pltpu.VMEM((rows, width), BF16), pltpu.VMEM((rows, features), BF16)],
        compiler_params=pltpu.CompilerParams(vmem_limit_bytes=32 * 2**20),
        cost_estimate=pl.CostEstimate(flops=2 * rows * width * 3 * features, bytes_accessed=10 * 2**20, transcendentals=0),
    )(home, x, gain, w)


def project_kernel(requests, heads, scal, received, gathered, w_out, *rest):
    outs, rows_in, decode_in = rest[:-2], rest[-2], rest[-1]
    n_head = len(outs)
    units = requests * heads
    per = outs[0].shape[0]
    half = received.shape[1]
    positions = 2 * half
    block_rows = positions // n_head
    share = per - requests * block_rows
    hosted = share * n_head
    decode_in[...] = gathered[...].astype(F32)
    rows_in[...] = jnp.zeros_like(rows_in)
    for r in range(requests):
        for g in range(0, heads, 2):
            left = received[scal[r * heads + g]].astype(F32)
            right = received[scal[r * heads + g + 1]].astype(F32)
            both = jnp.concatenate(
                [
                    jnp.concatenate([left[:, :HD], right[:, :HD]], axis=1),
                    jnp.concatenate([left[:, HD:], right[:, HD:]], axis=1),
                ],
                axis=0,
            )
            for h in range(n_head):
                rows_in[h, r * block_rows : (r + 1) * block_rows, g * HD : (g + 2) * HD] = both[
                    h * block_rows : (h + 1) * block_rows
                ]
    for j in range(hosted):
        rows_in[j // share, requests * block_rows + j % share, :] = decode_in[pl.ds(scal[units + j], 1), :][0]
    for k in range(n_head):
        mine = rows_in[scal[units + hosted + k]].astype(BF16)
        y = jnp.dot(mine, w_out[...], preferred_element_type=F32).astype(BF16)
        outs[k][...] = y[:per]


def project_out(scal, received, gathered, w_out, requests, heads, n_head, hosted):
    positions = 2 * received.shape[1]
    per = requests * (positions // n_head) + hosted // n_head
    padded = -(-per // 16) * 16
    features, width = w_out.shape
    return pl.pallas_call(
        functools.partial(project_kernel, requests, heads),
        out_shape=[jax.ShapeDtypeStruct((per, width), BF16)] * n_head,
        in_specs=[SMEM, VMEM, VMEM, VMEM],
        out_specs=[VMEM] * n_head,
        scratch_shapes=[pltpu.VMEM((n_head, padded, features), F32), pltpu.VMEM(gathered.shape, F32)],
        compiler_params=pltpu.CompilerParams(vmem_limit_bytes=32 * 2**20),
        cost_estimate=pl.CostEstimate(flops=2 * n_head * per * features * width, bytes_accessed=4 * 2**20, transcendentals=0),
    )(scal, received, gathered, w_out)


def feed_kernel(count, *refs):
    rows, (gate_up, down), outs = refs[:count], refs[count : count + 2], refs[count + 2 : 2 * count + 2]
    weights, down_weights, sems = refs[2 * count + 2 :]
    hidden_units = down.shape[0]
    tile = 128 if hidden_units % 128 == 0 else hidden_units
    steps = hidden_units // tile

    def load(step):
        cols = pl.ds(step * tile, tile)
        return pltpu.make_async_copy(gate_up.at[:, :, cols], weights.at[:, :, cols], sems.at[step])

    for step in range(steps):
        load(step).start()
    down_copy = pltpu.make_async_copy(down, down_weights, sems.at[steps])
    down_copy.start()
    hidden = [[] for _ in range(count)]
    for step in range(steps):
        load(step).wait()
        cols = slice(step * tile, (step + 1) * tile)
        both = jnp.concatenate([weights[0, :, cols], weights[1, :, cols]], axis=1) if tile == 128 else None
        for index in range(count):
            if tile == 128:
                y = jnp.dot(rows[index][...], both, preferred_element_type=F32)
                gate, upper = y[:, :tile], y[:, tile:]
            else:
                gate = jnp.dot(rows[index][...], weights[0], preferred_element_type=F32)
                upper = jnp.dot(rows[index][...], weights[1], preferred_element_type=F32)
            hidden[index].append((jax.nn.gelu(gate, approximate=True) * upper).astype(BF16))
    down_copy.wait()
    for index in range(count):
        full = jnp.concatenate(hidden[index], axis=1)
        outs[index][...] = jnp.dot(full, down_weights[...], preferred_element_type=F32).astype(BF16)


def feed_forward(chunks, gate_up, down):
    count = len(chunks)
    per, width = chunks[0].shape
    hidden_units = down.shape[0]
    return pl.pallas_call(
        functools.partial(feed_kernel, count),
        out_shape=[jax.ShapeDtypeStruct((per, width), BF16)] * count,
        in_specs=[VMEM] * count + [ANY, ANY],
        out_specs=[VMEM] * count,
        scratch_shapes=[
            pltpu.VMEM(gate_up.shape, BF16),
            pltpu.VMEM(down.shape, BF16),
            pltpu.SemaphoreType.DMA((hidden_units // 128 + 1,)),
        ],
        compiler_params=pltpu.CompilerParams(vmem_limit_bytes=32 * 2**20),
        cost_estimate=pl.CostEstimate(
            flops=6 * count * per * width * hidden_units, bytes_accessed=8 * 2**20, transcendentals=count * per * hidden_units
        ),
    )(*chunks, gate_up, down)


def ring_of(n_tok):
    if n_tok == 8:
        return [0, 2, 4, 6, 7, 5, 3, 1]
    return list(range(n_tok))


def shards(
    prefill_states,
    decode_states,
    attn_gain,
    w_qkv,
    w_out,
    ffn_gain,
    w_gate_up,
    w_down,
    prefill_pool,
    prefill_pages,
    prefill_lengths,
    prefill_home,
    decode_pool,
    decode_pages,
    decode_lengths,
    decode_home,
):
    n_tok = lax.axis_size("tok")
    n_head = lax.axis_size("head")
    my_tok = lax.axis_index("tok")
    my_head = lax.axis_index("head")
    requests, positions, width = prefill_states.shape
    hosted = decode_states.shape[0]
    features = w_qkv.shape[2]
    heads = features // HD
    units = requests * heads
    ring = ring_of(n_tok)
    ahead = [(ring[i], ring[(i + 1) % n_tok]) for i in range(n_tok)]
    behind = [(b, a) for a, b in ahead]
    far = n_tok // 2
    near = (n_tok - 1) // 2

    gain = attn_gain.reshape(1, width)
    w_three = jnp.transpose(w_qkv, (1, 0, 2))
    copies = jnp.broadcast_to(decode_states[None], (n_tok, hosted, width))
    all_decode = lax.all_to_all(copies, "tok", split_axis=0, concat_axis=0, tiled=True).reshape(n_tok * hosted, width)
    messages = qkv_messages(prefill_home, prefill_states.reshape(requests * positions, width), gain, w_three, requests)
    arrived = lax.all_to_all(messages, "tok", split_axis=0, concat_axis=0, tiled=True)

    slots = my_tok * hosted + jnp.arange(hosted, dtype=jnp.int32)
    all_requests = jnp.arange(decode_home.shape[0], dtype=jnp.int32)
    anchor = jnp.sum(jnp.where(decode_home[None, :] == slots[:, None], all_requests[None, :], 0), axis=1)
    decode_attn = decode_attention(
        jnp.concatenate([decode_lengths, anchor]), decode_pages, all_decode, gain, w_three, decode_pool
    )
    gathered = lax.all_gather(decode_attn, "tok", axis=0, tiled=True)
    gate_up = jnp.transpose(w_gate_up, (1, 0, 2))

    unit_ids = jnp.arange(units, dtype=jnp.int32)
    my_unit = jnp.sum(jnp.where(prefill_home == my_tok, unit_ids, 0))
    length = lax.dynamic_slice_in_dim(prefill_lengths, my_unit // heads, 1, 0)
    attn = prefill_attention(length, prefill_pages.reshape(-1), arrived, prefill_pool)
    returned = lax.all_to_all(attn, "tok", split_axis=0, concat_axis=0, tiled=True)

    my_slots = lax.dynamic_slice_in_dim(decode_home, my_tok * hosted, hosted, 0)
    targets = my_head ^ jnp.arange(n_head, dtype=jnp.int32)
    parts = project_out(
        jnp.concatenate([prefill_home, my_slots, targets]), returned, gathered, w_out, requests, heads, n_head, hosted
    )
    block_rows = positions // n_head
    share = hosted // n_head
    own_pre = lax.dynamic_slice_in_dim(prefill_states, my_head * block_rows, block_rows, 1)
    own_dec = lax.dynamic_slice_in_dim(decode_states, my_head * share, share, 0)
    resid = jnp.concatenate([own_pre.reshape(requests * block_rows, width), own_dec], axis=0).astype(F32)
    resid = resid + parts[0].astype(F32)
    for k in range(1, n_head):
        resid = resid + lax.ppermute(parts[k], "head", [(i, i ^ k) for i in range(n_head)]).astype(F32)
    mean = jnp.mean(resid * resid, axis=-1, keepdims=True)
    normed_mid = (resid * lax.rsqrt(mean + EPSILON) * ffn_gain).astype(BF16)

    plus, minus = {}, {}
    up, down = normed_mid, normed_mid
    (own_part,) = feed_forward([normed_mid], gate_up, w_down)
    for k in range(1, far + 1):
        up = lax.ppermute(up, "tok", ahead)
        if k <= near:
            down = lax.ppermute(down, "tok", behind)
            minus[k], plus[k] = feed_forward([up, down], gate_up, w_down)
        else:
            (minus[k],) = feed_forward([up], gate_up, w_down)
            plus[k] = minus[k]

    def joined(part, other):
        return (part.astype(F32) + other.astype(F32)).astype(BF16)

    up, down = plus[far], minus[near]
    for k in range(far - 1, 0, -1):
        up = joined(plus[k], lax.ppermute(up, "tok", ahead))
        if k < near:
            down = joined(minus[k], lax.ppermute(down, "tok", behind))
    up = lax.ppermute(up, "tok", ahead).astype(F32)
    down = lax.ppermute(down, "tok", behind).astype(F32)
    result = (resid + (own_part.astype(F32) + up + down)).astype(BF16)
    prefill_out = result[: requests * block_rows].reshape(requests, block_rows, width)
    return (prefill_out, result[requests * block_rows :])


def solution(mesh):
    placed = (
        P(None, "tok", None),
        P("tok", None),
        P(),
        P(None, None, "head"),
        P("head", None),
        P(),
        P(None, None, "tok"),
        P("tok", None),
        P("tok", None, "head"),
        P("tok", None),
        P(),
        P(),
        P("tok", None, "head"),
        P("tok", None),
        P("tok"),
        P(),
    )
    return jax.shard_map(
        shards,
        mesh=mesh,
        in_specs=placed,
        out_specs=(P(None, ("tok", "head"), None), P(("tok", "head"), None)),
        check_vma=False,
    )
```

```python
import functools
import jax
import jax.numpy as jnp
from jax import lax
from jax.experimental import pallas as pl
from jax.experimental.pallas import tpu as pltpu
from jax.sharding import PartitionSpec as P

HD = 64
PAGE = 128
EPSILON = 1e-06
SCALE = 0.125
MASKED = -1e30
LOG2E = 1.4426950408889634
BLOCK = 512
CHUNK = 1024
UNROLL = 2
AHEAD = 6
F32 = jnp.float32
BF16 = jnp.bfloat16
VMEM = pl.BlockSpec(memory_space=pltpu.VMEM)
SMEM = pl.BlockSpec(memory_space=pltpu.SMEM)
ANY = pl.BlockSpec(memory_space=pl.ANY)


def contract_last(left, right):
    return lax.dot_general(left, right, (((1,), (1,)), ((), ())), preferred_element_type=F32)


def cache_kernel(scal, pages, pool, flipped, values, raw, sems):
    length = scal[0]
    used = pl.cdiv(length, CHUNK)
    per_chunk = CHUNK // PAGE
    last = pages.shape[0] - 1

    def page_copy(index):
        page = pages[jnp.minimum(index, last)]
        return pltpu.make_async_copy(
            pool.at[page], raw.at[pl.ds(pl.multiple_of(index * PAGE, PAGE), PAGE), :], sems.at[index]
        )

    @pl.loop(0, used * per_chunk)
    def _(index):
        page_copy(index).start()

    @pl.loop(0, used)
    def _(c):
        for k in range(per_chunk):
            page_copy(c * per_chunk + k).wait()
        keys, mixed = doubled(raw[pl.ds(pl.multiple_of(c * CHUNK, CHUNK), CHUNK), :])
        flipped[c] = keys
        values[c] = mixed

        @pl.when(length - c * CHUNK < CHUNK)
        def _():
            valid = length - c * CHUNK
            columns = lax.broadcasted_iota(jnp.int32, keys.shape, 1) < valid
            flipped[c] = jnp.where(columns, keys, jnp.broadcast_to(keys[:, 0:1], keys.shape))
            inside = lax.broadcasted_iota(jnp.int32, mixed.shape, 0) < valid
            values[c] = jnp.where(inside, mixed, jnp.zeros_like(mixed))


def doubled(both):
    turned = both.T
    keys = jnp.concatenate([turned[:HD], turned[:HD]], axis=0)
    side = lax.broadcasted_iota(jnp.int32, both.shape, 1)
    return keys, jnp.where(side < HD, jnp.ones_like(both), both)


def prepare_cache(length, pages, pool):
    n_pages = pool.shape[0]
    chunks = pl.cdiv(n_pages * PAGE, CHUNK)
    return pl.pallas_call(
        cache_kernel,
        out_shape=[
            jax.ShapeDtypeStruct((chunks, 2 * HD, CHUNK), BF16),
            jax.ShapeDtypeStruct((chunks, CHUNK, 2 * HD), BF16),
        ],
        in_specs=[SMEM, SMEM, ANY],
        out_specs=[VMEM, VMEM],
        scratch_shapes=[
            pltpu.VMEM((chunks * CHUNK, 2 * HD), BF16),
            pltpu.SemaphoreType.DMA((chunks * (CHUNK // PAGE),)),
        ],
        compiler_params=pltpu.CompilerParams(vmem_limit_bytes=32 * 2**20),
        cost_estimate=pl.CostEstimate(flops=2 * 10**9, bytes_accessed=6 * 2**20, transcendentals=0),
    )(length, pages, pool)


def prefill_kernel(positions, scal, msg, old_flipped, old_values, decoded, out, flipped, values, queries, scores, top, total):
    blocks = msg.shape[0]
    stretch = blocks * positions
    half = positions // 2
    used = pl.cdiv(scal[0], CHUNK)
    steps = stretch // CHUNK

    @pl.loop(0, blocks)
    def _(b):
        packed = msg[b, pl.ds(positions, half), :].astype(F32) * (SCALE * LOG2E)
        high = packed.astype(BF16)
        low = (packed - high.astype(F32)).astype(BF16)
        row = pl.multiple_of(b * positions, positions)
        for part in range(2):
            lanes = slice(part * HD, (part + 1) * HD)
            queries[pl.ds(row + part * half, half), :] = jnp.concatenate([high[:, lanes], low[:, lanes]], axis=1)

    for c in range(steps):
        for k in range(CHUNK // positions):
            keys, mixed = doubled(msg[c * (CHUNK // positions) + k, 0:positions, :])
            flipped[c, :, k * positions : (k + 1) * positions] = keys
            values[c, k * positions : (k + 1) * positions, :] = mixed
    slots, features = decoded.shape
    for k in range(0, features // 128, 2):
        pair = jnp.concatenate([decoded[:, k * 128 : (k + 1) * 128], decoded[:, (k + 1) * 128 : (k + 2) * 128]], axis=0)
        pair = pair.astype(BF16)
        for b in range(blocks):
            out[b, half + k * slots : half + (k + 2) * slots, :] = pair

    def raise_top(s):
        best = top[...]
        for k in range(CHUNK // 128):
            best = jnp.maximum(best, s[:, k * 128 : (k + 1) * 128])
        top[...] = best

    def score(i, spot, keys, diagonal=False):
        q = queries[pl.ds(pl.multiple_of(i * CHUNK, CHUNK), CHUNK), :]
        s = jnp.dot(q, keys, preferred_element_type=F32)
        if diagonal:
            rows = lax.broadcasted_iota(jnp.int32, (CHUNK, CHUNK), 0)
            cols = lax.broadcasted_iota(jnp.int32, (CHUNK, CHUNK), 1)
            s = jnp.where(cols <= rows, s, MASKED)
        scores[spot] = s
        raise_top(s)

    def settle():
        best = jnp.max(top[...], axis=1, keepdims=True)
        total[1] = jnp.broadcast_to(best, (CHUNK, 128))
        top[...] = jnp.full_like(top, -jnp.inf)
        total[0] = jnp.zeros((CHUNK, 128), F32)

    def mix(spot, rows):
        best = total[1]
        s = scores[spot]
        weights = jnp.concatenate(
            [jnp.exp2(s[:, k * 128 : (k + 1) * 128] - best).astype(BF16) for k in range(CHUNK // 128)], axis=1
        )
        total[0] += jnp.dot(weights, rows, preferred_element_type=F32)

    def emit(i):
        done = total[0]
        mixed = (done[:, HD:] / done[:, :HD]).astype(BF16)
        for k in range(CHUNK // positions):
            part = mixed[k * positions : (k + 1) * positions]
            out[i * (CHUNK // positions) + k, 0:half, :] = jnp.concatenate([part[:half], part[half:]], axis=1)

    top[...] = jnp.full_like(top, -jnp.inf)

    @pl.loop(0, used)
    def _(c):
        score(0, c, old_flipped[c])

    score(0, used, flipped[0], diagonal=True)
    settle()

    @pl.loop(1, steps)
    def _(i):
        @pl.loop(0, used)
        def _(c):
            mix(c, old_values[c])
            score(i, c, old_flipped[c])

        @pl.loop(0, i)
        def _(c):
            mix(used + c, values[c])
            score(i, used + c, flipped[c])

        emit(i - 1)
        score(i, used + i, flipped[i], diagonal=True)
        settle()

    @pl.loop(0, used)
    def _(c):
        mix(c, old_values[c])

    @pl.loop(0, steps)
    def _(c):
        mix(used + c, values[c])

    emit(steps - 1)


def prefill_attention(length, msg, old_flipped, old_values, decoded):
    blocks, rows, _ = msg.shape
    positions = rows * 2 // 3
    stretch = blocks * positions
    steps = stretch // CHUNK
    chunks = old_values.shape[0] + steps
    slots, features = decoded.shape
    keys = chunks * CHUNK
    return pl.pallas_call(
        functools.partial(prefill_kernel, positions),
        out_shape=jax.ShapeDtypeStruct((blocks, positions // 2 + slots * features // 128, 2 * HD), BF16),
        in_specs=[SMEM, VMEM, VMEM, VMEM, VMEM],
        out_specs=VMEM,
        scratch_shapes=[
            pltpu.VMEM((steps, 2 * HD, CHUNK), BF16),
            pltpu.VMEM((steps, CHUNK, 2 * HD), BF16),
            pltpu.VMEM((stretch, 2 * HD), BF16),
            pltpu.VMEM((chunks, CHUNK, CHUNK), F32),
            pltpu.VMEM((CHUNK, 128), F32),
            pltpu.VMEM((2, CHUNK, 128), F32),
        ],
        compiler_params=pltpu.CompilerParams(vmem_limit_bytes=46 * 2**20),
        cost_estimate=pl.CostEstimate(flops=4 * stretch * keys * HD, bytes_accessed=4 * 2**20, transcendentals=stretch * keys),
    )(length, msg, old_flipped, old_values, decoded)


def decode_kernel(heads, scal, pages, x, gain, w, pool, out, buf, wbuf, normed, qrows, cacherows, rowout, bests, totals, mixes, owners, wsems, sems):
    slots = pages.shape[0]
    width = heads * 2 * HD
    per_group = BLOCK // PAGE
    depth = pages.shape[1]
    most = buf.shape[0] // BLOCK
    w_copies = [pltpu.make_async_copy(w.at[j], wbuf.at[j], wsems.at[j]) for j in range(3)]
    for copy in w_copies:
        copy.start()

    def page_copy(item, k):
        page = pages[owners[0, item], jnp.minimum(owners[2, item] * per_group + k, depth - 1)]
        place = item * per_group + k
        return pltpu.make_async_copy(
            pool.at[page], buf.at[pl.ds(pl.multiple_of(place * PAGE, PAGE), PAGE), :], sems.at[place]
        )

    def groups(s):
        return pl.cdiv(scal[s], BLOCK)

    @pl.loop(0, most + UNROLL)
    def _(item):
        owners[0, item] = 0
        owners[1, item] = 0
        owners[2, item] = 0

    def begin(s, start):
        @pl.loop(0, groups(s))
        def _(g):
            owners[0, start + g] = s
            owners[1, start + g] = scal[s] - g * BLOCK
            owners[2, start + g] = g

        return start + groups(s)

    items = lax.fori_loop(0, slots, begin, 0)

    def fetch(item):
        @pl.when(item < items)
        def _():
            for k in range(per_group):
                page_copy(item, k).start()

    for item in range(AHEAD):
        fetch(item)
    values = x[...].astype(F32)
    inverse = lax.rsqrt(jnp.mean(values * values, axis=-1, keepdims=True) + EPSILON)
    normed[...] = (values * inverse * gain[...]).astype(BF16)
    rows = values.shape[0]
    zero = jnp.zeros((rows, HD), F32)
    parts = []
    for j in range(3):
        w_copies[j].wait()
        parts.append(jnp.dot(normed[...], wbuf[j], preferred_element_type=F32).astype(BF16).astype(F32))
    for g in range(heads):
        cut = slice(g * HD, (g + 1) * HD)
        span = slice(g * 2 * HD, (g + 1) * 2 * HD)
        qrows[:, span] = jnp.concatenate([parts[0][:, cut] * SCALE, zero], axis=1)
        cacherows[:, span] = jnp.concatenate([parts[1][:, cut], parts[2][:, cut]], axis=1)
    owner = lax.broadcasted_iota(jnp.int32, (8, width), 1) // (2 * HD)
    diagonal = owner == lax.broadcasted_iota(jnp.int32, (8, width), 0)

    def spread(s):
        row = scal[slots + s]
        return jnp.where(diagonal, jnp.broadcast_to(qrows[pl.ds(row, 1), :], (8, width)), 0.0)

    @pl.loop(0, pl.cdiv(items, UNROLL))
    def _(turn):
        for u in range(UNROLL):
            @pl.when(turn * UNROLL + u < items)
            def _():
                for k in range(per_group):
                    page_copy(turn * UNROLL + u, k).wait()

            fetch(turn * UNROLL + u + AHEAD)
        for u in range(UNROLL):
            item = turn * UNROLL + u
            place = jnp.minimum(item, most - 1)
            cache = buf[pl.ds(pl.multiple_of(place * BLOCK, BLOCK), BLOCK), :]
            query = spread(owners[0, item]).astype(BF16)
            s = contract_last(query, cache)
            s = jnp.where(lax.broadcasted_iota(jnp.int32, (8, BLOCK), 1) < owners[1, item], s, MASKED)
            best = jnp.max(s, axis=1, keepdims=True)
            weights = jnp.exp(s - best)
            bests[item] = jnp.broadcast_to(best, (8, 128))
            totals[item] = jnp.broadcast_to(jnp.sum(weights, axis=1, keepdims=True), (8, 128))
            mixes[item] = jnp.dot(weights.astype(BF16), cache, preferred_element_type=F32)

    most_items = pl.cdiv(depth * PAGE, BLOCK)
    start = 0
    for s in range(slots):
        own = jnp.broadcast_to(cacherows[pl.ds(scal[slots + s], 1), :], (8, width))
        own_score = jnp.sum(spread(s) * own, axis=1, keepdims=True)
        count = groups(s)
        held = [jnp.where(i < count, bests[start + i], -jnp.inf) for i in range(most_items)]
        best = functools.reduce(jnp.maximum, held, jnp.broadcast_to(own_score, (8, 128)))
        own_weight = jnp.exp(own_score - best[:, 0:1])
        total = own_weight
        mixed = own_weight.astype(BF16).astype(F32) * own
        for i in range(most_items):
            share = jnp.exp(held[i] - best)[:, 0:1]
            total = total + jnp.where(i < count, totals[start + i][:, 0:1], 0.0) * share
            mixed = mixed + jnp.where(i < count, mixes[start + i], 0.0) * share
        mixed = jnp.where(diagonal, mixed / total, 0.0)
        rowout[s : s + 1, :] = jnp.sum(mixed, axis=0, keepdims=True)
        start = start + count
    done = rowout[...]
    for g in range(0, heads, 2):
        out[:, g * HD : (g + 2) * HD] = jnp.concatenate(
            [done[:, g * 2 * HD + HD : (g + 1) * 2 * HD], done[:, (g + 1) * 2 * HD + HD : (g + 2) * 2 * HD]], axis=1
        )


def decode_attention(scal, pages, x, gain, w, pool):
    slots = pages.shape[0]
    features = w.shape[2]
    heads = features // HD
    width = heads * 2 * HD
    rows = x.shape[0]
    per_group = BLOCK // PAGE
    most = pl.cdiv(pool.shape[0] + slots * (per_group - 1), per_group)
    spare = max(UNROLL, pl.cdiv(pages.shape[1], per_group))
    return pl.pallas_call(
        functools.partial(decode_kernel, heads),
        out_shape=jax.ShapeDtypeStruct((slots, features), F32),
        in_specs=[SMEM, SMEM, VMEM, VMEM, ANY, ANY],
        out_specs=VMEM,
        scratch_shapes=[
            pltpu.VMEM((most * BLOCK, width), BF16),
            pltpu.VMEM(w.shape, BF16),
            pltpu.VMEM(x.shape, BF16),
            pltpu.VMEM((rows, width), F32),
            pltpu.VMEM((rows, width), F32),
            pltpu.VMEM((slots, width), F32),
            pltpu.VMEM((most + spare, 8, 128), F32),
            pltpu.VMEM((most + spare, 8, 128), F32),
            pltpu.VMEM((most + spare, 8, width), F32),
            pltpu.SMEM((3, most + UNROLL), jnp.int32),
            pltpu.SemaphoreType.DMA((3,)),
            pltpu.SemaphoreType.DMA((most * per_group,)),
        ],
        compiler_params=pltpu.CompilerParams(vmem_limit_bytes=56 * 2**20),
        cost_estimate=pl.CostEstimate(flops=2 * 10**9, bytes_accessed=22 * 2**20, transcendentals=10**6),
    )(scal, pages, x, gain, w, pool)


def qkv_kernel(requests, heads, home, gain, x, w, out, xbuf, wbuf, normed, sems):
    rows = x.shape[0]
    positions = rows // requests
    half = positions // 2
    x_copy = pltpu.make_async_copy(x, xbuf, sems.at[3])
    x_copy.start()
    w_copies = [pltpu.make_async_copy(w.at[j], wbuf.at[j], sems.at[j]) for j in range(3)]
    for copy in w_copies:
        copy.start()
    x_copy.wait()
    values = xbuf[...].astype(F32)
    inverse = lax.rsqrt(jnp.mean(values * values, axis=-1, keepdims=True) + EPSILON)
    normed[...] = (values * inverse * gain[...]).astype(BF16)

    def project(j):
        w_copies[j].wait()
        return jnp.dot(normed[...], wbuf[j], preferred_element_type=F32).astype(BF16)

    y = project(0)
    for r in range(requests):
        for g in range(heads):
            part = y[r * positions : (r + 1) * positions, g * HD : (g + 1) * HD]
            out[home[r * heads + g], positions : positions + half, :] = jnp.concatenate([part[:half], part[half:]], axis=1)
    keys = project(1)
    y = project(2)
    for r in range(requests):
        span = slice(r * positions, (r + 1) * positions)
        for g in range(heads):
            cut = slice(g * HD, (g + 1) * HD)
            out[home[r * heads + g], 0:positions, :] = jnp.concatenate([keys[span, cut], y[span, cut]], axis=1)


def qkv_messages(home, x, gain, w, requests):
    rows, width = x.shape
    features = w.shape[2]
    heads = features // HD
    units = requests * heads
    positions = rows // requests
    return pl.pallas_call(
        functools.partial(qkv_kernel, requests, heads),
        out_shape=jax.ShapeDtypeStruct((units, positions * 3 // 2, 2 * HD), BF16),
        in_specs=[SMEM, VMEM, ANY, ANY],
        out_specs=VMEM,
        scratch_shapes=[
            pltpu.VMEM((rows, width), BF16),
            pltpu.VMEM(w.shape, BF16),
            pltpu.VMEM((rows, width), BF16),
            pltpu.SemaphoreType.DMA((4,)),
        ],
        compiler_params=pltpu.CompilerParams(vmem_limit_bytes=58 * 2**20),
        cost_estimate=pl.CostEstimate(flops=2 * rows * width * 3 * features, bytes_accessed=10 * 2**20, transcendentals=0),
    )(home, gain, x, w)


def project_kernel(requests, heads, scal, received, w_out, *rest):
    outs, rows_in, decode_in = rest[:-2], rest[-2], rest[-1]
    n_head = len(outs)
    n_tok = received.shape[0]
    units = requests * heads
    per = outs[0].shape[0]
    features = w_out.shape[0]
    slots = decode_in.shape[0] // n_tok
    half = received.shape[1] - slots * features // 128
    positions = 2 * half
    block_rows = positions // n_head
    share = per - requests * block_rows
    hosted = share * n_head
    for b in range(n_tok):
        for k in range(0, features // 128, 2):
            pair = received[b, half + k * slots : half + (k + 2) * slots, :].astype(F32)
            for j in range(2):
                decode_in[b * slots : (b + 1) * slots, (k + j) * 128 : (k + j + 1) * 128] = pair[
                    j * slots : (j + 1) * slots
                ]
    rows_in[...] = jnp.zeros_like(rows_in)
    for r in range(requests):
        for g in range(0, heads, 2):
            left = received[scal[r * heads + g], 0:half, :].astype(F32)
            right = received[scal[r * heads + g + 1], 0:half, :].astype(F32)
            both = jnp.concatenate(
                [
                    jnp.concatenate([left[:, :HD], right[:, :HD]], axis=1),
                    jnp.concatenate([left[:, HD:], right[:, HD:]], axis=1),
                ],
                axis=0,
            )
            for h in range(n_head):
                rows_in[h, r * block_rows : (r + 1) * block_rows, g * HD : (g + 2) * HD] = both[
                    h * block_rows : (h + 1) * block_rows
                ]
    for j in range(hosted):
        rows_in[j // share, requests * block_rows + j % share, :] = decode_in[pl.ds(scal[units + j], 1), :][0]
    for k in range(n_head):
        mine = rows_in[scal[units + hosted + k]].astype(BF16)
        y = jnp.dot(mine, w_out[...], preferred_element_type=F32).astype(BF16)
        outs[k][...] = y[:per]


def project_out(scal, received, w_out, requests, heads, n_head, hosted):
    features, width = w_out.shape
    positions = 2 * (received.shape[1] - hosted * features // 128)
    per = requests * (positions // n_head) + hosted // n_head
    padded = -(-per // 16) * 16
    return pl.pallas_call(
        functools.partial(project_kernel, requests, heads),
        out_shape=[jax.ShapeDtypeStruct((per, width), BF16)] * n_head,
        in_specs=[SMEM, VMEM, VMEM],
        out_specs=[VMEM] * n_head,
        scratch_shapes=[
            pltpu.VMEM((n_head, padded, features), F32),
            pltpu.VMEM((received.shape[0] * hosted, features), F32),
        ],
        compiler_params=pltpu.CompilerParams(vmem_limit_bytes=32 * 2**20),
        cost_estimate=pl.CostEstimate(flops=2 * n_head * per * features * width, bytes_accessed=4 * 2**20, transcendentals=0),
    )(scal, received, w_out)


def middle_kernel(own_pre, own_dec, gain, *rest):
    terms, (resid, normed) = rest[:-2], rest[-2:]
    split = own_pre.shape[0]
    for rows, own in ((slice(0, split), own_pre), (slice(split, resid.shape[0]), own_dec)):
        values = own[...].astype(F32)
        for term in terms:
            values = values + term[rows, :].astype(F32)
        resid[rows, :] = values
        inverse = lax.rsqrt(jnp.mean(values * values, axis=-1, keepdims=True) + EPSILON)
        normed[rows, :] = (values * inverse * gain[...]).astype(BF16)


def middle(own_pre, own_dec, gain, terms):
    shape = terms[0].shape
    return pl.pallas_call(
        middle_kernel,
        out_shape=[jax.ShapeDtypeStruct(shape, F32), jax.ShapeDtypeStruct(shape, BF16)],
        in_specs=[VMEM] * (3 + len(terms)),
        out_specs=[VMEM] * 2,
        compiler_params=pltpu.CompilerParams(vmem_limit_bytes=16 * 2**20),
        cost_estimate=pl.CostEstimate(flops=10**6, bytes_accessed=2 * 2**20, transcendentals=0),
    )(own_pre, own_dec, gain, *terms)


def feed_kernel(count, *refs):
    rows, (gate_up, down), outs = refs[:count], refs[count : count + 2], refs[count + 2 : 2 * count + 2]
    weights, down_weights, sems = refs[2 * count + 2 :]
    hidden_units = down.shape[0]
    tile = 128 if hidden_units % 128 == 0 else hidden_units
    steps = hidden_units // tile

    def load(step):
        cols = pl.ds(step * tile, tile)
        return pltpu.make_async_copy(gate_up.at[:, :, cols], weights.at[:, :, cols], sems.at[step])

    for step in range(steps):
        load(step).start()
    down_copy = pltpu.make_async_copy(down, down_weights, sems.at[steps])
    down_copy.start()
    hidden = [[] for _ in range(count)]
    for step in range(steps):
        load(step).wait()
        cols = slice(step * tile, (step + 1) * tile)
        both = jnp.concatenate([weights[0, :, cols], weights[1, :, cols]], axis=1) if tile == 128 else None
        for index in range(count):
            if tile == 128:
                y = jnp.dot(rows[index][...], both, preferred_element_type=F32)
                gate, upper = y[:, :tile], y[:, tile:]
            else:
                gate = jnp.dot(rows[index][...], weights[0], preferred_element_type=F32)
                upper = jnp.dot(rows[index][...], weights[1], preferred_element_type=F32)
            hidden[index].append((jax.nn.gelu(gate, approximate=True) * upper).astype(BF16))
    down_copy.wait()
    for index in range(count):
        full = jnp.concatenate(hidden[index], axis=1)
        outs[index][...] = jnp.dot(full, down_weights[...], preferred_element_type=F32).astype(BF16)


def feed_forward(chunks, gate_up, down):
    count = len(chunks)
    per, width = chunks[0].shape
    hidden_units = down.shape[0]
    return pl.pallas_call(
        functools.partial(feed_kernel, count),
        out_shape=[jax.ShapeDtypeStruct((per, width), BF16)] * count,
        in_specs=[VMEM] * count + [ANY, ANY],
        out_specs=[VMEM] * count,
        scratch_shapes=[
            pltpu.VMEM(gate_up.shape, BF16),
            pltpu.VMEM(down.shape, BF16),
            pltpu.SemaphoreType.DMA((hidden_units // 128 + 1,)),
        ],
        compiler_params=pltpu.CompilerParams(vmem_limit_bytes=32 * 2**20),
        cost_estimate=pl.CostEstimate(
            flops=6 * count * per * width * hidden_units, bytes_accessed=8 * 2**20, transcendentals=count * per * hidden_units
        ),
    )(*chunks, gate_up, down)


def ring_of(n_tok):
    if n_tok == 8:
        return [0, 2, 4, 6, 7, 5, 3, 1]
    return list(range(n_tok))


def shards(
    prefill_states,
    decode_states,
    attn_gain,
    w_qkv,
    w_out,
    ffn_gain,
    w_gate_up,
    w_down,
    prefill_pool,
    prefill_pages,
    prefill_lengths,
    prefill_home,
    decode_pool,
    decode_pages,
    decode_lengths,
    decode_home,
):
    n_tok = lax.axis_size("tok")
    n_head = lax.axis_size("head")
    my_tok = lax.axis_index("tok")
    my_head = lax.axis_index("head")
    requests, positions, width = prefill_states.shape
    hosted = decode_states.shape[0]
    features = w_qkv.shape[2]
    heads = features // HD
    units = requests * heads
    ring = ring_of(n_tok)
    ahead = [(ring[i], ring[(i + 1) % n_tok]) for i in range(n_tok)]
    behind = [(b, a) for a, b in ahead]
    far = n_tok // 2
    near = (n_tok - 1) // 2

    def joined(part, other):
        return (part.astype(F32) + other.astype(F32)).astype(BF16)

    gain = attn_gain.reshape(1, width)
    w_three = jnp.transpose(w_qkv, (1, 0, 2))
    unit_ids = jnp.arange(units, dtype=jnp.int32)
    my_unit = jnp.sum(jnp.where(prefill_home == my_tok, unit_ids, 0))
    length = lax.dynamic_slice_in_dim(prefill_lengths, my_unit // heads, 1, 0)
    slots = my_tok * hosted + jnp.arange(hosted, dtype=jnp.int32)
    all_requests = jnp.arange(decode_home.shape[0], dtype=jnp.int32)
    anchor = jnp.sum(jnp.where(decode_home[None, :] == slots[:, None], all_requests[None, :], 0), axis=1)
    anchor_row = ((anchor // hosted) ^ my_tok) * hosted + anchor % hosted

    first = lax.ppermute(decode_states, "tok", [(i, i ^ 1) for i in range(n_tok)])
    messages = qkv_messages(prefill_home, prefill_states.reshape(requests * positions, width), gain, w_three, requests)
    messages, first = lax.optimization_barrier((messages, first))
    pair = jnp.concatenate([decode_states, first], axis=0)
    rows = [pair] + [lax.ppermute(pair, "tok", [(i, i ^ step) for i in range(n_tok)]) for step in range(2, n_tok, 2)]
    held = lax.optimization_barrier([messages] + rows)
    messages, rows = held[0], held[1:]
    arrived = lax.all_to_all(messages, "tok", split_axis=0, concat_axis=0, tiled=True)
    rows = jnp.concatenate(rows, axis=0)
    decoded = decode_attention(
        jnp.concatenate([decode_lengths, anchor_row]), decode_pages, rows, gain, w_three, decode_pool
    )
    old_keys, old_values = prepare_cache(length, prefill_pages.reshape(-1), prefill_pool)
    arrived, decoded, old_keys, old_values = lax.optimization_barrier((arrived, decoded, old_keys, old_values))
    attn = prefill_attention(length, arrived, old_keys, old_values, decoded)
    attn, w_gate_up = lax.optimization_barrier((attn, w_gate_up))
    returned = lax.all_to_all(attn, "tok", split_axis=0, concat_axis=0, tiled=True)
    gate_up = jnp.transpose(w_gate_up, (1, 0, 2))
    returned, gate_up = lax.optimization_barrier((returned, gate_up))

    my_slots = lax.dynamic_slice_in_dim(decode_home, my_tok * hosted, hosted, 0)
    targets = my_head ^ jnp.arange(n_head, dtype=jnp.int32)
    parts = project_out(
        jnp.concatenate([prefill_home, my_slots, targets]), returned, w_out, requests, heads, n_head, hosted
    )
    block_rows = positions // n_head
    share = hosted // n_head
    own_pre = lax.dynamic_slice_in_dim(prefill_states, my_head * block_rows, block_rows, 1)
    own_dec = lax.dynamic_slice_in_dim(decode_states, my_head * share, share, 0)
    terms = [parts[0]]
    swap = [(i, i ^ 1) for i in range(n_head)]
    for k in range(2, n_head, 2):
        both = joined(parts[k], lax.ppermute(parts[k + 1], "head", swap))
        terms.append(lax.ppermute(both, "head", [(i, i ^ k) for i in range(n_head)]))
    terms.append(lax.ppermute(parts[1], "head", swap))
    resid, normed_mid = middle(own_pre.reshape(requests * block_rows, width), own_dec, ffn_gain.reshape(1, width), terms)

    plus, minus = {}, {}
    up, down = normed_mid, normed_mid
    waiting = [normed_mid]
    for k in range(1, far + 1):
        up = lax.ppermute(up, "tok", ahead)
        if k <= near:
            down = lax.ppermute(down, "tok", behind)
        done = feed_forward(waiting, gate_up, w_down)
        up, down, done = lax.optimization_barrier((up, down, done))
        if k == 1:
            (own_part,) = done
        else:
            minus[k - 1], plus[k - 1] = done
        waiting = [up, down]
    (minus[far],) = feed_forward([up], gate_up, w_down)
    plus[far] = minus[far]

    up, down = plus[far], minus[near]
    for k in range(far - 1, 0, -1):
        up = joined(plus[k], lax.ppermute(up, "tok", ahead))
        if k < near:
            down = joined(minus[k], lax.ppermute(down, "tok", behind))
    up = lax.ppermute(up, "tok", ahead).astype(F32)
    down = lax.ppermute(down, "tok", behind).astype(F32)
    result = (resid + (own_part.astype(F32) + up + down)).astype(BF16)
    prefill_out = result[: requests * block_rows].reshape(requests, block_rows, width)
    return (prefill_out, result[requests * block_rows :])


def solution(mesh):
    placed = (
        P(None, "tok", None),
        P("tok", None),
        P(),
        P(None, None, "head"),
        P("head", None),
        P(),
        P(None, None, "tok"),
        P("tok", None),
        P("tok", None, "head"),
        P("tok", None),
        P(),
        P(),
        P("tok", None, "head"),
        P("tok", None),
        P("tok"),
        P(),
    )
    return jax.shard_map(
        shards,
        mesh=mesh,
        in_specs=placed,
        out_specs=(P(None, ("tok", "head"), None), P(("tok", "head"), None)),
        check_vma=False,
    )
```

```python
import functools
import jax
import jax.numpy as jnp
from jax import lax
from jax.experimental import pallas as pl
from jax.experimental.pallas import tpu as pltpu
from jax.sharding import PartitionSpec as P

HD = 64
PAGE = 128
EPSILON = 1e-06
SCALE = 0.125
MASKED = -1e30
LOG2E = 1.4426950408889634
BLOCK = 512
CHUNK = 1024
UNROLL = 2
AHEAD = 6
F32 = jnp.float32
BF16 = jnp.bfloat16
VMEM = pl.BlockSpec(memory_space=pltpu.VMEM)
SMEM = pl.BlockSpec(memory_space=pltpu.SMEM)
ANY = pl.BlockSpec(memory_space=pl.ANY)


def contract_last(left, right):
    return lax.dot_general(left, right, (((1,), (1,)), ((), ())), preferred_element_type=F32)


def cache_kernel(scal, pages, pool, flipped, values, raw, sems):
    length = scal[0]
    used = pl.cdiv(length, CHUNK)
    per_chunk = CHUNK // PAGE
    last = pages.shape[0] - 1

    def page_copy(index):
        page = pages[jnp.minimum(index, last)]
        return pltpu.make_async_copy(
            pool.at[page], raw.at[pl.ds(pl.multiple_of(index * PAGE, PAGE), PAGE), :], sems.at[index]
        )

    @pl.loop(0, used * per_chunk)
    def _(index):
        page_copy(index).start()

    @pl.loop(0, used)
    def _(c):
        for k in range(per_chunk):
            page_copy(c * per_chunk + k).wait()
        keys, mixed = doubled(raw[pl.ds(pl.multiple_of(c * CHUNK, CHUNK), CHUNK), :])
        flipped[c] = keys
        values[c] = mixed

        @pl.when(length - c * CHUNK < CHUNK)
        def _():
            valid = length - c * CHUNK
            columns = lax.broadcasted_iota(jnp.int32, keys.shape, 1) < valid
            flipped[c] = jnp.where(columns, keys, jnp.broadcast_to(keys[:, 0:1], keys.shape))
            inside = lax.broadcasted_iota(jnp.int32, mixed.shape, 0) < valid
            values[c] = jnp.where(inside, mixed, jnp.zeros_like(mixed))


def doubled(both):
    turned = both.T
    keys = jnp.concatenate([turned[:HD], turned[:HD]], axis=0)
    side = lax.broadcasted_iota(jnp.int32, both.shape, 1)
    return keys, jnp.where(side < HD, jnp.ones_like(both), both)


def prepare_cache(length, pages, pool):
    n_pages = pool.shape[0]
    chunks = pl.cdiv(n_pages * PAGE, CHUNK)
    return pl.pallas_call(
        cache_kernel,
        out_shape=[
            jax.ShapeDtypeStruct((chunks, 2 * HD, CHUNK), BF16),
            jax.ShapeDtypeStruct((chunks, CHUNK, 2 * HD), BF16),
        ],
        in_specs=[SMEM, SMEM, ANY],
        out_specs=[VMEM, VMEM],
        scratch_shapes=[
            pltpu.VMEM((chunks * CHUNK, 2 * HD), BF16),
            pltpu.SemaphoreType.DMA((chunks * (CHUNK // PAGE),)),
        ],
        compiler_params=pltpu.CompilerParams(vmem_limit_bytes=60 * 2**20),
        cost_estimate=pl.CostEstimate(flops=2 * 10**9, bytes_accessed=6 * 2**20, transcendentals=0),
    )(length, pages, pool)


def prefill_kernel(
    positions, scal, msg, flipped_in, values_in, decoded, out,
    old_flipped, old_values, flipped, values, queries, scores, top, total, sems,
):
    blocks = msg.shape[0]
    stretch = blocks * positions
    half = positions // 2
    used = pl.cdiv(scal[0], CHUNK)
    steps = stretch // CHUNK
    loads = [
        pltpu.make_async_copy(flipped_in, old_flipped, sems.at[0]),
        pltpu.make_async_copy(values_in, old_values, sems.at[1]),
    ]
    for load in loads:
        load.start()

    @pl.loop(0, blocks)
    def _(b):
        packed = msg[b, pl.ds(positions, half), :].astype(F32) * (SCALE * LOG2E)
        high = packed.astype(BF16)
        low = (packed - high.astype(F32)).astype(BF16)
        row = pl.multiple_of(b * positions, positions)
        for part in range(2):
            lanes = slice(part * HD, (part + 1) * HD)
            queries[pl.ds(row + part * half, half), :] = jnp.concatenate([high[:, lanes], low[:, lanes]], axis=1)

    for c in range(steps):
        for k in range(CHUNK // positions):
            keys, mixed = doubled(msg[c * (CHUNK // positions) + k, 0:positions, :])
            flipped[c, :, k * positions : (k + 1) * positions] = keys
            values[c, k * positions : (k + 1) * positions, :] = mixed
    slots, features = decoded.shape
    for k in range(0, features // 128, 2):
        pair = jnp.concatenate([decoded[:, k * 128 : (k + 1) * 128], decoded[:, (k + 1) * 128 : (k + 2) * 128]], axis=0)
        pair = pair.astype(BF16)
        for b in range(blocks):
            out[b, half + k * slots : half + (k + 2) * slots, :] = pair

    def raise_top(s):
        best = top[...]
        for k in range(CHUNK // 128):
            best = jnp.maximum(best, s[:, k * 128 : (k + 1) * 128])
        top[...] = best

    def score(i, spot, keys, diagonal=False):
        q = queries[pl.ds(pl.multiple_of(i * CHUNK, CHUNK), CHUNK), :]
        s = jnp.dot(q, keys, preferred_element_type=F32)
        if diagonal:
            rows = lax.broadcasted_iota(jnp.int32, (CHUNK, CHUNK), 0)
            cols = lax.broadcasted_iota(jnp.int32, (CHUNK, CHUNK), 1)
            s = jnp.where(cols <= rows, s, MASKED)
        scores[spot] = s
        raise_top(s)

    def settle():
        best = jnp.max(top[...], axis=1, keepdims=True)
        total[1] = jnp.broadcast_to(best, (CHUNK, 128))
        top[...] = jnp.full_like(top, -jnp.inf)
        total[0] = jnp.zeros((CHUNK, 128), F32)

    def mix(spot, rows):
        best = total[1]
        s = scores[spot]
        weights = jnp.concatenate(
            [jnp.exp2(s[:, k * 128 : (k + 1) * 128] - best).astype(BF16) for k in range(CHUNK // 128)], axis=1
        )
        total[0] += jnp.dot(weights, rows, preferred_element_type=F32)

    def emit(i):
        done = total[0]
        mixed = (done[:, HD:] / done[:, :HD]).astype(BF16)
        for k in range(CHUNK // positions):
            part = mixed[k * positions : (k + 1) * positions]
            out[i * (CHUNK // positions) + k, 0:half, :] = jnp.concatenate([part[:half], part[half:]], axis=1)

    top[...] = jnp.full_like(top, -jnp.inf)
    for load in loads:
        load.wait()

    @pl.loop(0, used)
    def _(c):
        score(0, c, old_flipped[c])

    score(0, used, flipped[0], diagonal=True)
    settle()

    @pl.loop(1, steps)
    def _(i):
        @pl.loop(0, used)
        def _(c):
            mix(c, old_values[c])
            score(i, c, old_flipped[c])

        @pl.loop(0, i)
        def _(c):
            mix(used + c, values[c])
            score(i, used + c, flipped[c])

        emit(i - 1)
        score(i, used + i, flipped[i], diagonal=True)
        settle()

    @pl.loop(0, used)
    def _(c):
        mix(c, old_values[c])

    @pl.loop(0, steps)
    def _(c):
        mix(used + c, values[c])

    emit(steps - 1)


def prefill_attention(length, msg, old_flipped, old_values, decoded):
    blocks, rows, _ = msg.shape
    positions = rows * 2 // 3
    stretch = blocks * positions
    steps = stretch // CHUNK
    chunks = old_values.shape[0] + steps
    slots, features = decoded.shape
    keys = chunks * CHUNK
    return pl.pallas_call(
        functools.partial(prefill_kernel, positions),
        out_shape=jax.ShapeDtypeStruct((blocks, positions // 2 + slots * features // 128, 2 * HD), BF16),
        in_specs=[SMEM, VMEM, ANY, ANY, VMEM],
        out_specs=VMEM,
        scratch_shapes=[
            pltpu.VMEM(old_flipped.shape, BF16),
            pltpu.VMEM(old_values.shape, BF16),
            pltpu.VMEM((steps, 2 * HD, CHUNK), BF16),
            pltpu.VMEM((steps, CHUNK, 2 * HD), BF16),
            pltpu.VMEM((stretch, 2 * HD), BF16),
            pltpu.VMEM((chunks, CHUNK, CHUNK), F32),
            pltpu.VMEM((CHUNK, 128), F32),
            pltpu.VMEM((2, CHUNK, 128), F32),
            pltpu.SemaphoreType.DMA((2,)),
        ],
        compiler_params=pltpu.CompilerParams(vmem_limit_bytes=58 * 2**20),
        cost_estimate=pl.CostEstimate(flops=4 * stretch * keys * HD, bytes_accessed=4 * 2**20, transcendentals=stretch * keys),
    )(length, msg, old_flipped, old_values, decoded)


def decode_kernel(heads, scal, pages, x, gain, w, pool, out, buf, wbuf, normed, qrows, cacherows, rowout, bests, totals, mixes, owners, wsems, sems):
    slots = pages.shape[0]
    width = heads * 2 * HD
    per_group = BLOCK // PAGE
    depth = pages.shape[1]
    most = buf.shape[0] // BLOCK
    w_copies = [pltpu.make_async_copy(w.at[j], wbuf.at[j], wsems.at[j]) for j in range(3)]
    for copy in w_copies:
        copy.start()

    def page_copy(item, k):
        page = pages[owners[0, item], jnp.minimum(owners[2, item] * per_group + k, depth - 1)]
        place = item * per_group + k
        return pltpu.make_async_copy(
            pool.at[page], buf.at[pl.ds(pl.multiple_of(place * PAGE, PAGE), PAGE), :], sems.at[place]
        )

    def groups(s):
        return pl.cdiv(scal[s], BLOCK)

    @pl.loop(0, most + UNROLL)
    def _(item):
        owners[0, item] = 0
        owners[1, item] = 0
        owners[2, item] = 0

    def begin(s, start):
        @pl.loop(0, groups(s))
        def _(g):
            owners[0, start + g] = s
            owners[1, start + g] = scal[s] - g * BLOCK
            owners[2, start + g] = g

        return start + groups(s)

    items = lax.fori_loop(0, slots, begin, 0)

    def fetch(item):
        @pl.when(item < items)
        def _():
            for k in range(per_group):
                page_copy(item, k).start()

    for item in range(AHEAD):
        fetch(item)
    values = x[...].astype(F32)
    inverse = lax.rsqrt(jnp.mean(values * values, axis=-1, keepdims=True) + EPSILON)
    normed[...] = (values * inverse * gain[...]).astype(BF16)
    rows = values.shape[0]
    zero = jnp.zeros((rows, HD), F32)
    parts = []
    for j in range(3):
        w_copies[j].wait()
        parts.append(jnp.dot(normed[...], wbuf[j], preferred_element_type=F32).astype(BF16).astype(F32))
    for g in range(heads):
        cut = slice(g * HD, (g + 1) * HD)
        span = slice(g * 2 * HD, (g + 1) * 2 * HD)
        qrows[:, span] = jnp.concatenate([parts[0][:, cut] * SCALE, zero], axis=1)
        cacherows[:, span] = jnp.concatenate([parts[1][:, cut], parts[2][:, cut]], axis=1)
    owner = lax.broadcasted_iota(jnp.int32, (8, width), 1) // (2 * HD)
    diagonal = owner == lax.broadcasted_iota(jnp.int32, (8, width), 0)

    def spread(s):
        row = scal[slots + s]
        return jnp.where(diagonal, jnp.broadcast_to(qrows[pl.ds(row, 1), :], (8, width)), 0.0)

    @pl.loop(0, pl.cdiv(items, UNROLL))
    def _(turn):
        for u in range(UNROLL):
            @pl.when(turn * UNROLL + u < items)
            def _():
                for k in range(per_group):
                    page_copy(turn * UNROLL + u, k).wait()

            fetch(turn * UNROLL + u + AHEAD)
        for u in range(UNROLL):
            item = turn * UNROLL + u
            place = jnp.minimum(item, most - 1)
            cache = buf[pl.ds(pl.multiple_of(place * BLOCK, BLOCK), BLOCK), :]
            query = spread(owners[0, item]).astype(BF16)
            s = contract_last(query, cache)
            s = jnp.where(lax.broadcasted_iota(jnp.int32, (8, BLOCK), 1) < owners[1, item], s, MASKED)
            best = jnp.max(s, axis=1, keepdims=True)
            weights = jnp.exp(s - best)
            bests[item] = jnp.broadcast_to(best, (8, 128))
            totals[item] = jnp.broadcast_to(jnp.sum(weights, axis=1, keepdims=True), (8, 128))
            mixes[item] = jnp.dot(weights.astype(BF16), cache, preferred_element_type=F32)

    most_items = pl.cdiv(depth * PAGE, BLOCK)
    start = 0
    for s in range(slots):
        own = jnp.broadcast_to(cacherows[pl.ds(scal[slots + s], 1), :], (8, width))
        own_score = jnp.sum(spread(s) * own, axis=1, keepdims=True)
        count = groups(s)
        held = [jnp.where(i < count, bests[start + i], -jnp.inf) for i in range(most_items)]
        best = functools.reduce(jnp.maximum, held, jnp.broadcast_to(own_score, (8, 128)))
        own_weight = jnp.exp(own_score - best[:, 0:1])
        total = own_weight
        mixed = own_weight.astype(BF16).astype(F32) * own
        for i in range(most_items):
            share = jnp.exp(held[i] - best)[:, 0:1]
            total = total + jnp.where(i < count, totals[start + i][:, 0:1], 0.0) * share
            mixed = mixed + jnp.where(i < count, mixes[start + i], 0.0) * share
        mixed = jnp.where(diagonal, mixed / total, 0.0)
        rowout[s : s + 1, :] = jnp.sum(mixed, axis=0, keepdims=True)
        start = start + count
    done = rowout[...]
    for g in range(0, heads, 2):
        out[:, g * HD : (g + 2) * HD] = jnp.concatenate(
            [done[:, g * 2 * HD + HD : (g + 1) * 2 * HD], done[:, (g + 1) * 2 * HD + HD : (g + 2) * 2 * HD]], axis=1
        )


def decode_attention(scal, pages, x, gain, w, pool):
    slots = pages.shape[0]
    features = w.shape[2]
    heads = features // HD
    width = heads * 2 * HD
    rows = x.shape[0]
    per_group = BLOCK // PAGE
    most = pl.cdiv(pool.shape[0] + slots * (per_group - 1), per_group)
    spare = max(UNROLL, pl.cdiv(pages.shape[1], per_group))
    return pl.pallas_call(
        functools.partial(decode_kernel, heads),
        out_shape=jax.ShapeDtypeStruct((slots, features), F32),
        in_specs=[SMEM, SMEM, VMEM, VMEM, ANY, ANY],
        out_specs=VMEM,
        scratch_shapes=[
            pltpu.VMEM((most * BLOCK, width), BF16),
            pltpu.VMEM(w.shape, BF16),
            pltpu.VMEM(x.shape, BF16),
            pltpu.VMEM((rows, width), F32),
            pltpu.VMEM((rows, width), F32),
            pltpu.VMEM((slots, width), F32),
            pltpu.VMEM((most + spare, 8, 128), F32),
            pltpu.VMEM((most + spare, 8, 128), F32),
            pltpu.VMEM((most + spare, 8, width), F32),
            pltpu.SMEM((3, most + UNROLL), jnp.int32),
            pltpu.SemaphoreType.DMA((3,)),
            pltpu.SemaphoreType.DMA((most * per_group,)),
        ],
        compiler_params=pltpu.CompilerParams(vmem_limit_bytes=56 * 2**20),
        cost_estimate=pl.CostEstimate(flops=2 * 10**9, bytes_accessed=22 * 2**20, transcendentals=10**6),
    )(scal, pages, x, gain, w, pool)


def qkv_kernel(requests, heads, home, gain, x, w, out, xbuf, wbuf, normed, sems):
    rows = x.shape[0]
    positions = rows // requests
    half = positions // 2
    x_copy = pltpu.make_async_copy(x, xbuf, sems.at[3])
    x_copy.start()
    w_copies = [pltpu.make_async_copy(w.at[j], wbuf.at[j], sems.at[j]) for j in range(3)]
    for copy in w_copies:
        copy.start()
    x_copy.wait()
    values = xbuf[...].astype(F32)
    inverse = lax.rsqrt(jnp.mean(values * values, axis=-1, keepdims=True) + EPSILON)
    normed[...] = (values * inverse * gain[...]).astype(BF16)

    def project(j):
        w_copies[j].wait()
        return jnp.dot(normed[...], wbuf[j], preferred_element_type=F32).astype(BF16)

    y = project(0)
    for r in range(requests):
        for g in range(heads):
            part = y[r * positions : (r + 1) * positions, g * HD : (g + 1) * HD]
            out[home[r * heads + g], positions : positions + half, :] = jnp.concatenate([part[:half], part[half:]], axis=1)
    keys = project(1)
    y = project(2)
    for r in range(requests):
        span = slice(r * positions, (r + 1) * positions)
        for g in range(heads):
            cut = slice(g * HD, (g + 1) * HD)
            out[home[r * heads + g], 0:positions, :] = jnp.concatenate([keys[span, cut], y[span, cut]], axis=1)


def qkv_messages(home, x, gain, w, requests):
    rows, width = x.shape
    features = w.shape[2]
    heads = features // HD
    units = requests * heads
    positions = rows // requests
    return pl.pallas_call(
        functools.partial(qkv_kernel, requests, heads),
        out_shape=jax.ShapeDtypeStruct((units, positions * 3 // 2, 2 * HD), BF16),
        in_specs=[SMEM, VMEM, ANY, ANY],
        out_specs=VMEM,
        scratch_shapes=[
            pltpu.VMEM((rows, width), BF16),
            pltpu.VMEM(w.shape, BF16),
            pltpu.VMEM((rows, width), BF16),
            pltpu.SemaphoreType.DMA((4,)),
        ],
        compiler_params=pltpu.CompilerParams(vmem_limit_bytes=58 * 2**20),
        cost_estimate=pl.CostEstimate(flops=2 * rows * width * 3 * features, bytes_accessed=10 * 2**20, transcendentals=0),
    )(home, gain, x, w)


def project_kernel(requests, heads, scal, received, w_out, *rest):
    outs, (rows_in, decode_in, weights, sem) = rest[:-4], rest[-4:]
    fetch = pltpu.make_async_copy(w_out, weights, sem)
    fetch.start()
    n_head = len(outs)
    n_tok = received.shape[0]
    units = requests * heads
    per = outs[0].shape[0]
    features = w_out.shape[0]
    slots = decode_in.shape[0] // n_tok
    half = received.shape[1] - slots * features // 128
    positions = 2 * half
    block_rows = positions // n_head
    share = per - requests * block_rows
    hosted = share * n_head
    for b in range(n_tok):
        for k in range(0, features // 128, 2):
            pair = received[b, half + k * slots : half + (k + 2) * slots, :].astype(F32)
            for j in range(2):
                decode_in[b * slots : (b + 1) * slots, (k + j) * 128 : (k + j + 1) * 128] = pair[
                    j * slots : (j + 1) * slots
                ]
    rows_in[...] = jnp.zeros_like(rows_in)
    for r in range(requests):
        for g in range(0, heads, 2):
            left = received[scal[r * heads + g], 0:half, :].astype(F32)
            right = received[scal[r * heads + g + 1], 0:half, :].astype(F32)
            both = jnp.concatenate(
                [
                    jnp.concatenate([left[:, :HD], right[:, :HD]], axis=1),
                    jnp.concatenate([left[:, HD:], right[:, HD:]], axis=1),
                ],
                axis=0,
            )
            for h in range(n_head):
                rows_in[h, r * block_rows : (r + 1) * block_rows, g * HD : (g + 2) * HD] = both[
                    h * block_rows : (h + 1) * block_rows
                ]
    for j in range(hosted):
        rows_in[j // share, requests * block_rows + j % share, :] = decode_in[pl.ds(scal[units + j], 1), :][0]
    fetch.wait()
    for k in range(n_head):
        mine = rows_in[scal[units + hosted + k]].astype(BF16)
        y = jnp.dot(mine, weights[...], preferred_element_type=F32).astype(BF16)
        outs[k][...] = y[:per]


def project_out(scal, received, w_out, requests, heads, n_head, hosted):
    features, width = w_out.shape
    positions = 2 * (received.shape[1] - hosted * features // 128)
    per = requests * (positions // n_head) + hosted // n_head
    padded = -(-per // 16) * 16
    return pl.pallas_call(
        functools.partial(project_kernel, requests, heads),
        out_shape=[jax.ShapeDtypeStruct((per, width), BF16)] * n_head,
        in_specs=[SMEM, VMEM, ANY],
        out_specs=[VMEM] * n_head,
        scratch_shapes=[
            pltpu.VMEM((n_head, padded, features), F32),
            pltpu.VMEM((received.shape[0] * hosted, features), F32),
            pltpu.VMEM(w_out.shape, BF16),
            pltpu.SemaphoreType.DMA,
        ],
        compiler_params=pltpu.CompilerParams(vmem_limit_bytes=56 * 2**20),
        cost_estimate=pl.CostEstimate(flops=2 * n_head * per * features * width, bytes_accessed=4 * 2**20, transcendentals=0),
    )(scal, received, w_out)


def middle_kernel(own_pre, own_dec, gain, *rest):
    terms, (resid, normed) = rest[:-2], rest[-2:]
    split = own_pre.shape[0]
    for rows, own in ((slice(0, split), own_pre), (slice(split, resid.shape[0]), own_dec)):
        values = own[...].astype(F32)
        for term in terms:
            values = values + term[rows, :].astype(F32)
        resid[rows, :] = values
        inverse = lax.rsqrt(jnp.mean(values * values, axis=-1, keepdims=True) + EPSILON)
        normed[rows, :] = (values * inverse * gain[...]).astype(BF16)


def middle(own_pre, own_dec, gain, terms):
    shape = terms[0].shape
    return pl.pallas_call(
        middle_kernel,
        out_shape=[jax.ShapeDtypeStruct(shape, F32), jax.ShapeDtypeStruct(shape, BF16)],
        in_specs=[VMEM] * (3 + len(terms)),
        out_specs=[VMEM] * 2,
        compiler_params=pltpu.CompilerParams(vmem_limit_bytes=16 * 2**20),
        cost_estimate=pl.CostEstimate(flops=10**6, bytes_accessed=2 * 2**20, transcendentals=0),
    )(own_pre, own_dec, gain, *terms)


def finish_kernel(resid, own_left, own_right, *rest):
    sums, outs = rest[:-2], rest[-2:]
    middle = own_left.shape[1]
    first = 0
    for out in outs:
        rows = slice(first, first + out.shape[0])
        first += out.shape[0]
        for side, own in enumerate((own_left, own_right)):
            cols = slice(side * middle, (side + 1) * middle)
            added = own[rows, :].astype(F32)
            for term in sums[2 * side : 2 * side + 2]:
                added = added + term[rows, :].astype(F32)
            out[:, cols] = (resid[rows, cols] + added).astype(BF16)


def finish(resid, own, sums, split):
    per, width = resid.shape
    return pl.pallas_call(
        finish_kernel,
        out_shape=[jax.ShapeDtypeStruct((split, width), BF16), jax.ShapeDtypeStruct((per - split, width), BF16)],
        in_specs=[VMEM] * 7,
        out_specs=[VMEM] * 2,
        compiler_params=pltpu.CompilerParams(vmem_limit_bytes=16 * 2**20),
        cost_estimate=pl.CostEstimate(flops=10**6, bytes_accessed=2 * 2**20, transcendentals=0),
    )(resid, *own, *sums)


def feed_kernel(count, *refs):
    rows, (gate_up, down), outs = refs[:count], refs[count : count + 2], refs[count + 2 :]
    middle = down.shape[1] // 2
    hidden_units = down.shape[0]
    tile = 128 if hidden_units % 128 == 0 else hidden_units
    steps = hidden_units // tile

    hidden = [[] for _ in range(count)]
    for step in range(steps):
        cols = slice(step * tile, (step + 1) * tile)
        both = jnp.concatenate([gate_up[0, :, cols], gate_up[1, :, cols]], axis=1) if tile == 128 else None
        for index in range(count):
            if tile == 128:
                y = jnp.dot(rows[index][...], both, preferred_element_type=F32)
                gate, upper = y[:, :tile], y[:, tile:]
            else:
                gate = jnp.dot(rows[index][...], gate_up[0], preferred_element_type=F32)
                upper = jnp.dot(rows[index][...], gate_up[1], preferred_element_type=F32)
            hidden[index].append((jax.nn.gelu(gate, approximate=True) * upper).astype(BF16))
    for index in range(count):
        full = jnp.concatenate(hidden[index], axis=1)
        for side in range(2):
            cols = slice(side * middle, (side + 1) * middle)
            y = jnp.dot(full, down[:, cols], preferred_element_type=F32)
            outs[2 * index + side][...] = y.astype(BF16)


def feed_forward(chunks, gate_up, down):
    count = len(chunks)
    per, width = chunks[0].shape
    hidden_units = down.shape[0]
    return pl.pallas_call(
        functools.partial(feed_kernel, count),
        out_shape=[jax.ShapeDtypeStruct((per, width // 2), BF16)] * (2 * count),
        in_specs=[VMEM] * (count + 2),
        out_specs=[VMEM] * (2 * count),
        compiler_params=pltpu.CompilerParams(vmem_limit_bytes=24 * 2**20),
        cost_estimate=pl.CostEstimate(
            flops=6 * count * per * width * hidden_units, bytes_accessed=8 * 2**20, transcendentals=count * per * hidden_units
        ),
    )(*chunks, gate_up, down)


def ring_of(n_tok):
    if n_tok == 8:
        return [0, 2, 4, 6, 7, 5, 3, 1]
    return list(range(n_tok))


def shards(
    prefill_states,
    decode_states,
    attn_gain,
    w_qkv,
    w_out,
    ffn_gain,
    w_gate_up,
    w_down,
    prefill_pool,
    prefill_pages,
    prefill_lengths,
    prefill_home,
    decode_pool,
    decode_pages,
    decode_lengths,
    decode_home,
):
    n_tok = lax.axis_size("tok")
    n_head = lax.axis_size("head")
    my_tok = lax.axis_index("tok")
    my_head = lax.axis_index("head")
    requests, positions, width = prefill_states.shape
    hosted = decode_states.shape[0]
    features = w_qkv.shape[2]
    heads = features // HD
    units = requests * heads
    ring = ring_of(n_tok)
    ahead = [(ring[i], ring[(i + 1) % n_tok]) for i in range(n_tok)]
    behind = [(b, a) for a, b in ahead]
    far = n_tok // 2
    near = (n_tok - 1) // 2

    def joined(part, other):
        return (part.astype(F32) + other.astype(F32)).astype(BF16)

    gain = attn_gain.reshape(1, width)
    w_three = jnp.transpose(w_qkv, (1, 0, 2))
    unit_ids = jnp.arange(units, dtype=jnp.int32)
    my_unit = jnp.sum(jnp.where(prefill_home == my_tok, unit_ids, 0))
    length = lax.dynamic_slice_in_dim(prefill_lengths, my_unit // heads, 1, 0)
    slots = my_tok * hosted + jnp.arange(hosted, dtype=jnp.int32)
    all_requests = jnp.arange(decode_home.shape[0], dtype=jnp.int32)
    anchor = jnp.sum(jnp.where(decode_home[None, :] == slots[:, None], all_requests[None, :], 0), axis=1)

    copies = jnp.broadcast_to(decode_states[None], (n_tok, hosted, width))
    rows = lax.all_to_all(copies, "tok", split_axis=0, concat_axis=0, tiled=True).reshape(n_tok * hosted, width)
    messages = qkv_messages(prefill_home, prefill_states.reshape(requests * positions, width), gain, w_three, requests)
    messages, rows = lax.optimization_barrier((messages, rows))
    arrived = lax.all_to_all(messages, "tok", split_axis=0, concat_axis=0, tiled=True)
    decoded = decode_attention(
        jnp.concatenate([decode_lengths, anchor]), decode_pages, rows, gain, w_three, decode_pool
    )
    table, decoded = lax.optimization_barrier((prefill_pages.reshape(-1), decoded))
    old_keys, old_values = prepare_cache(length, table, prefill_pool)
    attn = prefill_attention(length, arrived, old_keys, old_values, decoded)
    returned = lax.all_to_all(attn, "tok", split_axis=0, concat_axis=0, tiled=True)
    gate_up = jnp.transpose(w_gate_up, (1, 0, 2))

    my_slots = lax.dynamic_slice_in_dim(decode_home, my_tok * hosted, hosted, 0)
    targets = my_head ^ jnp.arange(n_head, dtype=jnp.int32)
    parts = project_out(
        jnp.concatenate([prefill_home, my_slots, targets]), returned, w_out, requests, heads, n_head, hosted
    )
    block_rows = positions // n_head
    share = hosted // n_head
    own_pre = lax.dynamic_slice_in_dim(prefill_states, my_head * block_rows, block_rows, 1)
    own_dec = lax.dynamic_slice_in_dim(decode_states, my_head * share, share, 0)
    terms = [parts[0]]
    swap = [(i, i ^ 1) for i in range(n_head)]
    for k in range(2, n_head, 2):
        both = joined(parts[k], lax.ppermute(parts[k + 1], "head", swap))
        terms.append(lax.ppermute(both, "head", [(i, i ^ k) for i in range(n_head)]))
    terms.append(lax.ppermute(parts[1], "head", swap))
    resid, normed_mid = middle(own_pre.reshape(requests * block_rows, width), own_dec, ffn_gain.reshape(1, width), terms)

    plus, minus = {}, {}
    up, down = normed_mid, normed_mid
    waiting = [normed_mid]
    for k in range(1, far + 1):
        up = lax.ppermute(up, "tok", ahead)
        if k <= near:
            down = lax.ppermute(down, "tok", behind)
        done = feed_forward(waiting, gate_up, w_down)
        up, down, done = lax.optimization_barrier((up, down, done))
        if k == 1:
            own_part = done
        else:
            minus[k - 1], plus[k - 1] = done[:2], done[2:]
        waiting = [up, down]
    farthest = feed_forward([up], gate_up, w_down)

    def chain(part, table, side, hops, steps):
        for k in range(hops, 0, -1):
            part = joined(table[k][side], lax.ppermute(part, "tok", steps))
        return lax.ppermute(part, "tok", steps)

    sums = [
        chain(minus[near][0], minus, 0, near - 1, behind),
        chain(farthest[0], plus, 0, far - 1, ahead),
        chain(plus[near][1], plus, 1, near - 1, ahead),
        chain(farthest[1], minus, 1, far - 1, behind),
    ]
    pre, dec = finish(resid, own_part, sums, requests * block_rows)
    return (pre.reshape(requests, block_rows, width), dec)


def solution(mesh):
    placed = (
        P(None, "tok", None),
        P("tok", None),
        P(),
        P(None, None, "head"),
        P("head", None),
        P(),
        P(None, None, "tok"),
        P("tok", None),
        P("tok", None, "head"),
        P("tok", None),
        P(),
        P(),
        P("tok", None, "head"),
        P("tok", None),
        P("tok"),
        P(),
    )
    return jax.shard_map(
        shards,
        mesh=mesh,
        in_specs=placed,
        out_specs=(P(None, ("tok", "head"), None), P(("tok", "head"), None)),
        check_vma=False,
    )
```

```python
import functools
import jax
import jax.numpy as jnp
from jax import lax
from jax.experimental import pallas as pl
from jax.experimental.pallas import tpu as pltpu
from jax.sharding import PartitionSpec as P

HD = 64
PAGE = 128
EPSILON = 1e-06
SCALE = 0.125
MASKED = -1e30
LOG2E = 1.4426950408889634
BLOCK = 512
CHUNK = 1024
UNROLL = 2
AHEAD = 6
F32 = jnp.float32
BF16 = jnp.bfloat16
VMEM = pl.BlockSpec(memory_space=pltpu.VMEM)
SMEM = pl.BlockSpec(memory_space=pltpu.SMEM)
ANY = pl.BlockSpec(memory_space=pl.ANY)


def contract_last(left, right):
    return lax.dot_general(left, right, (((1,), (1,)), ((), ())), preferred_element_type=F32)


def own_length(lengths, home, ids):
    units = home.shape[0]
    heads = units // lengths.shape[0]
    length = lengths[0]
    for unit in range(units):
        length = jnp.where(home[unit] == ids[0], lengths[unit // heads], length)
    return length


def start_cache(length, pages, pool, raw, sems):
    last = pages.shape[0] - 1

    def page_copy(index):
        page = pages[jnp.minimum(index, last)]
        return pltpu.make_async_copy(
            pool.at[page], raw.at[pl.ds(pl.multiple_of(index * PAGE, PAGE), PAGE), :], sems.at[index]
        )

    @pl.loop(0, pl.cdiv(length, CHUNK) * (CHUNK // PAGE))
    def _(index):
        page_copy(index).start()

    return page_copy


def turn_cache(length, page_copy, raw, flipped, values):
    per_chunk = CHUNK // PAGE

    @pl.loop(0, pl.cdiv(length, CHUNK))
    def _(c):
        for k in range(per_chunk):
            page_copy(c * per_chunk + k).wait()
        keys, mixed = doubled(raw[pl.ds(pl.multiple_of(c * CHUNK, CHUNK), CHUNK), :])
        flipped[c] = keys
        values[c] = mixed

        @pl.when(length - c * CHUNK < CHUNK)
        def _():
            valid = length - c * CHUNK
            columns = lax.broadcasted_iota(jnp.int32, keys.shape, 1) < valid
            flipped[c] = jnp.where(columns, keys, jnp.broadcast_to(keys[:, 0:1], keys.shape))
            inside = lax.broadcasted_iota(jnp.int32, mixed.shape, 0) < valid
            values[c] = jnp.where(inside, mixed, jnp.zeros_like(mixed))


def doubled(both):
    turned = both.T
    keys = jnp.concatenate([turned[:HD], turned[:HD]], axis=0)
    side = lax.broadcasted_iota(jnp.int32, both.shape, 1)
    return keys, jnp.where(side < HD, jnp.ones_like(both), both)


def prefill_kernel(
    positions, lengths, home, ids, msg, flipped_in, values_in, decoded_in, out,
    old_flipped, old_values, decoded, flipped, values, queries, scores, top, total, sems,
):
    blocks = msg.shape[0]
    stretch = blocks * positions
    half = positions // 2
    used = pl.cdiv(own_length(lengths, home, ids), CHUNK)
    steps = stretch // CHUNK
    loads = [
        pltpu.make_async_copy(flipped_in, old_flipped, sems.at[0]),
        pltpu.make_async_copy(values_in, old_values, sems.at[1]),
        pltpu.make_async_copy(decoded_in, decoded, sems.at[2]),
    ]
    for load in loads:
        load.start()

    @pl.loop(0, blocks)
    def _(b):
        packed = msg[b, pl.ds(positions, half), :].astype(F32) * (SCALE * LOG2E)
        high = packed.astype(BF16)
        low = (packed - high.astype(F32)).astype(BF16)
        row = pl.multiple_of(b * positions, positions)
        for part in range(2):
            lanes = slice(part * HD, (part + 1) * HD)
            queries[pl.ds(row + part * half, half), :] = jnp.concatenate([high[:, lanes], low[:, lanes]], axis=1)

    for c in range(steps):
        for k in range(CHUNK // positions):
            keys, mixed = doubled(msg[c * (CHUNK // positions) + k, 0:positions, :])
            flipped[c, :, k * positions : (k + 1) * positions] = keys
            values[c, k * positions : (k + 1) * positions, :] = mixed
    def raise_top(s):
        best = top[...]
        for k in range(CHUNK // 128):
            best = jnp.maximum(best, s[:, k * 128 : (k + 1) * 128])
        top[...] = best

    def score(i, spot, keys, diagonal=False):
        q = queries[pl.ds(pl.multiple_of(i * CHUNK, CHUNK), CHUNK), :]
        s = jnp.dot(q, keys, preferred_element_type=F32)
        if diagonal:
            rows = lax.broadcasted_iota(jnp.int32, (CHUNK, CHUNK), 0)
            cols = lax.broadcasted_iota(jnp.int32, (CHUNK, CHUNK), 1)
            s = jnp.where(cols <= rows, s, MASKED)
        scores[spot] = s
        raise_top(s)

    def settle():
        best = jnp.max(top[...], axis=1, keepdims=True)
        total[1] = jnp.broadcast_to(best, (CHUNK, 128))
        top[...] = jnp.full_like(top, -jnp.inf)
        total[0] = jnp.zeros((CHUNK, 128), F32)

    def mix(spot, rows):
        best = total[1]
        s = scores[spot]
        weights = jnp.concatenate(
            [jnp.exp2(s[:, k * 128 : (k + 1) * 128] - best).astype(BF16) for k in range(CHUNK // 128)], axis=1
        )
        total[0] += jnp.dot(weights, rows, preferred_element_type=F32)

    def emit(i):
        done = total[0]
        mixed = (done[:, HD:] / done[:, :HD]).astype(BF16)
        for k in range(CHUNK // positions):
            part = mixed[k * positions : (k + 1) * positions]
            out[i * (CHUNK // positions) + k, 0:half, :] = jnp.concatenate([part[:half], part[half:]], axis=1)

    top[...] = jnp.full_like(top, -jnp.inf)
    for load in loads:
        load.wait()
    slots, features = decoded.shape
    for k in range(0, features // 128, 2):
        pair = jnp.concatenate([decoded[:, k * 128 : (k + 1) * 128], decoded[:, (k + 1) * 128 : (k + 2) * 128]], axis=0)
        pair = pair.astype(BF16)
        for b in range(blocks):
            out[b, half + k * slots : half + (k + 2) * slots, :] = pair

    @pl.loop(0, used)
    def _(c):
        score(0, c, old_flipped[c])

    score(0, used, flipped[0], diagonal=True)
    settle()

    @pl.loop(1, steps)
    def _(i):
        @pl.loop(0, used)
        def _(c):
            mix(c, old_values[c])
            score(i, c, old_flipped[c])

        @pl.loop(0, i)
        def _(c):
            mix(used + c, values[c])
            score(i, used + c, flipped[c])

        emit(i - 1)
        score(i, used + i, flipped[i], diagonal=True)
        settle()

    @pl.loop(0, used)
    def _(c):
        mix(c, old_values[c])

    @pl.loop(0, steps)
    def _(c):
        mix(used + c, values[c])

    emit(steps - 1)


def prefill_attention(lengths, home, ids, msg, old_flipped, old_values, decoded):
    blocks, rows, _ = msg.shape
    positions = rows * 2 // 3
    stretch = blocks * positions
    steps = stretch // CHUNK
    chunks = old_values.shape[0] + steps
    slots, features = decoded.shape
    keys = chunks * CHUNK
    return pl.pallas_call(
        functools.partial(prefill_kernel, positions),
        out_shape=jax.ShapeDtypeStruct((blocks, positions // 2 + slots * features // 128, 2 * HD), BF16),
        in_specs=[SMEM, SMEM, SMEM, VMEM, ANY, ANY, ANY],
        out_specs=VMEM,
        scratch_shapes=[
            pltpu.VMEM(old_flipped.shape, BF16),
            pltpu.VMEM(old_values.shape, BF16),
            pltpu.VMEM(decoded.shape, F32),
            pltpu.VMEM((steps, 2 * HD, CHUNK), BF16),
            pltpu.VMEM((steps, CHUNK, 2 * HD), BF16),
            pltpu.VMEM((stretch, 2 * HD), BF16),
            pltpu.VMEM((chunks, CHUNK, CHUNK), F32),
            pltpu.VMEM((CHUNK, 128), F32),
            pltpu.VMEM((2, CHUNK, 128), F32),
            pltpu.SemaphoreType.DMA((3,)),
        ],
        compiler_params=pltpu.CompilerParams(vmem_limit_bytes=48 * 2**20),
        cost_estimate=pl.CostEstimate(flops=4 * stretch * keys * HD, bytes_accessed=4 * 2**20, transcendentals=stretch * keys),
    )(lengths, home, ids, msg, old_flipped, old_values, decoded)


def decode_kernel(
    heads, lengths, home, ids, pages, old_lengths, old_home, old_pages, x, gain, w, pool, old_pool,
    out, flipped, values_in, raw, old_sems, buf, wbuf, normed, qrows, cacherows, rowout, bests, totals, mixes, owners, anchors, wsems, sems,
):
    slots = pages.shape[0]
    width = heads * 2 * HD
    per_group = BLOCK // PAGE
    depth = pages.shape[1]
    most = buf.shape[0] // BLOCK
    old_length = own_length(old_lengths, old_home, ids)
    old_copy = start_cache(old_length, old_pages, old_pool, raw, old_sems)
    w_copies = [pltpu.make_async_copy(w.at[j], wbuf.at[j], wsems.at[j]) for j in range(3)]
    for copy in w_copies:
        copy.start()

    def page_copy(item, k):
        page = pages[owners[0, item], jnp.minimum(owners[2, item] * per_group + k, depth - 1)]
        place = item * per_group + k
        return pltpu.make_async_copy(
            pool.at[page], buf.at[pl.ds(pl.multiple_of(place * PAGE, PAGE), PAGE), :], sems.at[place]
        )

    def groups(s):
        return pl.cdiv(lengths[s], BLOCK)

    @pl.loop(0, home.shape[0])
    def _(request):
        s = home[request] - ids[0] * slots
        anchors[jnp.where((s >= 0) & (s < slots), s, slots)] = request

    @pl.loop(0, most + UNROLL)
    def _(item):
        owners[0, item] = 0
        owners[1, item] = 0
        owners[2, item] = 0

    def begin(s, start):
        @pl.loop(0, groups(s))
        def _(g):
            owners[0, start + g] = s
            owners[1, start + g] = lengths[s] - g * BLOCK
            owners[2, start + g] = g

        return start + groups(s)

    items = lax.fori_loop(0, slots, begin, 0)

    def fetch(item):
        @pl.when(item < items)
        def _():
            for k in range(per_group):
                page_copy(item, k).start()

    for item in range(AHEAD):
        fetch(item)
    turn_cache(old_length, old_copy, raw, flipped, values_in)
    values = x[...].astype(F32)
    inverse = lax.rsqrt(jnp.mean(values * values, axis=-1, keepdims=True) + EPSILON)
    normed[...] = (values * inverse * gain[...]).astype(BF16)
    rows = values.shape[0]
    zero = jnp.zeros((rows, HD), F32)
    parts = []
    for j in range(3):
        w_copies[j].wait()
        parts.append(jnp.dot(normed[...], wbuf[j], preferred_element_type=F32).astype(BF16).astype(F32))
    for g in range(heads):
        cut = slice(g * HD, (g + 1) * HD)
        span = slice(g * 2 * HD, (g + 1) * 2 * HD)
        qrows[:, span] = jnp.concatenate([parts[0][:, cut] * SCALE, zero], axis=1)
        cacherows[:, span] = jnp.concatenate([parts[1][:, cut], parts[2][:, cut]], axis=1)
    owner = lax.broadcasted_iota(jnp.int32, (8, width), 1) // (2 * HD)
    diagonal = owner == lax.broadcasted_iota(jnp.int32, (8, width), 0)

    def spread(s):
        row = anchors[s]
        return jnp.where(diagonal, jnp.broadcast_to(qrows[pl.ds(row, 1), :], (8, width)), 0.0)

    @pl.loop(0, pl.cdiv(items, UNROLL))
    def _(turn):
        for u in range(UNROLL):
            @pl.when(turn * UNROLL + u < items)
            def _():
                for k in range(per_group):
                    page_copy(turn * UNROLL + u, k).wait()

            fetch(turn * UNROLL + u + AHEAD)
        for u in range(UNROLL):
            item = turn * UNROLL + u
            place = jnp.minimum(item, most - 1)
            cache = buf[pl.ds(pl.multiple_of(place * BLOCK, BLOCK), BLOCK), :]
            query = spread(owners[0, item]).astype(BF16)
            s = contract_last(query, cache)
            s = jnp.where(lax.broadcasted_iota(jnp.int32, (8, BLOCK), 1) < owners[1, item], s, MASKED)
            best = jnp.max(s, axis=1, keepdims=True)
            weights = jnp.exp(s - best)
            bests[item] = jnp.broadcast_to(best, (8, 128))
            totals[item] = jnp.broadcast_to(jnp.sum(weights, axis=1, keepdims=True), (8, 128))
            mixes[item] = jnp.dot(weights.astype(BF16), cache, preferred_element_type=F32)

    most_items = pl.cdiv(depth * PAGE, BLOCK)
    start = 0
    for s in range(slots):
        own = jnp.broadcast_to(cacherows[pl.ds(anchors[s], 1), :], (8, width))
        own_score = jnp.sum(spread(s) * own, axis=1, keepdims=True)
        count = groups(s)
        held = [jnp.where(i < count, bests[start + i], -jnp.inf) for i in range(most_items)]
        best = functools.reduce(jnp.maximum, held, jnp.broadcast_to(own_score, (8, 128)))
        own_weight = jnp.exp(own_score - best[:, 0:1])
        total = own_weight
        mixed = own_weight.astype(BF16).astype(F32) * own
        for i in range(most_items):
            share = jnp.exp(held[i] - best)[:, 0:1]
            total = total + jnp.where(i < count, totals[start + i][:, 0:1], 0.0) * share
            mixed = mixed + jnp.where(i < count, mixes[start + i], 0.0) * share
        mixed = jnp.where(diagonal, mixed / total, 0.0)
        rowout[s : s + 1, :] = jnp.sum(mixed, axis=0, keepdims=True)
        start = start + count
    done = rowout[...]
    for g in range(0, heads, 2):
        out[:, g * HD : (g + 2) * HD] = jnp.concatenate(
            [done[:, g * 2 * HD + HD : (g + 1) * 2 * HD], done[:, (g + 1) * 2 * HD + HD : (g + 2) * 2 * HD]], axis=1
        )


def decode_attention(lengths, home, ids, pages, old_lengths, old_home, old_pages, x, gain, w, pool, old_pool):
    slots = pages.shape[0]
    features = w.shape[2]
    heads = features // HD
    width = heads * 2 * HD
    rows = x.shape[0]
    per_group = BLOCK // PAGE
    most = pl.cdiv(pool.shape[0] + slots * (per_group - 1), per_group)
    chunks = pl.cdiv(old_pool.shape[0] * PAGE, CHUNK)
    flipped, values = (chunks, 2 * HD, CHUNK), (chunks, CHUNK, 2 * HD)
    spare = max(UNROLL, pl.cdiv(pages.shape[1], per_group))
    return pl.pallas_call(
        functools.partial(decode_kernel, heads),
        out_shape=[
            jax.ShapeDtypeStruct((slots, features), F32),
            jax.ShapeDtypeStruct(flipped, BF16),
            jax.ShapeDtypeStruct(values, BF16),
        ],
        in_specs=[SMEM] * 7 + [VMEM, VMEM, ANY, ANY, ANY],
        out_specs=[VMEM, VMEM, VMEM],
        scratch_shapes=[
            pltpu.VMEM((chunks * CHUNK, 2 * HD), BF16),
            pltpu.SemaphoreType.DMA((chunks * (CHUNK // PAGE),)),
            pltpu.VMEM((most * BLOCK, width), BF16),
            pltpu.VMEM(w.shape, BF16),
            pltpu.VMEM(x.shape, BF16),
            pltpu.VMEM((rows, width), F32),
            pltpu.VMEM((rows, width), F32),
            pltpu.VMEM((slots, width), F32),
            pltpu.VMEM((most + spare, 8, 128), F32),
            pltpu.VMEM((most + spare, 8, 128), F32),
            pltpu.VMEM((most + spare, 8, width), F32),
            pltpu.SMEM((3, most + UNROLL), jnp.int32),
            pltpu.SMEM((slots + 1,), jnp.int32),
            pltpu.SemaphoreType.DMA((3,)),
            pltpu.SemaphoreType.DMA((most * per_group,)),
        ],
        compiler_params=pltpu.CompilerParams(vmem_limit_bytes=52 * 2**20),
        cost_estimate=pl.CostEstimate(flops=2 * 10**9, bytes_accessed=22 * 2**20, transcendentals=10**6),
    )(lengths, home, ids, pages, old_lengths, old_home, old_pages, x, gain, w, pool, old_pool)


def qkv_kernel(requests, heads, home, gain, x, w, out, xbuf, wbuf, normed, sems):
    rows = x.shape[0]
    positions = rows // requests
    half = positions // 2
    x_copy = pltpu.make_async_copy(x, xbuf, sems.at[3])
    x_copy.start()
    w_copies = [pltpu.make_async_copy(w.at[j], wbuf.at[j], sems.at[j]) for j in range(3)]
    for copy in w_copies:
        copy.start()
    x_copy.wait()
    values = xbuf[...].astype(F32)
    inverse = lax.rsqrt(jnp.mean(values * values, axis=-1, keepdims=True) + EPSILON)
    normed[...] = (values * inverse * gain[...]).astype(BF16)

    def project(j):
        w_copies[j].wait()
        return jnp.dot(normed[...], wbuf[j], preferred_element_type=F32).astype(BF16)

    y = project(0)
    for r in range(requests):
        for g in range(heads):
            part = y[r * positions : (r + 1) * positions, g * HD : (g + 1) * HD]
            out[home[r * heads + g], positions : positions + half, :] = jnp.concatenate([part[:half], part[half:]], axis=1)
    keys = project(1)
    y = project(2)
    for r in range(requests):
        span = slice(r * positions, (r + 1) * positions)
        for g in range(heads):
            cut = slice(g * HD, (g + 1) * HD)
            out[home[r * heads + g], 0:positions, :] = jnp.concatenate([keys[span, cut], y[span, cut]], axis=1)


def qkv_messages(home, x, gain, w, requests):
    rows, width = x.shape
    features = w.shape[2]
    heads = features // HD
    units = requests * heads
    positions = rows // requests
    return pl.pallas_call(
        functools.partial(qkv_kernel, requests, heads),
        out_shape=jax.ShapeDtypeStruct((units, positions * 3 // 2, 2 * HD), BF16),
        in_specs=[SMEM, VMEM, ANY, ANY],
        out_specs=VMEM,
        scratch_shapes=[
            pltpu.VMEM((rows, width), BF16),
            pltpu.VMEM(w.shape, BF16),
            pltpu.VMEM((rows, width), BF16),
            pltpu.SemaphoreType.DMA((4,)),
        ],
        compiler_params=pltpu.CompilerParams(vmem_limit_bytes=58 * 2**20),
        cost_estimate=pl.CostEstimate(flops=2 * rows * width * 3 * features, bytes_accessed=10 * 2**20, transcendentals=0),
    )(home, gain, x, w)


def project_kernel(requests, heads, home, slots_of, ids, received, w_out, *rest):
    outs, (rows_in, decode_in, weights, products, sem) = rest[:-5], rest[-5:]
    fetch = pltpu.make_async_copy(w_out, weights, sem)
    fetch.start()
    n_head = len(outs)
    n_tok = received.shape[0]
    per = outs[0].shape[0]
    features = w_out.shape[0]
    slots = decode_in.shape[0] // n_tok
    half = received.shape[1] - slots * features // 128
    positions = 2 * half
    block_rows = positions // n_head
    share = per - requests * block_rows
    hosted = share * n_head
    for b in range(n_tok):
        for k in range(0, features // 128, 2):
            pair = received[b, half + k * slots : half + (k + 2) * slots, :].astype(F32)
            for j in range(2):
                decode_in[b * slots : (b + 1) * slots, (k + j) * 128 : (k + j + 1) * 128] = pair[
                    j * slots : (j + 1) * slots
                ]
    rows_in[...] = jnp.zeros_like(rows_in)
    for r in range(requests):
        for g in range(0, heads, 2):
            left = received[home[r * heads + g], 0:half, :].astype(F32)
            right = received[home[r * heads + g + 1], 0:half, :].astype(F32)
            both = jnp.concatenate(
                [
                    jnp.concatenate([left[:, :HD], right[:, :HD]], axis=1),
                    jnp.concatenate([left[:, HD:], right[:, HD:]], axis=1),
                ],
                axis=0,
            )
            for h in range(n_head):
                rows_in[h, r * block_rows : (r + 1) * block_rows, g * HD : (g + 2) * HD] = both[
                    h * block_rows : (h + 1) * block_rows
                ]
    for j in range(hosted):
        rows_in[j // share, requests * block_rows + j % share, :] = decode_in[pl.ds(slots_of[ids[0] * hosted + j], 1), :][0]
    fetch.wait()
    padded = rows_in.shape[1]
    everyone = rows_in[...].reshape(n_head * padded, features).astype(BF16)
    products[...] = jnp.dot(everyone, weights[...], preferred_element_type=F32).astype(BF16).reshape(products.shape)
    for k in range(n_head):
        outs[k][...] = products[ids[1] ^ k, 0:per, :]


def project_out(home, slots_of, ids, received, w_out, requests, heads, n_head, hosted):
    features, width = w_out.shape
    positions = 2 * (received.shape[1] - hosted * features // 128)
    per = requests * (positions // n_head) + hosted // n_head
    padded = -(-per // 16) * 16
    return pl.pallas_call(
        functools.partial(project_kernel, requests, heads),
        out_shape=[jax.ShapeDtypeStruct((per, width), BF16)] * n_head,
        in_specs=[SMEM, SMEM, SMEM, VMEM, ANY],
        out_specs=[VMEM] * n_head,
        scratch_shapes=[
            pltpu.VMEM((n_head, padded, features), F32),
            pltpu.VMEM((received.shape[0] * hosted, features), F32),
            pltpu.VMEM(w_out.shape, BF16),
            pltpu.VMEM((n_head, padded, width), BF16),
            pltpu.SemaphoreType.DMA,
        ],
        compiler_params=pltpu.CompilerParams(vmem_limit_bytes=24 * 2**20),
        cost_estimate=pl.CostEstimate(flops=2 * n_head * per * features * width, bytes_accessed=4 * 2**20, transcendentals=0),
    )(home, slots_of, ids, received, w_out)


def middle_kernel(own_pre, own_dec, gain, *rest):
    terms, (resid, normed_left, normed_right) = rest[:-3], rest[-3:]
    middle = normed_left.shape[1]
    split = own_pre.shape[0]
    for rows, own in ((slice(0, split), own_pre), (slice(split, resid.shape[0]), own_dec)):
        values = own[...].astype(F32)
        for term in terms:
            values = values + term[rows, :].astype(F32)
        resid[rows, :] = values
        inverse = lax.rsqrt(jnp.mean(values * values, axis=-1, keepdims=True) + EPSILON)
        normed = (values * inverse * gain[...]).astype(BF16)
        normed_left[rows, :] = normed[:, :middle]
        normed_right[rows, :] = normed[:, middle:]


def middle(own_pre, own_dec, gain, terms):
    shape = terms[0].shape
    return pl.pallas_call(
        middle_kernel,
        out_shape=[jax.ShapeDtypeStruct(shape, F32)] + [jax.ShapeDtypeStruct((shape[0], shape[1] // 2), BF16)] * 2,
        in_specs=[VMEM] * (3 + len(terms)),
        out_specs=[VMEM] * 3,
        compiler_params=pltpu.CompilerParams(vmem_limit_bytes=16 * 2**20),
        cost_estimate=pl.CostEstimate(flops=10**6, bytes_accessed=2 * 2**20, transcendentals=0),
    )(own_pre, own_dec, gain, *terms)


def finish_kernel(resid, own_left, own_right, *rest):
    sums, outs = rest[:-2], rest[-2:]
    middle = own_left.shape[1]
    first = 0
    for out in outs:
        rows = slice(first, first + out.shape[0])
        first += out.shape[0]
        for side, own in enumerate((own_left, own_right)):
            cols = slice(side * middle, (side + 1) * middle)
            added = own[rows, :].astype(F32)
            for term in sums[2 * side : 2 * side + 2]:
                added = added + term[rows, :].astype(F32)
            out[:, cols] = (resid[rows, cols] + added).astype(BF16)


def finish(resid, own, sums, split):
    per, width = resid.shape
    return pl.pallas_call(
        finish_kernel,
        out_shape=[jax.ShapeDtypeStruct((split, width), BF16), jax.ShapeDtypeStruct((per - split, width), BF16)],
        in_specs=[VMEM] * 7,
        out_specs=[VMEM] * 2,
        compiler_params=pltpu.CompilerParams(vmem_limit_bytes=16 * 2**20),
        cost_estimate=pl.CostEstimate(flops=10**6, bytes_accessed=2 * 2**20, transcendentals=0),
    )(resid, *own, *sums)


def feed_kernel(shape, *refs):
    count, pieces = len(shape), sum(shape)
    parts, (gate_up, down), outs = list(refs[:pieces]), refs[pieces : pieces + 2], refs[pieces + 2 :]
    outs, rows = outs[:-1], outs[-1]
    per = outs[0].shape[0]
    padded = rows.shape[0] // count
    for index, size in enumerate(shape):
        first = 0
        for _ in range(size):
            part = parts.pop(0)
            rows[index * padded : index * padded + per, first : first + part.shape[1]] = part[...]
            first += part.shape[1]
    middle = down.shape[1] // 2
    hidden_units = down.shape[0]
    tile = 128 if hidden_units % 128 == 0 else hidden_units
    steps = hidden_units // tile

    hidden = []
    for step in range(steps):
        cols = slice(step * tile, (step + 1) * tile)
        if tile == 128:
            both = jnp.concatenate([gate_up[0, :, cols], gate_up[1, :, cols]], axis=1)
            y = jnp.dot(rows[...], both, preferred_element_type=F32)
            gate, upper = y[:, :tile], y[:, tile:]
        else:
            gate = jnp.dot(rows[...], gate_up[0], preferred_element_type=F32)
            upper = jnp.dot(rows[...], gate_up[1], preferred_element_type=F32)
        hidden.append((jax.nn.gelu(gate, approximate=True) * upper).astype(BF16))
    full = jnp.concatenate(hidden, axis=1)
    for side in range(2):
        cols = slice(side * middle, (side + 1) * middle)
        y = jnp.dot(full, down[:, cols], preferred_element_type=F32).astype(BF16)
        for index in range(count):
            outs[2 * index + side][...] = y[index * padded : index * padded + per]


def feed_forward(chunks, gate_up, down):
    count = len(chunks)
    pieces = [piece for chunk in chunks for piece in chunk]
    per, width = pieces[0].shape[0], down.shape[1]
    hidden_units = down.shape[0]
    return pl.pallas_call(
        functools.partial(feed_kernel, [len(chunk) for chunk in chunks]),
        out_shape=[jax.ShapeDtypeStruct((per, width // 2), BF16)] * (2 * count),
        in_specs=[VMEM] * (len(pieces) + 2),
        out_specs=[VMEM] * (2 * count),
        scratch_shapes=[pltpu.VMEM((count * (-(-per // 16) * 16), width), BF16)],
        compiler_params=pltpu.CompilerParams(vmem_limit_bytes=24 * 2**20),
        cost_estimate=pl.CostEstimate(
            flops=6 * count * per * width * hidden_units, bytes_accessed=8 * 2**20, transcendentals=count * per * hidden_units
        ),
    )(*pieces, gate_up, down)


def ring_of(n_tok):
    if n_tok == 8:
        return [0, 2, 4, 6, 7, 5, 3, 1]
    return list(range(n_tok))


def shards(
    prefill_states,
    decode_states,
    attn_gain,
    w_qkv,
    w_out,
    ffn_gain,
    w_gate_up,
    w_down,
    prefill_pool,
    prefill_pages,
    prefill_lengths,
    prefill_home,
    decode_pool,
    decode_pages,
    decode_lengths,
    decode_home,
):
    n_tok = lax.axis_size("tok")
    n_head = lax.axis_size("head")
    my_tok = lax.axis_index("tok")
    my_head = lax.axis_index("head")
    requests, positions, width = prefill_states.shape
    hosted = decode_states.shape[0]
    features = w_qkv.shape[2]
    heads = features // HD
    units = requests * heads
    ring = ring_of(n_tok)
    ahead = [(ring[i], ring[(i + 1) % n_tok]) for i in range(n_tok)]
    behind = [(b, a) for a, b in ahead]
    far = n_tok // 2
    near = (n_tok - 1) // 2

    def joined(part, other):
        return (part.astype(F32) + other.astype(F32)).astype(BF16)

    gain = attn_gain.reshape(1, width)
    w_three = jnp.transpose(w_qkv, (1, 0, 2))
    ids = jnp.stack([my_tok, my_head]).astype(jnp.int32)
    copies = jnp.broadcast_to(decode_states[None], (n_tok, hosted, width))
    rows = lax.all_to_all(copies, "tok", split_axis=0, concat_axis=0, tiled=True).reshape(n_tok * hosted, width)
    messages = qkv_messages(prefill_home, prefill_states.reshape(requests * positions, width), gain, w_three, requests)
    messages, rows = lax.optimization_barrier((messages, rows))
    arrived = lax.all_to_all(messages, "tok", split_axis=0, concat_axis=0, tiled=True)
    decoded, old_keys, old_values = decode_attention(
        decode_lengths, decode_home, ids, decode_pages, prefill_lengths, prefill_home, prefill_pages.reshape(-1),
        rows, gain, w_three, decode_pool, prefill_pool,
    )
    attn = prefill_attention(prefill_lengths, prefill_home, ids, arrived, old_keys, old_values, decoded)
    returned = lax.all_to_all(attn, "tok", split_axis=0, concat_axis=0, tiled=True)
    gate_up = jnp.transpose(w_gate_up, (1, 0, 2))

    parts = project_out(prefill_home, decode_home, ids, returned, w_out, requests, heads, n_head, hosted)
    block_rows = positions // n_head
    share = hosted // n_head
    own_pre = lax.dynamic_slice_in_dim(prefill_states, my_head * block_rows, block_rows, 1)
    own_dec = lax.dynamic_slice_in_dim(decode_states, my_head * share, share, 0)
    terms = [parts[0]]
    swap = [(i, i ^ 1) for i in range(n_head)]
    for k in range(2, n_head, 2):
        both = joined(parts[k], lax.ppermute(parts[k + 1], "head", swap))
        terms.append(lax.ppermute(both, "head", [(i, i ^ k) for i in range(n_head)]))
    terms.append(lax.ppermute(parts[1], "head", swap))
    terms[1], gate_up = lax.optimization_barrier((terms[1], gate_up))
    resid, left, right = middle(own_pre.reshape(requests * block_rows, width), own_dec, ffn_gain.reshape(1, width), terms)

    plus, minus = {}, {}
    up_left, up_right, down_left, down_right = left, right, left, right
    waiting = None
    for k in range(1, far + 1):
        up_left = lax.ppermute(up_left, "tok", ahead)
        down_right = lax.ppermute(down_right, "tok", behind)
        if k <= near:
            down_left = lax.ppermute(down_left, "tok", behind)
            up_right = lax.ppermute(up_right, "tok", ahead)
        if waiting is not None:
            done = feed_forward(waiting, gate_up, w_down)
            up_left, down_right, done = lax.optimization_barrier((up_left, down_right, done))
            minus[k - 1], plus[k - 1] = done[:2], done[2:]
        waiting = [(up_left, up_right), (down_left, down_right)]
    farthest = feed_forward([(up_left, down_right)], gate_up, w_down)
    left, right, farthest = lax.optimization_barrier((left, right, farthest))
    own_part = feed_forward([(left, right)], gate_up, w_down)

    def chain(part, table, side, hops, steps):
        for k in range(hops, 0, -1):
            part = joined(table[k][side], lax.ppermute(part, "tok", steps))
        return lax.ppermute(part, "tok", steps)

    sums = [
        chain(minus[near][0], minus, 0, near - 1, behind),
        chain(farthest[0], plus, 0, far - 1, ahead),
        chain(plus[near][1], plus, 1, near - 1, ahead),
        chain(farthest[1], minus, 1, far - 1, behind),
    ]
    pre, dec = finish(resid, own_part, sums, requests * block_rows)
    return (pre.reshape(requests, block_rows, width), dec)


def solution(mesh):
    placed = (
        P(None, "tok", None),
        P("tok", None),
        P(),
        P(None, None, "head"),
        P("head", None),
        P(),
        P(None, None, "tok"),
        P("tok", None),
        P("tok", None, "head"),
        P("tok", None),
        P(),
        P(),
        P("tok", None, "head"),
        P("tok", None),
        P("tok"),
        P(),
    )
    return jax.shard_map(
        shards,
        mesh=mesh,
        in_specs=placed,
        out_specs=(P(None, ("tok", "head"), None), P(("tok", "head"), None)),
        check_vma=False,
    )
```

```python
import functools
import jax
import jax.numpy as jnp
from jax import lax
from jax.experimental import pallas as pl
from jax.experimental.pallas import tpu as pltpu
from jax.sharding import PartitionSpec as P

HD = 64
PAGE = 128
EPSILON = 1e-06
SCALE = 0.125
MASKED = -1e30
LOG2E = 1.4426950408889634
BLOCK = 512
CHUNK = 1024
UNROLL = 2
AHEAD = 6
F32 = jnp.float32
BF16 = jnp.bfloat16
VMEM = pl.BlockSpec(memory_space=pltpu.VMEM)
SMEM = pl.BlockSpec(memory_space=pltpu.SMEM)
ANY = pl.BlockSpec(memory_space=pl.ANY)


def contract_last(left, right):
    return lax.dot_general(left, right, (((1,), (1,)), ((), ())), preferred_element_type=F32)


def own_length(lengths, home, ids):
    units = home.shape[0]
    heads = units // lengths.shape[0]
    length = lengths[0]
    for unit in range(units):
        length = jnp.where(home[unit] == ids[0], lengths[unit // heads], length)
    return length


def start_cache(length, pages, pool, raw, sems):
    last = pages.shape[0] - 1

    def page_copy(index):
        page = pages[jnp.minimum(index, last)]
        return pltpu.make_async_copy(
            pool.at[page], raw.at[pl.ds(pl.multiple_of(index * PAGE, PAGE), PAGE), :], sems.at[index]
        )

    @pl.loop(0, pl.cdiv(length, CHUNK) * (CHUNK // PAGE))
    def _(index):
        page_copy(index).start()

    return page_copy


def turn_cache(length, page_copy, raw, flipped, values):
    per_chunk = CHUNK // PAGE

    @pl.loop(0, pl.cdiv(length, CHUNK))
    def _(c):
        for k in range(per_chunk):
            page_copy(c * per_chunk + k).wait()
        keys, mixed = doubled(raw[pl.ds(pl.multiple_of(c * CHUNK, CHUNK), CHUNK), :])
        flipped[c] = keys
        values[c] = mixed

        @pl.when(length - c * CHUNK < CHUNK)
        def _():
            valid = length - c * CHUNK
            columns = lax.broadcasted_iota(jnp.int32, keys.shape, 1) < valid
            flipped[c] = jnp.where(columns, keys, jnp.broadcast_to(keys[:, 0:1], keys.shape))
            inside = lax.broadcasted_iota(jnp.int32, mixed.shape, 0) < valid
            values[c] = jnp.where(inside, mixed, jnp.zeros_like(mixed))


def doubled(both):
    turned = both.T
    keys = jnp.concatenate([turned[:HD], turned[:HD]], axis=0)
    side = lax.broadcasted_iota(jnp.int32, both.shape, 1)
    return keys, jnp.where(side < HD, jnp.ones_like(both), both)


def prefill_kernel(
    positions, lengths, home, ids, msg, flipped_in, values_in, decoded_in, out,
    old_flipped, old_values, decoded, flipped, values, queries, scores, top, total, sems,
):
    blocks = msg.shape[0]
    stretch = blocks * positions
    half = positions // 2
    used = pl.cdiv(own_length(lengths, home, ids), CHUNK)
    steps = stretch // CHUNK
    loads = [
        pltpu.make_async_copy(flipped_in, old_flipped, sems.at[0]),
        pltpu.make_async_copy(values_in, old_values, sems.at[1]),
        pltpu.make_async_copy(decoded_in, decoded, sems.at[2]),
    ]
    for load in loads:
        load.start()

    @pl.loop(0, blocks)
    def _(b):
        packed = msg[b, pl.ds(positions, half), :].astype(F32) * (SCALE * LOG2E)
        high = packed.astype(BF16)
        low = (packed - high.astype(F32)).astype(BF16)
        row = pl.multiple_of(b * positions, positions)
        for part in range(2):
            lanes = slice(part * HD, (part + 1) * HD)
            queries[pl.ds(row + part * half, half), :] = jnp.concatenate([high[:, lanes], low[:, lanes]], axis=1)

    for c in range(steps):
        for k in range(CHUNK // positions):
            keys, mixed = doubled(msg[c * (CHUNK // positions) + k, 0:positions, :])
            flipped[c, :, k * positions : (k + 1) * positions] = keys
            values[c, k * positions : (k + 1) * positions, :] = mixed
    def raise_top(s):
        best = top[...]
        for k in range(CHUNK // 128):
            best = jnp.maximum(best, s[:, k * 128 : (k + 1) * 128])
        top[...] = best

    def score(i, spot, keys, diagonal=False):
        q = queries[pl.ds(pl.multiple_of(i * CHUNK, CHUNK), CHUNK), :]
        s = jnp.dot(q, keys, preferred_element_type=F32)
        if diagonal:
            rows = lax.broadcasted_iota(jnp.int32, (CHUNK, CHUNK), 0)
            cols = lax.broadcasted_iota(jnp.int32, (CHUNK, CHUNK), 1)
            s = jnp.where(cols <= rows, s, MASKED)
        scores[spot] = s
        raise_top(s)

    def settle():
        best = jnp.max(top[...], axis=1, keepdims=True)
        total[1] = jnp.broadcast_to(best, (CHUNK, 128))
        top[...] = jnp.full_like(top, -jnp.inf)
        total[0] = jnp.zeros((CHUNK, 128), F32)

    def mix(spot, rows):
        best = total[1]
        s = scores[spot]
        weights = jnp.concatenate(
            [jnp.exp2(s[:, k * 128 : (k + 1) * 128] - best).astype(BF16) for k in range(CHUNK // 128)], axis=1
        )
        total[0] += jnp.dot(weights, rows, preferred_element_type=F32)

    def emit(i):
        done = total[0]
        mixed = (done[:, HD:] / done[:, :HD]).astype(BF16)
        for k in range(CHUNK // positions):
            part = mixed[k * positions : (k + 1) * positions]
            out[i * (CHUNK // positions) + k, 0:half, :] = jnp.concatenate([part[:half], part[half:]], axis=1)

    top[...] = jnp.full_like(top, -jnp.inf)
    for load in loads:
        load.wait()
    slots, features = decoded.shape
    for k in range(0, features // 128, 2):
        pair = jnp.concatenate([decoded[:, k * 128 : (k + 1) * 128], decoded[:, (k + 1) * 128 : (k + 2) * 128]], axis=0)
        pair = pair.astype(BF16)
        for b in range(blocks):
            out[b, half + k * slots : half + (k + 2) * slots, :] = pair

    @pl.loop(0, used)
    def _(c):
        score(0, c, old_flipped[c])

    score(0, used, flipped[0], diagonal=True)
    settle()

    @pl.loop(1, steps)
    def _(i):
        @pl.loop(0, used)
        def _(c):
            mix(c, old_values[c])
            score(i, c, old_flipped[c])

        @pl.loop(0, i)
        def _(c):
            mix(used + c, values[c])
            score(i, used + c, flipped[c])

        emit(i - 1)
        score(i, used + i, flipped[i], diagonal=True)
        settle()

    @pl.loop(0, used)
    def _(c):
        mix(c, old_values[c])

    @pl.loop(0, steps)
    def _(c):
        mix(used + c, values[c])

    emit(steps - 1)


def prefill_attention(lengths, home, ids, msg, old_flipped, old_values, decoded):
    blocks, rows, _ = msg.shape
    positions = rows * 2 // 3
    stretch = blocks * positions
    steps = stretch // CHUNK
    chunks = old_values.shape[0] + steps
    slots, features = decoded.shape
    keys = chunks * CHUNK
    return pl.pallas_call(
        functools.partial(prefill_kernel, positions),
        out_shape=jax.ShapeDtypeStruct((blocks, positions // 2 + slots * features // 128, 2 * HD), BF16),
        in_specs=[SMEM, SMEM, SMEM, VMEM, ANY, ANY, ANY],
        out_specs=VMEM,
        scratch_shapes=[
            pltpu.VMEM(old_flipped.shape, BF16),
            pltpu.VMEM(old_values.shape, BF16),
            pltpu.VMEM(decoded.shape, F32),
            pltpu.VMEM((steps, 2 * HD, CHUNK), BF16),
            pltpu.VMEM((steps, CHUNK, 2 * HD), BF16),
            pltpu.VMEM((stretch, 2 * HD), BF16),
            pltpu.VMEM((chunks, CHUNK, CHUNK), F32),
            pltpu.VMEM((CHUNK, 128), F32),
            pltpu.VMEM((2, CHUNK, 128), F32),
            pltpu.SemaphoreType.DMA((3,)),
        ],
        compiler_params=pltpu.CompilerParams(vmem_limit_bytes=48 * 2**20),
        cost_estimate=pl.CostEstimate(flops=4 * stretch * keys * HD, bytes_accessed=4 * 2**20, transcendentals=stretch * keys),
    )(lengths, home, ids, msg, old_flipped, old_values, decoded)


def decode_kernel(
    heads, lengths, home, ids, pages, old_lengths, old_home, old_pages, x, gain, w, pool, old_pool,
    out, flipped, values_in, raw, old_sems, buf, wbuf, normed, qrows, cacherows, rowout, bests, totals, mixes, owners, anchors, wsems, sems,
):
    slots = pages.shape[0]
    width = heads * 2 * HD
    per_group = BLOCK // PAGE
    depth = pages.shape[1]
    most = buf.shape[0] // BLOCK
    old_length = own_length(old_lengths, old_home, ids)
    old_copy = start_cache(old_length, old_pages, old_pool, raw, old_sems)
    w_copies = [pltpu.make_async_copy(w.at[j], wbuf.at[j], wsems.at[j]) for j in range(3)]
    for copy in w_copies:
        copy.start()

    def page_copy(item, k):
        page = pages[owners[0, item], jnp.minimum(owners[2, item] * per_group + k, depth - 1)]
        place = item * per_group + k
        return pltpu.make_async_copy(
            pool.at[page], buf.at[pl.ds(pl.multiple_of(place * PAGE, PAGE), PAGE), :], sems.at[place]
        )

    def groups(s):
        return pl.cdiv(lengths[s], BLOCK)

    @pl.loop(0, home.shape[0])
    def _(request):
        s = home[request] - ids[0] * slots
        anchors[jnp.where((s >= 0) & (s < slots), s, slots)] = request

    @pl.loop(0, most + UNROLL)
    def _(item):
        owners[0, item] = 0
        owners[1, item] = 0
        owners[2, item] = 0

    def begin(s, start):
        @pl.loop(0, groups(s))
        def _(g):
            owners[0, start + g] = s
            owners[1, start + g] = lengths[s] - g * BLOCK
            owners[2, start + g] = g

        return start + groups(s)

    items = lax.fori_loop(0, slots, begin, 0)

    def fetch(item):
        @pl.when(item < items)
        def _():
            for k in range(per_group):
                page_copy(item, k).start()

    for item in range(AHEAD):
        fetch(item)
    turn_cache(old_length, old_copy, raw, flipped, values_in)
    values = x[...].astype(F32)
    inverse = lax.rsqrt(jnp.mean(values * values, axis=-1, keepdims=True) + EPSILON)
    normed[...] = (values * inverse * gain[...]).astype(BF16)
    rows = values.shape[0]
    zero = jnp.zeros((rows, HD), F32)
    parts = []
    for j in range(3):
        w_copies[j].wait()
        parts.append(jnp.dot(normed[...], wbuf[j], preferred_element_type=F32).astype(BF16).astype(F32))
    for g in range(heads):
        cut = slice(g * HD, (g + 1) * HD)
        span = slice(g * 2 * HD, (g + 1) * 2 * HD)
        qrows[:, span] = jnp.concatenate([parts[0][:, cut] * SCALE, zero], axis=1)
        cacherows[:, span] = jnp.concatenate([parts[1][:, cut], parts[2][:, cut]], axis=1)
    owner = lax.broadcasted_iota(jnp.int32, (8, width), 1) // (2 * HD)
    diagonal = owner == lax.broadcasted_iota(jnp.int32, (8, width), 0)

    def spread(s):
        row = anchors[s]
        return jnp.where(diagonal, jnp.broadcast_to(qrows[pl.ds(row, 1), :], (8, width)), 0.0)

    @pl.loop(0, pl.cdiv(items, UNROLL))
    def _(turn):
        for u in range(UNROLL):
            @pl.when(turn * UNROLL + u < items)
            def _():
                for k in range(per_group):
                    page_copy(turn * UNROLL + u, k).wait()

            fetch(turn * UNROLL + u + AHEAD)
        for u in range(UNROLL):
            item = turn * UNROLL + u
            place = jnp.minimum(item, most - 1)
            cache = buf[pl.ds(pl.multiple_of(place * BLOCK, BLOCK), BLOCK), :]
            query = spread(owners[0, item]).astype(BF16)
            s = contract_last(query, cache)
            s = jnp.where(lax.broadcasted_iota(jnp.int32, (8, BLOCK), 1) < owners[1, item], s, MASKED)
            best = jnp.max(s, axis=1, keepdims=True)
            weights = jnp.exp(s - best)
            bests[item] = jnp.broadcast_to(best, (8, 128))
            totals[item] = jnp.broadcast_to(jnp.sum(weights, axis=1, keepdims=True), (8, 128))
            mixes[item] = jnp.dot(weights.astype(BF16), cache, preferred_element_type=F32)

    most_items = pl.cdiv(depth * PAGE, BLOCK)
    start = 0
    for s in range(slots):
        own = jnp.broadcast_to(cacherows[pl.ds(anchors[s], 1), :], (8, width))
        own_score = jnp.sum(spread(s) * own, axis=1, keepdims=True)
        count = groups(s)
        held = [jnp.where(i < count, bests[start + i], -jnp.inf) for i in range(most_items)]
        best = functools.reduce(jnp.maximum, held, jnp.broadcast_to(own_score, (8, 128)))
        own_weight = jnp.exp(own_score - best[:, 0:1])
        total = own_weight
        mixed = own_weight.astype(BF16).astype(F32) * own
        for i in range(most_items):
            share = jnp.exp(held[i] - best)[:, 0:1]
            total = total + jnp.where(i < count, totals[start + i][:, 0:1], 0.0) * share
            mixed = mixed + jnp.where(i < count, mixes[start + i], 0.0) * share
        mixed = jnp.where(diagonal, mixed / total, 0.0)
        rowout[s : s + 1, :] = jnp.sum(mixed, axis=0, keepdims=True)
        start = start + count
    done = rowout[...]
    for g in range(0, heads, 2):
        out[:, g * HD : (g + 2) * HD] = jnp.concatenate(
            [done[:, g * 2 * HD + HD : (g + 1) * 2 * HD], done[:, (g + 1) * 2 * HD + HD : (g + 2) * 2 * HD]], axis=1
        )


def decode_attention(lengths, home, ids, pages, old_lengths, old_home, old_pages, x, gain, w, pool, old_pool):
    slots = pages.shape[0]
    features = w.shape[2]
    heads = features // HD
    width = heads * 2 * HD
    rows = x.shape[0]
    per_group = BLOCK // PAGE
    most = pl.cdiv(pool.shape[0] + slots * (per_group - 1), per_group)
    chunks = pl.cdiv(old_pool.shape[0] * PAGE, CHUNK)
    flipped, values = (chunks, 2 * HD, CHUNK), (chunks, CHUNK, 2 * HD)
    spare = max(UNROLL, pl.cdiv(pages.shape[1], per_group))
    return pl.pallas_call(
        functools.partial(decode_kernel, heads),
        out_shape=[
            jax.ShapeDtypeStruct((slots, features), F32),
            jax.ShapeDtypeStruct(flipped, BF16),
            jax.ShapeDtypeStruct(values, BF16),
        ],
        in_specs=[SMEM] * 7 + [VMEM, VMEM, ANY, ANY, ANY],
        out_specs=[VMEM, VMEM, VMEM],
        scratch_shapes=[
            pltpu.VMEM((chunks * CHUNK, 2 * HD), BF16),
            pltpu.SemaphoreType.DMA((chunks * (CHUNK // PAGE),)),
            pltpu.VMEM((most * BLOCK, width), BF16),
            pltpu.VMEM(w.shape, BF16),
            pltpu.VMEM(x.shape, BF16),
            pltpu.VMEM((rows, width), F32),
            pltpu.VMEM((rows, width), F32),
            pltpu.VMEM((slots, width), F32),
            pltpu.VMEM((most + spare, 8, 128), F32),
            pltpu.VMEM((most + spare, 8, 128), F32),
            pltpu.VMEM((most + spare, 8, width), F32),
            pltpu.SMEM((3, most + UNROLL), jnp.int32),
            pltpu.SMEM((slots + 1,), jnp.int32),
            pltpu.SemaphoreType.DMA((3,)),
            pltpu.SemaphoreType.DMA((most * per_group,)),
        ],
        compiler_params=pltpu.CompilerParams(vmem_limit_bytes=52 * 2**20),
        cost_estimate=pl.CostEstimate(flops=2 * 10**9, bytes_accessed=22 * 2**20, transcendentals=10**6),
    )(lengths, home, ids, pages, old_lengths, old_home, old_pages, x, gain, w, pool, old_pool)


def qkv_kernel(requests, heads, home, gain, x, w, out, xbuf, wbuf, normed, sems):
    rows = x.shape[0]
    positions = rows // requests
    half = positions // 2
    x_copy = pltpu.make_async_copy(x, xbuf, sems.at[3])
    x_copy.start()
    w_copies = [pltpu.make_async_copy(w.at[j], wbuf.at[j], sems.at[j]) for j in range(3)]
    for copy in w_copies:
        copy.start()
    x_copy.wait()
    values = xbuf[...].astype(F32)
    inverse = lax.rsqrt(jnp.mean(values * values, axis=-1, keepdims=True) + EPSILON)
    normed[...] = (values * inverse * gain[...]).astype(BF16)

    def project(j):
        w_copies[j].wait()
        return jnp.dot(normed[...], wbuf[j], preferred_element_type=F32).astype(BF16)

    y = project(0)
    for r in range(requests):
        for g in range(heads):
            part = y[r * positions : (r + 1) * positions, g * HD : (g + 1) * HD]
            out[home[r * heads + g], positions : positions + half, :] = jnp.concatenate([part[:half], part[half:]], axis=1)
    keys = project(1)
    y = project(2)
    for r in range(requests):
        span = slice(r * positions, (r + 1) * positions)
        for g in range(heads):
            cut = slice(g * HD, (g + 1) * HD)
            out[home[r * heads + g], 0:positions, :] = jnp.concatenate([keys[span, cut], y[span, cut]], axis=1)


def qkv_messages(home, x, gain, w, requests):
    rows, width = x.shape
    features = w.shape[2]
    heads = features // HD
    units = requests * heads
    positions = rows // requests
    return pl.pallas_call(
        functools.partial(qkv_kernel, requests, heads),
        out_shape=jax.ShapeDtypeStruct((units, positions * 3 // 2, 2 * HD), BF16),
        in_specs=[SMEM, VMEM, ANY, ANY],
        out_specs=VMEM,
        scratch_shapes=[
            pltpu.VMEM((rows, width), BF16),
            pltpu.VMEM(w.shape, BF16),
            pltpu.VMEM((rows, width), BF16),
            pltpu.SemaphoreType.DMA((4,)),
        ],
        compiler_params=pltpu.CompilerParams(vmem_limit_bytes=58 * 2**20),
        cost_estimate=pl.CostEstimate(flops=2 * rows * width * 3 * features, bytes_accessed=10 * 2**20, transcendentals=0),
    )(home, gain, x, w)


def project_kernel(requests, heads, home, slots_of, ids, received, w_out, *rest):
    outs, (rows_in, decode_in, weights, products, sem) = rest[:-5], rest[-5:]
    fetch = pltpu.make_async_copy(w_out, weights, sem)
    fetch.start()
    n_head = len(outs)
    n_tok = received.shape[0]
    per = outs[0].shape[0]
    features = w_out.shape[0]
    slots = decode_in.shape[0] // n_tok
    half = received.shape[1] - slots * features // 128
    positions = 2 * half
    block_rows = positions // n_head
    share = per - requests * block_rows
    hosted = share * n_head
    for b in range(n_tok):
        for k in range(0, features // 128, 2):
            pair = received[b, half + k * slots : half + (k + 2) * slots, :].astype(F32)
            for j in range(2):
                decode_in[b * slots : (b + 1) * slots, (k + j) * 128 : (k + j + 1) * 128] = pair[
                    j * slots : (j + 1) * slots
                ]
    rows_in[...] = jnp.zeros_like(rows_in)
    for r in range(requests):
        for g in range(0, heads, 2):
            left = received[home[r * heads + g], 0:half, :].astype(F32)
            right = received[home[r * heads + g + 1], 0:half, :].astype(F32)
            both = jnp.concatenate(
                [
                    jnp.concatenate([left[:, :HD], right[:, :HD]], axis=1),
                    jnp.concatenate([left[:, HD:], right[:, HD:]], axis=1),
                ],
                axis=0,
            )
            for h in range(n_head):
                rows_in[h, r * block_rows : (r + 1) * block_rows, g * HD : (g + 2) * HD] = both[
                    h * block_rows : (h + 1) * block_rows
                ]
    for j in range(hosted):
        rows_in[j // share, requests * block_rows + j % share, :] = decode_in[pl.ds(slots_of[ids[0] * hosted + j], 1), :][0]
    fetch.wait()
    padded = rows_in.shape[1]
    everyone = rows_in[...].reshape(n_head * padded, features).astype(BF16)
    products[...] = jnp.dot(everyone, weights[...], preferred_element_type=F32).astype(BF16).reshape(products.shape)
    for k in range(n_head):
        outs[k][...] = products[ids[1] ^ k, 0:per, :]


def project_out(home, slots_of, ids, received, w_out, requests, heads, n_head, hosted):
    features, width = w_out.shape
    positions = 2 * (received.shape[1] - hosted * features // 128)
    per = requests * (positions // n_head) + hosted // n_head
    padded = -(-per // 16) * 16
    return pl.pallas_call(
        functools.partial(project_kernel, requests, heads),
        out_shape=[jax.ShapeDtypeStruct((per, width), BF16)] * n_head,
        in_specs=[SMEM, SMEM, SMEM, VMEM, ANY],
        out_specs=[VMEM] * n_head,
        scratch_shapes=[
            pltpu.VMEM((n_head, padded, features), F32),
            pltpu.VMEM((received.shape[0] * hosted, features), F32),
            pltpu.VMEM(w_out.shape, BF16),
            pltpu.VMEM((n_head, padded, width), BF16),
            pltpu.SemaphoreType.DMA,
        ],
        compiler_params=pltpu.CompilerParams(vmem_limit_bytes=24 * 2**20),
        cost_estimate=pl.CostEstimate(flops=2 * n_head * per * features * width, bytes_accessed=4 * 2**20, transcendentals=0),
    )(home, slots_of, ids, received, w_out)


def middle_kernel(own_pre, own_dec, gain, *rest):
    terms, (resid, normed_left, normed_right) = rest[:-3], rest[-3:]
    middle = normed_left.shape[1]
    split = own_pre.shape[0]
    for rows, own in ((slice(0, split), own_pre), (slice(split, resid.shape[0]), own_dec)):
        values = own[...].astype(F32)
        for term in terms:
            values = values + term[rows, :].astype(F32)
        resid[rows, :] = values
        inverse = lax.rsqrt(jnp.mean(values * values, axis=-1, keepdims=True) + EPSILON)
        normed = (values * inverse * gain[...]).astype(BF16)
        normed_left[rows, :] = normed[:, :middle]
        normed_right[rows, :] = normed[:, middle:]


def middle(own_pre, own_dec, gain, terms):
    shape = terms[0].shape
    return pl.pallas_call(
        middle_kernel,
        out_shape=[jax.ShapeDtypeStruct(shape, F32)] + [jax.ShapeDtypeStruct((shape[0], shape[1] // 2), BF16)] * 2,
        in_specs=[VMEM] * (3 + len(terms)),
        out_specs=[VMEM] * 3,
        compiler_params=pltpu.CompilerParams(vmem_limit_bytes=16 * 2**20),
        cost_estimate=pl.CostEstimate(flops=10**6, bytes_accessed=2 * 2**20, transcendentals=0),
    )(own_pre, own_dec, gain, *terms)


def hold_kernel(source, out, sem):
    copy = pltpu.make_async_copy(source, out, sem)
    copy.start()
    copy.wait()


def hold(array):
    return pl.pallas_call(
        hold_kernel,
        out_shape=jax.ShapeDtypeStruct(array.shape, array.dtype),
        in_specs=[ANY],
        out_specs=VMEM,
        scratch_shapes=[pltpu.SemaphoreType.DMA],
        compiler_params=pltpu.CompilerParams(vmem_limit_bytes=24 * 2**20),
        cost_estimate=pl.CostEstimate(flops=0, bytes_accessed=2 * array.size * 2, transcendentals=0),
    )(array)


def finish_kernel(resid, own_left, own_right, *rest):
    sums, outs = rest[:-2], rest[-2:]
    middle = own_left.shape[1]
    first = 0
    for out in outs:
        rows = slice(first, first + out.shape[0])
        first += out.shape[0]
        for side, own in enumerate((own_left, own_right)):
            cols = slice(side * middle, (side + 1) * middle)
            added = own[rows, :].astype(F32)
            for term in sums[2 * side : 2 * side + 2]:
                added = added + term[rows, :].astype(F32)
            out[:, cols] = (resid[rows, cols] + added).astype(BF16)


def finish(resid, own, sums, split):
    per, width = resid.shape
    return pl.pallas_call(
        finish_kernel,
        out_shape=[jax.ShapeDtypeStruct((split, width), BF16), jax.ShapeDtypeStruct((per - split, width), BF16)],
        in_specs=[VMEM] * 7,
        out_specs=[VMEM] * 2,
        compiler_params=pltpu.CompilerParams(vmem_limit_bytes=16 * 2**20),
        cost_estimate=pl.CostEstimate(flops=10**6, bytes_accessed=2 * 2**20, transcendentals=0),
    )(resid, *own, *sums)


def feed_kernel(shape, *refs):
    count, pieces = len(shape), sum(shape)
    parts, (gate_up, down), outs = list(refs[:pieces]), refs[pieces : pieces + 2], refs[pieces + 2 :]
    outs, rows = outs[:-1], outs[-1]
    per = outs[0].shape[0]
    padded = rows.shape[0] // count
    for index, size in enumerate(shape):
        first = 0
        for _ in range(size):
            part = parts.pop(0)
            rows[index * padded : index * padded + per, first : first + part.shape[1]] = part[...]
            first += part.shape[1]
    middle = down.shape[1] // 2
    hidden_units = down.shape[0]
    tile = 128 if hidden_units % 128 == 0 else hidden_units
    steps = hidden_units // tile

    hidden = []
    for step in range(steps):
        cols = slice(step * tile, (step + 1) * tile)
        if tile == 128:
            both = jnp.concatenate([gate_up[0, :, cols], gate_up[1, :, cols]], axis=1)
            y = jnp.dot(rows[...], both, preferred_element_type=F32)
            gate, upper = y[:, :tile], y[:, tile:]
        else:
            gate = jnp.dot(rows[...], gate_up[0], preferred_element_type=F32)
            upper = jnp.dot(rows[...], gate_up[1], preferred_element_type=F32)
        hidden.append((jax.nn.gelu(gate, approximate=True) * upper).astype(BF16))
    full = jnp.concatenate(hidden, axis=1)
    for side in range(2):
        cols = slice(side * middle, (side + 1) * middle)
        y = jnp.dot(full, down[:, cols], preferred_element_type=F32).astype(BF16)
        for index in range(count):
            outs[2 * index + side][...] = y[index * padded : index * padded + per]


def feed_forward(chunks, gate_up, down):
    count = len(chunks)
    pieces = [piece for chunk in chunks for piece in chunk]
    per, width = pieces[0].shape[0], down.shape[1]
    hidden_units = down.shape[0]
    return pl.pallas_call(
        functools.partial(feed_kernel, [len(chunk) for chunk in chunks]),
        out_shape=[jax.ShapeDtypeStruct((per, width // 2), BF16)] * (2 * count),
        in_specs=[VMEM] * (len(pieces) + 2),
        out_specs=[VMEM] * (2 * count),
        scratch_shapes=[pltpu.VMEM((count * (-(-per // 16) * 16), width), BF16)],
        compiler_params=pltpu.CompilerParams(vmem_limit_bytes=24 * 2**20),
        cost_estimate=pl.CostEstimate(
            flops=6 * count * per * width * hidden_units, bytes_accessed=8 * 2**20, transcendentals=count * per * hidden_units
        ),
    )(*pieces, gate_up, down)


def ring_of(n_tok):
    if n_tok == 8:
        return [0, 2, 4, 6, 7, 5, 3, 1]
    return list(range(n_tok))


def shards(
    prefill_states,
    decode_states,
    attn_gain,
    w_qkv,
    w_out,
    ffn_gain,
    w_gate_up,
    w_down,
    prefill_pool,
    prefill_pages,
    prefill_lengths,
    prefill_home,
    decode_pool,
    decode_pages,
    decode_lengths,
    decode_home,
):
    n_tok = lax.axis_size("tok")
    n_head = lax.axis_size("head")
    my_tok = lax.axis_index("tok")
    my_head = lax.axis_index("head")
    requests, positions, width = prefill_states.shape
    hosted = decode_states.shape[0]
    features = w_qkv.shape[2]
    heads = features // HD
    units = requests * heads
    ring = ring_of(n_tok)
    ahead = [(ring[i], ring[(i + 1) % n_tok]) for i in range(n_tok)]
    behind = [(b, a) for a, b in ahead]
    far = n_tok // 2
    near = (n_tok - 1) // 2

    def joined(part, other):
        return (part.astype(F32) + other.astype(F32)).astype(BF16)

    gain = attn_gain.reshape(1, width)
    w_three = jnp.transpose(w_qkv, (1, 0, 2))
    ids = jnp.stack([my_tok, my_head]).astype(jnp.int32)
    copies = jnp.broadcast_to(decode_states[None], (n_tok, hosted, width))
    rows = lax.all_to_all(copies, "tok", split_axis=0, concat_axis=0, tiled=True).reshape(n_tok * hosted, width)
    messages = qkv_messages(prefill_home, prefill_states.reshape(requests * positions, width), gain, w_three, requests)
    messages, rows = lax.optimization_barrier((messages, rows))
    arrived = lax.all_to_all(messages, "tok", split_axis=0, concat_axis=0, tiled=True)
    decoded, old_keys, old_values = decode_attention(
        decode_lengths, decode_home, ids, decode_pages, prefill_lengths, prefill_home, prefill_pages.reshape(-1),
        rows, gain, w_three, decode_pool, prefill_pool,
    )
    attn = prefill_attention(prefill_lengths, prefill_home, ids, arrived, old_keys, old_values, decoded)
    attn, w_gate_up = lax.optimization_barrier((attn, w_gate_up))
    returned = lax.all_to_all(attn, "tok", split_axis=0, concat_axis=0, tiled=True)
    gate_up = jnp.transpose(w_gate_up, (1, 0, 2))
    returned, gate_up = lax.optimization_barrier((returned, gate_up))

    parts = project_out(prefill_home, decode_home, ids, returned, w_out, requests, heads, n_head, hosted)
    block_rows = positions // n_head
    share = hosted // n_head
    own_pre = lax.dynamic_slice_in_dim(prefill_states, my_head * block_rows, block_rows, 1)
    own_dec = lax.dynamic_slice_in_dim(decode_states, my_head * share, share, 0)
    terms = [parts[0]]
    swap = [(i, i ^ 1) for i in range(n_head)]
    for k in range(2, n_head, 2):
        both = joined(parts[k], lax.ppermute(parts[k + 1], "head", swap))
        terms.append(lax.ppermute(both, "head", [(i, i ^ k) for i in range(n_head)]))
    terms.append(lax.ppermute(parts[1], "head", swap))
    gate_up = hold(gate_up)
    terms[1], gate_up = lax.optimization_barrier((terms[1], gate_up))
    resid, left, right = middle(own_pre.reshape(requests * block_rows, width), own_dec, ffn_gain.reshape(1, width), terms)

    plus, minus = {}, {}
    up_left, up_right, down_left, down_right = left, right, left, right
    waiting = None
    for k in range(1, far + 1):
        up_left = lax.ppermute(up_left, "tok", ahead)
        down_right = lax.ppermute(down_right, "tok", behind)
        if k <= near:
            down_left = lax.ppermute(down_left, "tok", behind)
            up_right = lax.ppermute(up_right, "tok", ahead)
        if waiting is not None:
            done = feed_forward(waiting, gate_up, w_down)
            up_left, down_right, done = lax.optimization_barrier((up_left, down_right, done))
            minus[k - 1], plus[k - 1] = done[:2], done[2:]
        waiting = [(up_left, up_right), (down_left, down_right)]
    farthest = feed_forward([(up_left, down_right)], gate_up, w_down)
    left, right, farthest = lax.optimization_barrier((left, right, farthest))
    own_part = feed_forward([(left, right)], gate_up, w_down)

    def chain(part, table, side, hops, steps):
        for k in range(hops, 0, -1):
            part = joined(table[k][side], lax.ppermute(part, "tok", steps))
        return lax.ppermute(part, "tok", steps)

    sums = [
        chain(minus[near][0], minus, 0, near - 1, behind),
        chain(farthest[0], plus, 0, far - 1, ahead),
        chain(plus[near][1], plus, 1, near - 1, ahead),
        chain(farthest[1], minus, 1, far - 1, behind),
    ]
    pre, dec = finish(resid, own_part, sums, requests * block_rows)
    return (pre.reshape(requests, block_rows, width), dec)


def solution(mesh):
    placed = (
        P(None, "tok", None),
        P("tok", None),
        P(),
        P(None, None, "head"),
        P("head", None),
        P(),
        P(None, None, "tok"),
        P("tok", None),
        P("tok", None, "head"),
        P("tok", None),
        P(),
        P(),
        P("tok", None, "head"),
        P("tok", None),
        P("tok"),
        P(),
    )
    return jax.shard_map(
        shards,
        mesh=mesh,
        in_specs=placed,
        out_specs=(P(None, ("tok", "head"), None), P(("tok", "head"), None)),
        check_vma=False,
    )
```

```python
import functools
import jax
import jax.numpy as jnp
from jax import lax
from jax.experimental import pallas as pl
from jax.experimental.pallas import tpu as pltpu
from jax.sharding import PartitionSpec as P

HD = 64
PAGE = 128
EPSILON = 1e-06
SCALE = 0.125
MASKED = -1e30
LOG2E = 1.4426950408889634
BLOCK = 512
CHUNK = 1024
UNROLL = 2
AHEAD = 6
F32 = jnp.float32
BF16 = jnp.bfloat16
VMEM = pl.BlockSpec(memory_space=pltpu.VMEM)
SMEM = pl.BlockSpec(memory_space=pltpu.SMEM)
ANY = pl.BlockSpec(memory_space=pl.ANY)


def contract_last(left, right):
    return lax.dot_general(left, right, (((1,), (1,)), ((), ())), preferred_element_type=F32)


def own_length(lengths, home, ids):
    units = home.shape[0]
    heads = units // lengths.shape[0]
    length = lengths[0]
    for unit in range(units):
        length = jnp.where(home[unit] == ids[0], lengths[unit // heads], length)
    return length


def start_cache(length, pages, pool, raw, sems):
    last = pages.shape[0] - 1

    def page_copy(index):
        page = pages[jnp.minimum(index, last)]
        return pltpu.make_async_copy(
            pool.at[page], raw.at[pl.ds(pl.multiple_of(index * PAGE, PAGE), PAGE), :], sems.at[index]
        )

    @pl.loop(0, pl.cdiv(length, CHUNK) * (CHUNK // PAGE))
    def _(index):
        page_copy(index).start()

    return page_copy


def turn_cache(length, page_copy, raw, flipped, values):
    per_chunk = CHUNK // PAGE

    @pl.loop(0, pl.cdiv(length, CHUNK))
    def _(c):
        for k in range(per_chunk):
            page_copy(c * per_chunk + k).wait()
        keys, mixed = doubled(raw[pl.ds(pl.multiple_of(c * CHUNK, CHUNK), CHUNK), :])
        flipped[c] = keys
        values[c] = mixed

        @pl.when(length - c * CHUNK < CHUNK)
        def _():
            valid = length - c * CHUNK
            columns = lax.broadcasted_iota(jnp.int32, keys.shape, 1) < valid
            flipped[c] = jnp.where(columns, keys, jnp.broadcast_to(keys[:, 0:1], keys.shape))
            inside = lax.broadcasted_iota(jnp.int32, mixed.shape, 0) < valid
            values[c] = jnp.where(inside, mixed, jnp.zeros_like(mixed))


def doubled(both):
    turned = both.T
    keys = jnp.concatenate([turned[:HD], turned[:HD]], axis=0)
    side = lax.broadcasted_iota(jnp.int32, both.shape, 1)
    return keys, jnp.where(side < HD, jnp.ones_like(both), both)


def prefill_kernel(
    positions, lengths, home, ids, msg, flipped_in, values_in, decoded_in, out,
    old_flipped, old_values, decoded, flipped, values, queries, scores, top, total, sems,
):
    blocks = msg.shape[0]
    stretch = blocks * positions
    half = positions // 2
    used = pl.cdiv(own_length(lengths, home, ids), CHUNK)
    steps = stretch // CHUNK
    loads = [
        pltpu.make_async_copy(flipped_in, old_flipped, sems.at[0]),
        pltpu.make_async_copy(values_in, old_values, sems.at[1]),
        pltpu.make_async_copy(decoded_in, decoded, sems.at[2]),
    ]
    for load in loads:
        load.start()

    @pl.loop(0, blocks)
    def _(b):
        packed = msg[b, pl.ds(positions, half), :].astype(F32) * (SCALE * LOG2E)
        high = packed.astype(BF16)
        low = (packed - high.astype(F32)).astype(BF16)
        row = pl.multiple_of(b * positions, positions)
        for part in range(2):
            lanes = slice(part * HD, (part + 1) * HD)
            queries[pl.ds(row + part * half, half), :] = jnp.concatenate([high[:, lanes], low[:, lanes]], axis=1)

    for c in range(steps):
        for k in range(CHUNK // positions):
            keys, mixed = doubled(msg[c * (CHUNK // positions) + k, 0:positions, :])
            flipped[c, :, k * positions : (k + 1) * positions] = keys
            values[c, k * positions : (k + 1) * positions, :] = mixed
    def raise_top(s):
        best = top[...]
        for k in range(CHUNK // 128):
            best = jnp.maximum(best, s[:, k * 128 : (k + 1) * 128])
        top[...] = best

    def score(i, spot, keys, diagonal=False):
        q = queries[pl.ds(pl.multiple_of(i * CHUNK, CHUNK), CHUNK), :]
        s = jnp.dot(q, keys, preferred_element_type=F32)
        if diagonal:
            rows = lax.broadcasted_iota(jnp.int32, (CHUNK, CHUNK), 0)
            cols = lax.broadcasted_iota(jnp.int32, (CHUNK, CHUNK), 1)
            s = jnp.where(cols <= rows, s, MASKED)
        scores[spot] = s
        raise_top(s)

    def settle():
        best = jnp.max(top[...], axis=1, keepdims=True)
        total[1] = jnp.broadcast_to(best, (CHUNK, 128))
        top[...] = jnp.full_like(top, -jnp.inf)
        total[0] = jnp.zeros((CHUNK, 128), F32)

    def mix(spot, rows):
        best = total[1]
        s = scores[spot]
        weights = jnp.concatenate(
            [jnp.exp2(s[:, k * 128 : (k + 1) * 128] - best).astype(BF16) for k in range(CHUNK // 128)], axis=1
        )
        total[0] += jnp.dot(weights, rows, preferred_element_type=F32)

    def emit(i):
        done = total[0]
        mixed = (done[:, HD:] / done[:, :HD]).astype(BF16)
        for k in range(CHUNK // positions):
            part = mixed[k * positions : (k + 1) * positions]
            out[i * (CHUNK // positions) + k, 0:half, :] = jnp.concatenate([part[:half], part[half:]], axis=1)

    top[...] = jnp.full_like(top, -jnp.inf)
    for load in loads:
        load.wait()
    slots, features = decoded.shape
    for k in range(0, features // 128, 2):
        pair = jnp.concatenate([decoded[:, k * 128 : (k + 1) * 128], decoded[:, (k + 1) * 128 : (k + 2) * 128]], axis=0)
        pair = pair.astype(BF16)
        for b in range(blocks):
            out[b, half + k * slots : half + (k + 2) * slots, :] = pair

    @pl.loop(0, used)
    def _(c):
        score(0, c, old_flipped[c])

    score(0, used, flipped[0], diagonal=True)
    settle()

    @pl.loop(1, steps)
    def _(i):
        @pl.loop(0, used)
        def _(c):
            mix(c, old_values[c])
            score(i, c, old_flipped[c])

        @pl.loop(0, i)
        def _(c):
            mix(used + c, values[c])
            score(i, used + c, flipped[c])

        emit(i - 1)
        score(i, used + i, flipped[i], diagonal=True)
        settle()

    @pl.loop(0, used)
    def _(c):
        mix(c, old_values[c])

    @pl.loop(0, steps)
    def _(c):
        mix(used + c, values[c])

    emit(steps - 1)


def prefill_attention(lengths, home, ids, msg, old_flipped, old_values, decoded):
    blocks, rows, _ = msg.shape
    positions = rows * 2 // 3
    stretch = blocks * positions
    steps = stretch // CHUNK
    chunks = old_values.shape[0] + steps
    slots, features = decoded.shape
    keys = chunks * CHUNK
    return pl.pallas_call(
        functools.partial(prefill_kernel, positions),
        out_shape=jax.ShapeDtypeStruct((blocks, positions // 2 + slots * features // 128, 2 * HD), BF16),
        in_specs=[SMEM, SMEM, SMEM, VMEM, ANY, ANY, ANY],
        out_specs=VMEM,
        scratch_shapes=[
            pltpu.VMEM(old_flipped.shape, BF16),
            pltpu.VMEM(old_values.shape, BF16),
            pltpu.VMEM(decoded.shape, F32),
            pltpu.VMEM((steps, 2 * HD, CHUNK), BF16),
            pltpu.VMEM((steps, CHUNK, 2 * HD), BF16),
            pltpu.VMEM((stretch, 2 * HD), BF16),
            pltpu.VMEM((chunks, CHUNK, CHUNK), F32),
            pltpu.VMEM((CHUNK, 128), F32),
            pltpu.VMEM((2, CHUNK, 128), F32),
            pltpu.SemaphoreType.DMA((3,)),
        ],
        compiler_params=pltpu.CompilerParams(vmem_limit_bytes=48 * 2**20),
        cost_estimate=pl.CostEstimate(flops=4 * stretch * keys * HD, bytes_accessed=4 * 2**20, transcendentals=stretch * keys),
    )(lengths, home, ids, msg, old_flipped, old_values, decoded)


def decode_kernel(
    heads, lengths, home, ids, pages, old_lengths, old_home, old_pages, x, gain, w, pool, old_pool,
    out, flipped, values_in, raw, old_sems, buf, wbuf, normed, qrows, cacherows, rowout, bests, totals, mixes, owners, anchors, wsems, sems,
):
    slots = pages.shape[0]
    width = heads * 2 * HD
    per_group = BLOCK // PAGE
    depth = pages.shape[1]
    most = buf.shape[0] // BLOCK
    old_length = own_length(old_lengths, old_home, ids)
    old_copy = start_cache(old_length, old_pages, old_pool, raw, old_sems)
    w_copies = [pltpu.make_async_copy(w.at[j], wbuf.at[j], wsems.at[j]) for j in range(3)]
    for copy in w_copies:
        copy.start()

    def page_copy(item, k):
        page = pages[owners[0, item], jnp.minimum(owners[2, item] * per_group + k, depth - 1)]
        place = item * per_group + k
        return pltpu.make_async_copy(
            pool.at[page], buf.at[pl.ds(pl.multiple_of(place * PAGE, PAGE), PAGE), :], sems.at[place]
        )

    def groups(s):
        return pl.cdiv(lengths[s], BLOCK)

    @pl.loop(0, home.shape[0])
    def _(request):
        s = home[request] - ids[0] * slots
        anchors[jnp.where((s >= 0) & (s < slots), s, slots)] = request

    @pl.loop(0, most + UNROLL)
    def _(item):
        owners[0, item] = 0
        owners[1, item] = 0
        owners[2, item] = 0

    def begin(s, start):
        @pl.loop(0, groups(s))
        def _(g):
            owners[0, start + g] = s
            owners[1, start + g] = lengths[s] - g * BLOCK
            owners[2, start + g] = g

        return start + groups(s)

    items = lax.fori_loop(0, slots, begin, 0)

    def fetch(item):
        @pl.when(item < items)
        def _():
            for k in range(per_group):
                page_copy(item, k).start()

    for item in range(AHEAD):
        fetch(item)
    turn_cache(old_length, old_copy, raw, flipped, values_in)
    values = x[...].astype(F32)
    inverse = lax.rsqrt(jnp.mean(values * values, axis=-1, keepdims=True) + EPSILON)
    normed[...] = (values * inverse * gain[...]).astype(BF16)
    rows = values.shape[0]
    zero = jnp.zeros((rows, HD), F32)
    parts = []
    for j in range(3):
        w_copies[j].wait()
        parts.append(jnp.dot(normed[...], wbuf[j], preferred_element_type=F32).astype(BF16).astype(F32))
    for g in range(heads):
        cut = slice(g * HD, (g + 1) * HD)
        span = slice(g * 2 * HD, (g + 1) * 2 * HD)
        qrows[:, span] = jnp.concatenate([parts[0][:, cut] * SCALE, zero], axis=1)
        cacherows[:, span] = jnp.concatenate([parts[1][:, cut], parts[2][:, cut]], axis=1)
    owner = lax.broadcasted_iota(jnp.int32, (8, width), 1) // (2 * HD)
    diagonal = owner == lax.broadcasted_iota(jnp.int32, (8, width), 0)

    def spread(s):
        row = anchors[s]
        return jnp.where(diagonal, jnp.broadcast_to(qrows[pl.ds(row, 1), :], (8, width)), 0.0)

    @pl.loop(0, pl.cdiv(items, UNROLL))
    def _(turn):
        for u in range(UNROLL):
            @pl.when(turn * UNROLL + u < items)
            def _():
                for k in range(per_group):
                    page_copy(turn * UNROLL + u, k).wait()

            fetch(turn * UNROLL + u + AHEAD)
        for u in range(UNROLL):
            item = turn * UNROLL + u
            place = jnp.minimum(item, most - 1)
            cache = buf[pl.ds(pl.multiple_of(place * BLOCK, BLOCK), BLOCK), :]
            query = spread(owners[0, item]).astype(BF16)
            s = contract_last(query, cache)
            s = jnp.where(lax.broadcasted_iota(jnp.int32, (8, BLOCK), 1) < owners[1, item], s, MASKED)
            best = jnp.max(s, axis=1, keepdims=True)
            weights = jnp.exp(s - best)
            bests[item] = jnp.broadcast_to(best, (8, 128))
            totals[item] = jnp.broadcast_to(jnp.sum(weights, axis=1, keepdims=True), (8, 128))
            mixes[item] = jnp.dot(weights.astype(BF16), cache, preferred_element_type=F32)

    most_items = pl.cdiv(depth * PAGE, BLOCK)
    start = 0
    for s in range(slots):
        own = jnp.broadcast_to(cacherows[pl.ds(anchors[s], 1), :], (8, width))
        own_score = jnp.sum(spread(s) * own, axis=1, keepdims=True)
        count = groups(s)
        held = [jnp.where(i < count, bests[start + i], -jnp.inf) for i in range(most_items)]
        best = functools.reduce(jnp.maximum, held, jnp.broadcast_to(own_score, (8, 128)))
        own_weight = jnp.exp(own_score - best[:, 0:1])
        total = own_weight
        mixed = own_weight.astype(BF16).astype(F32) * own
        for i in range(most_items):
            share = jnp.exp(held[i] - best)[:, 0:1]
            total = total + jnp.where(i < count, totals[start + i][:, 0:1], 0.0) * share
            mixed = mixed + jnp.where(i < count, mixes[start + i], 0.0) * share
        mixed = jnp.where(diagonal, mixed / total, 0.0)
        rowout[s : s + 1, :] = jnp.sum(mixed, axis=0, keepdims=True)
        start = start + count
    done = rowout[...]
    for g in range(0, heads, 2):
        out[:, g * HD : (g + 2) * HD] = jnp.concatenate(
            [done[:, g * 2 * HD + HD : (g + 1) * 2 * HD], done[:, (g + 1) * 2 * HD + HD : (g + 2) * 2 * HD]], axis=1
        )


def decode_attention(lengths, home, ids, pages, old_lengths, old_home, old_pages, x, gain, w, pool, old_pool):
    slots = pages.shape[0]
    features = w.shape[2]
    heads = features // HD
    width = heads * 2 * HD
    rows = x.shape[0]
    per_group = BLOCK // PAGE
    most = pl.cdiv(pool.shape[0] + slots * (per_group - 1), per_group)
    chunks = pl.cdiv(old_pool.shape[0] * PAGE, CHUNK)
    flipped, values = (chunks, 2 * HD, CHUNK), (chunks, CHUNK, 2 * HD)
    spare = max(UNROLL, pl.cdiv(pages.shape[1], per_group))
    return pl.pallas_call(
        functools.partial(decode_kernel, heads),
        out_shape=[
            jax.ShapeDtypeStruct((slots, features), F32),
            jax.ShapeDtypeStruct(flipped, BF16),
            jax.ShapeDtypeStruct(values, BF16),
        ],
        in_specs=[SMEM] * 7 + [VMEM, VMEM, ANY, ANY, ANY],
        out_specs=[VMEM, VMEM, VMEM],
        scratch_shapes=[
            pltpu.VMEM((chunks * CHUNK, 2 * HD), BF16),
            pltpu.SemaphoreType.DMA((chunks * (CHUNK // PAGE),)),
            pltpu.VMEM((most * BLOCK, width), BF16),
            pltpu.VMEM(w.shape, BF16),
            pltpu.VMEM(x.shape, BF16),
            pltpu.VMEM((rows, width), F32),
            pltpu.VMEM((rows, width), F32),
            pltpu.VMEM((slots, width), F32),
            pltpu.VMEM((most + spare, 8, 128), F32),
            pltpu.VMEM((most + spare, 8, 128), F32),
            pltpu.VMEM((most + spare, 8, width), F32),
            pltpu.SMEM((3, most + UNROLL), jnp.int32),
            pltpu.SMEM((slots + 1,), jnp.int32),
            pltpu.SemaphoreType.DMA((3,)),
            pltpu.SemaphoreType.DMA((most * per_group,)),
        ],
        compiler_params=pltpu.CompilerParams(vmem_limit_bytes=52 * 2**20),
        cost_estimate=pl.CostEstimate(flops=2 * 10**9, bytes_accessed=22 * 2**20, transcendentals=10**6),
    )(lengths, home, ids, pages, old_lengths, old_home, old_pages, x, gain, w, pool, old_pool)


def qkv_kernel(requests, heads, home, gain, x, w, out, xbuf, wbuf, normed, sems):
    rows = x.shape[0]
    positions = rows // requests
    half = positions // 2
    x_copy = pltpu.make_async_copy(x, xbuf, sems.at[3])
    x_copy.start()
    w_copies = [pltpu.make_async_copy(w.at[j], wbuf.at[j], sems.at[j]) for j in range(3)]
    for copy in w_copies:
        copy.start()
    x_copy.wait()
    values = xbuf[...].astype(F32)
    inverse = lax.rsqrt(jnp.mean(values * values, axis=-1, keepdims=True) + EPSILON)
    normed[...] = (values * inverse * gain[...]).astype(BF16)

    def project(j):
        w_copies[j].wait()
        return jnp.dot(normed[...], wbuf[j], preferred_element_type=F32).astype(BF16)

    y = project(0)
    for r in range(requests):
        for g in range(heads):
            part = y[r * positions : (r + 1) * positions, g * HD : (g + 1) * HD]
            out[home[r * heads + g], positions : positions + half, :] = jnp.concatenate([part[:half], part[half:]], axis=1)
    keys = project(1)
    y = project(2)
    for r in range(requests):
        span = slice(r * positions, (r + 1) * positions)
        for g in range(heads):
            cut = slice(g * HD, (g + 1) * HD)
            out[home[r * heads + g], 0:positions, :] = jnp.concatenate([keys[span, cut], y[span, cut]], axis=1)


def qkv_messages(home, x, gain, w, requests):
    rows, width = x.shape
    features = w.shape[2]
    heads = features // HD
    units = requests * heads
    positions = rows // requests
    return pl.pallas_call(
        functools.partial(qkv_kernel, requests, heads),
        out_shape=jax.ShapeDtypeStruct((units, positions * 3 // 2, 2 * HD), BF16),
        in_specs=[SMEM, VMEM, ANY, ANY],
        out_specs=VMEM,
        scratch_shapes=[
            pltpu.VMEM((rows, width), BF16),
            pltpu.VMEM(w.shape, BF16),
            pltpu.VMEM((rows, width), BF16),
            pltpu.SemaphoreType.DMA((4,)),
        ],
        compiler_params=pltpu.CompilerParams(vmem_limit_bytes=58 * 2**20),
        cost_estimate=pl.CostEstimate(flops=2 * rows * width * 3 * features, bytes_accessed=10 * 2**20, transcendentals=0),
    )(home, gain, x, w)


def project_kernel(requests, heads, home, slots_of, ids, received, w_out, *rest):
    outs, (rows_in, decode_in, weights, products, sem) = rest[:-5], rest[-5:]
    fetch = pltpu.make_async_copy(w_out, weights, sem)
    fetch.start()
    n_head = len(outs)
    n_tok = received.shape[0]
    per = outs[0].shape[0]
    features = w_out.shape[0]
    slots = decode_in.shape[0] // n_tok
    half = received.shape[1] - slots * features // 128
    positions = 2 * half
    block_rows = positions // n_head
    share = per - requests * block_rows
    hosted = share * n_head
    for b in range(n_tok):
        for k in range(0, features // 128, 2):
            pair = received[b, half + k * slots : half + (k + 2) * slots, :].astype(F32)
            for j in range(2):
                decode_in[b * slots : (b + 1) * slots, (k + j) * 128 : (k + j + 1) * 128] = pair[
                    j * slots : (j + 1) * slots
                ]
    rows_in[...] = jnp.zeros_like(rows_in)
    for r in range(requests):
        for g in range(0, heads, 2):
            left = received[home[r * heads + g], 0:half, :].astype(F32)
            right = received[home[r * heads + g + 1], 0:half, :].astype(F32)
            both = jnp.concatenate(
                [
                    jnp.concatenate([left[:, :HD], right[:, :HD]], axis=1),
                    jnp.concatenate([left[:, HD:], right[:, HD:]], axis=1),
                ],
                axis=0,
            )
            for h in range(n_head):
                rows_in[h, r * block_rows : (r + 1) * block_rows, g * HD : (g + 2) * HD] = both[
                    h * block_rows : (h + 1) * block_rows
                ]
    for j in range(hosted):
        rows_in[j // share, requests * block_rows + j % share, :] = decode_in[pl.ds(slots_of[ids[0] * hosted + j], 1), :][0]
    fetch.wait()
    padded = rows_in.shape[1]
    everyone = rows_in[...].reshape(n_head * padded, features).astype(BF16)
    products[...] = jnp.dot(everyone, weights[...], preferred_element_type=F32).astype(BF16).reshape(products.shape)
    for k in range(n_head):
        outs[k][...] = products[ids[1] ^ k, 0:per, :]


def project_out(home, slots_of, ids, received, w_out, requests, heads, n_head, hosted):
    features, width = w_out.shape
    positions = 2 * (received.shape[1] - hosted * features // 128)
    per = requests * (positions // n_head) + hosted // n_head
    padded = -(-per // 16) * 16
    return pl.pallas_call(
        functools.partial(project_kernel, requests, heads),
        out_shape=[jax.ShapeDtypeStruct((per, width), BF16)] * n_head,
        in_specs=[SMEM, SMEM, SMEM, VMEM, ANY],
        out_specs=[VMEM] * n_head,
        scratch_shapes=[
            pltpu.VMEM((n_head, padded, features), F32),
            pltpu.VMEM((received.shape[0] * hosted, features), F32),
            pltpu.VMEM(w_out.shape, BF16),
            pltpu.VMEM((n_head, padded, width), BF16),
            pltpu.SemaphoreType.DMA,
        ],
        compiler_params=pltpu.CompilerParams(vmem_limit_bytes=24 * 2**20),
        cost_estimate=pl.CostEstimate(flops=2 * n_head * per * features * width, bytes_accessed=4 * 2**20, transcendentals=0),
    )(home, slots_of, ids, received, w_out)


def middle_kernel(own_pre, own_dec, gain, *rest):
    terms, (resid, normed_left, normed_right) = rest[:-3], rest[-3:]
    middle = normed_left.shape[1]
    split = own_pre.shape[0]
    for rows, own in ((slice(0, split), own_pre), (slice(split, resid.shape[0]), own_dec)):
        values = own[...].astype(F32)
        for term in terms:
            values = values + term[rows, :].astype(F32)
        resid[rows, :] = values
        inverse = lax.rsqrt(jnp.mean(values * values, axis=-1, keepdims=True) + EPSILON)
        normed = (values * inverse * gain[...]).astype(BF16)
        normed_left[rows, :] = normed[:, :middle]
        normed_right[rows, :] = normed[:, middle:]


def middle(own_pre, own_dec, gain, terms):
    shape = terms[0].shape
    return pl.pallas_call(
        middle_kernel,
        out_shape=[jax.ShapeDtypeStruct(shape, F32)] + [jax.ShapeDtypeStruct((shape[0], shape[1] // 2), BF16)] * 2,
        in_specs=[VMEM] * (3 + len(terms)),
        out_specs=[VMEM] * 3,
        compiler_params=pltpu.CompilerParams(vmem_limit_bytes=16 * 2**20),
        cost_estimate=pl.CostEstimate(flops=10**6, bytes_accessed=2 * 2**20, transcendentals=0),
    )(own_pre, own_dec, gain, *terms)


def hold_kernel(source, out, sem):
    copy = pltpu.make_async_copy(source, out, sem)
    copy.start()
    copy.wait()


def hold(array):
    return pl.pallas_call(
        hold_kernel,
        out_shape=jax.ShapeDtypeStruct(array.shape, array.dtype),
        in_specs=[ANY],
        out_specs=VMEM,
        scratch_shapes=[pltpu.SemaphoreType.DMA],
        compiler_params=pltpu.CompilerParams(vmem_limit_bytes=24 * 2**20),
        cost_estimate=pl.CostEstimate(flops=0, bytes_accessed=2 * array.size * 2, transcendentals=0),
    )(array)


def finish_kernel(resid, own_left, own_right, *rest):
    sums, outs = rest[:-2], rest[-2:]
    middle = own_left.shape[1]
    first = 0
    for out in outs:
        rows = slice(first, first + out.shape[0])
        first += out.shape[0]
        for side, own in enumerate((own_left, own_right)):
            cols = slice(side * middle, (side + 1) * middle)
            added = own[rows, :].astype(F32)
            for term in sums[2 * side : 2 * side + 2]:
                added = added + term[rows, :].astype(F32)
            out[:, cols] = (resid[rows, cols] + added).astype(BF16)


def finish(resid, own, sums, split):
    per, width = resid.shape
    return pl.pallas_call(
        finish_kernel,
        out_shape=[jax.ShapeDtypeStruct((split, width), BF16), jax.ShapeDtypeStruct((per - split, width), BF16)],
        in_specs=[VMEM] * 7,
        out_specs=[VMEM] * 2,
        compiler_params=pltpu.CompilerParams(vmem_limit_bytes=16 * 2**20),
        cost_estimate=pl.CostEstimate(flops=10**6, bytes_accessed=2 * 2**20, transcendentals=0),
    )(resid, *own, *sums)


def feed_kernel(shape, *refs):
    count, pieces = len(shape), sum(shape)
    parts, (gate_up, down), outs = list(refs[:pieces]), refs[pieces : pieces + 2], refs[pieces + 2 :]
    outs, rows = outs[:-1], outs[-1]
    per = outs[0].shape[0]
    padded = rows.shape[0] // count
    for index, size in enumerate(shape):
        first = 0
        for _ in range(size):
            part = parts.pop(0)
            rows[index * padded : index * padded + per, first : first + part.shape[1]] = part[...]
            first += part.shape[1]
    middle = down.shape[1] // 2
    hidden_units = down.shape[0]
    tile = 128 if hidden_units % 128 == 0 else hidden_units
    steps = hidden_units // tile

    hidden = []
    for step in range(steps):
        cols = slice(step * tile, (step + 1) * tile)
        if tile == 128:
            both = jnp.concatenate([gate_up[0, :, cols], gate_up[1, :, cols]], axis=1)
            y = jnp.dot(rows[...], both, preferred_element_type=F32)
            gate, upper = y[:, :tile], y[:, tile:]
        else:
            gate = jnp.dot(rows[...], gate_up[0], preferred_element_type=F32)
            upper = jnp.dot(rows[...], gate_up[1], preferred_element_type=F32)
        hidden.append((jax.nn.gelu(gate, approximate=True) * upper).astype(BF16))
    full = jnp.concatenate(hidden, axis=1)
    for side in range(2):
        cols = slice(side * middle, (side + 1) * middle)
        y = jnp.dot(full, down[:, cols], preferred_element_type=F32).astype(BF16)
        for index in range(count):
            outs[2 * index + side][...] = y[index * padded : index * padded + per]


def feed_forward(chunks, gate_up, down):
    count = len(chunks)
    pieces = [piece for chunk in chunks for piece in chunk]
    per, width = pieces[0].shape[0], down.shape[1]
    hidden_units = down.shape[0]
    return pl.pallas_call(
        functools.partial(feed_kernel, [len(chunk) for chunk in chunks]),
        out_shape=[jax.ShapeDtypeStruct((per, width // 2), BF16)] * (2 * count),
        in_specs=[VMEM] * (len(pieces) + 2),
        out_specs=[VMEM] * (2 * count),
        scratch_shapes=[pltpu.VMEM((count * (-(-per // 16) * 16), width), BF16)],
        compiler_params=pltpu.CompilerParams(vmem_limit_bytes=24 * 2**20),
        cost_estimate=pl.CostEstimate(
            flops=6 * count * per * width * hidden_units, bytes_accessed=8 * 2**20, transcendentals=count * per * hidden_units
        ),
    )(*pieces, gate_up, down)


def ring_of(n_tok):
    if n_tok == 8:
        return [0, 2, 4, 6, 7, 5, 3, 1]
    return list(range(n_tok))


def shards(
    prefill_states,
    decode_states,
    attn_gain,
    w_qkv,
    w_out,
    ffn_gain,
    w_gate_up,
    w_down,
    prefill_pool,
    prefill_pages,
    prefill_lengths,
    prefill_home,
    decode_pool,
    decode_pages,
    decode_lengths,
    decode_home,
):
    n_tok = lax.axis_size("tok")
    n_head = lax.axis_size("head")
    my_tok = lax.axis_index("tok")
    my_head = lax.axis_index("head")
    requests, positions, width = prefill_states.shape
    hosted = decode_states.shape[0]
    features = w_qkv.shape[2]
    heads = features // HD
    units = requests * heads
    ring = ring_of(n_tok)
    ahead = [(ring[i], ring[(i + 1) % n_tok]) for i in range(n_tok)]
    behind = [(b, a) for a, b in ahead]
    far = n_tok // 2
    near = (n_tok - 1) // 2

    def joined(part, other):
        return (part.astype(F32) + other.astype(F32)).astype(BF16)

    gain = attn_gain.reshape(1, width)
    w_three = jnp.transpose(w_qkv, (1, 0, 2))
    ids = jnp.stack([my_tok, my_head]).astype(jnp.int32)
    copies = jnp.broadcast_to(decode_states[None], (n_tok, hosted, width))
    rows = lax.all_to_all(copies, "tok", split_axis=0, concat_axis=0, tiled=True).reshape(n_tok * hosted, width)
    messages = qkv_messages(prefill_home, prefill_states.reshape(requests * positions, width), gain, w_three, requests)
    messages, rows, ids = lax.optimization_barrier((messages, rows, ids))
    arrived = lax.all_to_all(messages, "tok", split_axis=0, concat_axis=0, tiled=True)
    decoded, old_keys, old_values = decode_attention(
        decode_lengths, decode_home, ids, decode_pages, prefill_lengths, prefill_home, prefill_pages.reshape(-1),
        rows, gain, w_three, decode_pool, prefill_pool,
    )
    attn = prefill_attention(prefill_lengths, prefill_home, ids, arrived, old_keys, old_values, decoded)
    attn, w_gate_up = lax.optimization_barrier((attn, w_gate_up))
    returned = lax.all_to_all(attn, "tok", split_axis=0, concat_axis=0, tiled=True)
    gate_up = jnp.transpose(w_gate_up, (1, 0, 2))
    returned, gate_up = lax.optimization_barrier((returned, gate_up))

    parts = project_out(prefill_home, decode_home, ids, returned, w_out, requests, heads, n_head, hosted)
    block_rows = positions // n_head
    share = hosted // n_head
    own_pre = lax.dynamic_slice_in_dim(prefill_states, my_head * block_rows, block_rows, 1)
    own_dec = lax.dynamic_slice_in_dim(decode_states, my_head * share, share, 0)
    terms = [parts[0]]
    swap = [(i, i ^ 1) for i in range(n_head)]
    for k in range(2, n_head, 2):
        both = joined(parts[k], lax.ppermute(parts[k + 1], "head", swap))
        terms.append(lax.ppermute(both, "head", [(i, i ^ k) for i in range(n_head)]))
    terms.append(lax.ppermute(parts[1], "head", swap))
    gate_up = hold(gate_up)
    terms[1], gate_up = lax.optimization_barrier((terms[1], gate_up))
    resid, left, right = middle(own_pre.reshape(requests * block_rows, width), own_dec, ffn_gain.reshape(1, width), terms)

    plus, minus = {}, {}
    up_left, up_right, down_left, down_right = left, right, left, right
    waiting = None
    for k in range(1, far + 1):
        up_left = lax.ppermute(up_left, "tok", ahead)
        down_right = lax.ppermute(down_right, "tok", behind)
        if k <= near:
            down_left = lax.ppermute(down_left, "tok", behind)
            up_right = lax.ppermute(up_right, "tok", ahead)
        if waiting is not None:
            done = feed_forward(waiting, gate_up, w_down)
            if k < far:
                up_left, down_right, done = lax.optimization_barrier((up_left, down_right, done))
            minus[k - 1], plus[k - 1] = done[:2], done[2:]
        waiting = [(up_left, up_right), (down_left, down_right)]
    farthest = feed_forward([(up_left, down_right)], gate_up, w_down)
    left, right, farthest = lax.optimization_barrier((left, right, farthest))
    own_part = feed_forward([(left, right)], gate_up, w_down)

    def chain(part, table, side, hops, steps):
        for k in range(hops, 0, -1):
            part = joined(table[k][side], lax.ppermute(part, "tok", steps))
        return lax.ppermute(part, "tok", steps)

    near_left = chain(minus[near][0], minus, 0, near - 1, behind)
    near_right = chain(plus[near][1], plus, 1, near - 1, ahead)
    far_left = chain(farthest[0], plus, 0, far - 1, ahead)
    far_right = chain(farthest[1], minus, 1, far - 1, behind)
    sums = [near_left, far_left, near_right, far_right]
    pre, dec = finish(resid, own_part, sums, requests * block_rows)
    return (pre.reshape(requests, block_rows, width), dec)


def solution(mesh):
    placed = (
        P(None, "tok", None),
        P("tok", None),
        P(),
        P(None, None, "head"),
        P("head", None),
        P(),
        P(None, None, "tok"),
        P("tok", None),
        P("tok", None, "head"),
        P("tok", None),
        P(),
        P(),
        P("tok", None, "head"),
        P("tok", None),
        P("tok"),
        P(),
    )
    return jax.shard_map(
        shards,
        mesh=mesh,
        in_specs=placed,
        out_specs=(P(None, ("tok", "head"), None), P(("tok", "head"), None)),
        check_vma=False,
    )
```
